128 devices in a mesh: dp: 8 (over y_lo, z), ctx: 16 (over y_hi, x, core).
Axes of the slice: x: 4, y: 4 (y_hi: 2, y_lo: 2; y = y_hi * 2 + y_lo), z: 4, core: 2. Of those that a mesh axis runs over, the one named last changes fastest.
Arguments:
- tokens: bfloat16 [8, 2048, 1024], P('dp', 'ctx'), may hold values from -6 to 6
- cotangent: bfloat16 [8, 2048, 1024], P('dp', 'ctx')
- positions: int32 [8, 2048], replicated, may hold values from 0 to 2047, as said below
- weights: bfloat16 [1024, 15360], P(('dp', 'ctx'))
- norm_gains: bfloat16 [2304], P(('dp', 'ctx'))
- moment_weights: float32 [1024, 15360], P(('dp', 'ctx')), may hold values from -0.0004272461 to 0.0004272461
- second_weights: float32 [1024, 15360], P(('dp', 'ctx')), may hold values from 1.6527933e-09 to 2.669897e-08
- moment_gains: float32 [2304], P(('dp', 'ctx')), may hold values from -0.0012207031 to 0.0012207031
- second_gains: float32 [2304], P(('dp', 'ctx')), may hold values from 1.5256553e-08 to 2.415621e-07
Outputs:
- block_output: float32 [8, 2048, 1024], P('dp', 'ctx')
- grad_tokens: float32 [8, 2048, 1024], P('dp', 'ctx')
- grad_norm: float32 [1], replicated
- new_weights: float32 [1024, 15360], P(('dp', 'ctx'))
- new_moment_weights: float32 [1024, 15360], P(('dp', 'ctx'))
- new_second_weights: float32 [1024, 15360], P(('dp', 'ctx'))
- new_gains: float32 [2304], P(('dp', 'ctx'))
- new_moment_gains: float32 [2304], P(('dp', 'ctx'))
- new_second_gains: float32 [2304], P(('dp', 'ctx'))
The draws below stay inside these ranges and needn't reach their ends.
Inputs may be any that keep to these rules, and one draw needn't show every extreme that they name: Each sequence's 2048 positions are a permutation made of 32 blocks of 64 consecutive rising positions; the 128 rows [c * 128, (c + 1) * 128) of a sequence hold the two blocks b and 31 - b for some b, in either order, each pair once per sequence.
All inputs are finite; a program needn't handle non-finite values.
Results may differ from the reference program's by a relative error of at most 0.015.
Values may be sent and summed in bfloat16 or wider, within the bound.
No kernel may reach another device: no remote copies, remote signals or barrier semaphores. Data moves between devices by JAX's collectives and lax.ppermute only.
A program may use at most 320 MiB of HBM per device.

```python
import math
import jax
import jax.numpy as jnp
from jax import lax

D = 1024
FF = 3072
QUERY_HEADS = 16
KEY_VALUE_HEADS = 8
HEAD_SIZE = 128
ADAM_STEP = 10
ROWS_GROUP = 2048
SEQS = 8
LEN = 2048
PAIRS = 16
BLK = 64
QKVC = 4096
WCOLS = 15360
GAINS = 2304
NPARAM = 15730944
OUTFAN = 2
N_DP = 8


def draw_cotangent(key, part):
    key = jax.random.fold_in(key, 1)
    column = jnp.arange(D, dtype=jnp.float32) / (D - 1)
    sample = jnp.clip(jax.random.normal(key, (N_DP, ROWS_GROUP, D), jnp.float32), -6.0, 6.0)
    rising = 0.6 + 1.2 * column
    return (sample * rising[None, None, :]).astype(jnp.bfloat16)


def draw_positions(key, part):
    key = jax.random.fold_in(key, 2)

    def one_sequence(seq_key):
        order_key, flip_key = jax.random.split(seq_key)
        arrangement = jax.random.permutation(order_key, PAIRS).astype(jnp.int32)
        flipped = jax.random.randint(flip_key, (PAIRS,), 0, 2)
        mirror = 2 * PAIRS - 1 - arrangement
        front_block = jnp.where(flipped == 1, mirror, arrangement)
        back_block = jnp.where(flipped == 1, arrangement, mirror)
        blocks = jnp.stack([front_block, back_block], axis=1)
        offsets = jnp.arange(BLK, dtype=jnp.int32)
        return (blocks[:, :, None] * BLK + offsets[None, None, :]).reshape(PAIRS * 2 * BLK)
    table = jax.vmap(one_sequence)(jax.random.split(key, SEQS))
    return table.reshape(N_DP, ROWS_GROUP).astype(jnp.int32)


def draw_weights(key, part):
    key = jax.random.fold_in(key, 3)
    column = jnp.arange(WCOLS)
    spread = jnp.where(column < QKVC, D ** (-0.5), jnp.where(column < QKVC + QUERY_HEADS * HEAD_SIZE, OUTFAN ** (-0.5), jnp.where(column < QKVC + QUERY_HEADS * HEAD_SIZE + 2 * FF, D ** (-0.5), FF ** (-0.5))))
    sample = jnp.clip(jax.random.normal(key, (D, WCOLS), jnp.float32), -6.0, 6.0)
    return (sample * spread[None, :].astype(jnp.float32)).astype(jnp.bfloat16)


def draw_norm_gains(key, part):
    key = jax.random.fold_in(key, 4)
    factor_key, head_key = jax.random.split(key)
    place = jnp.arange(D, dtype=jnp.float32) / (D - 1)
    rising = 0.6 + 1.2 * place
    jitter = jax.random.uniform(factor_key, (2, D), jnp.float32, 0.8, 1.25)
    layer_gains = (rising[None, :] * jitter).reshape(2 * D)
    head_gains = jax.random.uniform(head_key, (2 * HEAD_SIZE,), jnp.float32, 0.7, 1.4)
    return jnp.concatenate([layer_gains, head_gains]).astype(jnp.bfloat16)


def levels(stream_key, dims, shards, smallest, high):
    factor_of = 1.0
    for dim, parts in shards:
        steps = jax.random.uniform(jax.random.fold_in(jax.random.fold_in(stream_key, 6), dim), (parts,), jnp.float32, smallest / len(shards), high / len(shards))
        factor_of = factor_of * jnp.repeat(jnp.exp(steps), dims[dim] // parts).reshape((-1,) + (1,) * (len(dims) - 1 - dim))
    return factor_of


def noise(rng, dims, deviation, reach, shards=(), kind=jnp.bfloat16):
    values = jax.random.normal(rng, dims, jnp.float32) * deviation
    if len(shards) > 0:
        values = levels(rng, dims, shards, -0.22, 0.18) * values
    return jnp.clip(values, min=-reach, max=reach).astype(kind)


def setup_inputs(seed: int = 0) -> dict:
    seeds = jax.random.split(jax.random.key(seed), 10)
    tokens = noise(seeds[0], (N_DP, ROWS_GROUP, D), 1.0, 6.0, ((0, 8), (1, 16)))
    cotangent = draw_cotangent(jax.random.fold_in(seeds[9], 71), 0)
    positions = draw_positions(jax.random.fold_in(seeds[9], 71), 0)
    weights = draw_weights(jax.random.fold_in(seeds[9], 71), 0)
    norm_gains = draw_norm_gains(jax.random.fold_in(seeds[9], 71), 0)
    moment_weights = noise(seeds[5], (D, WCOLS), (0.11 * NPARAM ** -0.5), 0.0004272461, ((0, 128),), jnp.float32)
    second_weights = jnp.clip(jnp.exp(math.log(2.6698970145844214e-08) - 2.7821582 * jax.random.uniform(seeds[6], (D, WCOLS), jnp.float32) ** levels(seeds[6], (D, WCOLS), ((0, 128),), -0.2, 0.2)), 1.6527933466292666e-09, 2.6698970145844214e-08)
    moment_gains = noise(seeds[7], (GAINS,), (0.33 * NPARAM ** -0.5), 0.0012207031, ((0, 128),), jnp.float32)
    second_gains = jnp.clip(jnp.exp(math.log(2.415621054296935e-07) - 2.7621175 * jax.random.uniform(seeds[8], (GAINS,), jnp.float32) ** levels(seeds[8], (GAINS,), ((0, 128),), -0.2, 0.2)), 1.5256553353992786e-08, 2.415621054296935e-07)
    return dict(tokens=tokens, cotangent=cotangent, positions=positions, weights=weights, norm_gains=norm_gains, moment_weights=moment_weights, second_weights=second_weights, moment_gains=moment_gains, second_gains=second_gains)


eps_norm = 1e-06
rope_base = 1000000.0
clip_limit = 1.0
beta_one = 0.9
beta_two = 0.95
adam_eps = 1e-08
decay_rate = 0.1
rate_matrix = 0.06
rate_output = 2.0
rate_gain = 1.0
highest = lax.Precision.HIGHEST

@jax.custom_vjp
def low(v):
    return lax.optimization_barrier(v.astype(jnp.bfloat16)).astype(jnp.float32)

@jax.custom_vjp
def low_back(v):
    return v

def low_keep(v):
    return (low(v), None)

def low_pass(kept, grad):
    return (grad,)

def back_keep(v):
    return (v, None)

def back_low(kept, grad):
    return (low(grad),)
low.defvjp(low_keep, low_pass)
low_back.defvjp(back_keep, back_low)

def rms_scale(value_rows):
    return lax.rsqrt(lax.optimization_barrier(jnp.mean(value_rows * value_rows, axis=-1, keepdims=True)) + eps_norm)

def angles(places, width):
    half_width = width // 2
    inverse = jnp.exp(jnp.arange(half_width, dtype=jnp.float32) * (-2.0 / width) * math.log(rope_base))
    turned = places.astype(jnp.float32)[:, None] * inverse[None, :]
    return (jnp.cos(turned), jnp.sin(turned))

def rotate(value_rows, cosine_table, sine_table):
    half_width = value_rows.shape[-1] // 2
    front_half = value_rows[..., :half_width]
    back_half = value_rows[..., half_width:]
    cos_part = cosine_table[:, None, :]
    sin_part = sine_table[:, None, :]
    return jnp.concatenate([front_half * cos_part - back_half * sin_part, back_half * cos_part + front_half * sin_part], axis=-1)

def forward(inputs, weight_all, gain_all, places):
    token_length = inputs.shape[0]
    query_columns = QUERY_HEADS * HEAD_SIZE
    key_columns = KEY_VALUE_HEADS * HEAD_SIZE
    w_qkv = weight_all[:, :QKVC]
    w_out = weight_all[:, QKVC:QKVC + query_columns]
    w_gateup = weight_all[:, QKVC + query_columns:QKVC + query_columns + 2 * FF]
    w_down = weight_all[:, QKVC + query_columns + 2 * FF:]
    gain_attn = gain_all[:D]
    gain_mlp = gain_all[D:2 * D]
    gain_query = gain_all[2 * D:2 * D + HEAD_SIZE]
    key_norm_gain = gain_all[2 * D + HEAD_SIZE:]
    normed = low(inputs * rms_scale(inputs) * gain_attn)
    projected_rows = low_back(jnp.dot(normed, w_qkv, precision=highest))
    query_raw = projected_rows[:, :query_columns].reshape(token_length, QUERY_HEADS, HEAD_SIZE)
    unrotated_key = projected_rows[:, query_columns:query_columns + key_columns].reshape(token_length, KEY_VALUE_HEADS, HEAD_SIZE)
    unprojected_value = projected_rows[:, query_columns + key_columns:].reshape(token_length, KEY_VALUE_HEADS, HEAD_SIZE)
    cosine_table, sine_table = angles(places, HEAD_SIZE)
    query_rows = low(rotate(query_raw * rms_scale(query_raw) * gain_query, cosine_table, sine_table))
    key_rows = low(rotate(unrotated_key * rms_scale(unrotated_key) * key_norm_gain, cosine_table, sine_table))
    value_rows = low(unprojected_value)
    allowed = places[None, :] <= places[:, None]
    query_groups = jnp.transpose(query_rows.reshape(token_length, KEY_VALUE_HEADS, QUERY_HEADS // KEY_VALUE_HEADS, HEAD_SIZE), (1, 2, 0, 3))
    key_groups = jnp.transpose(key_rows, (1, 0, 2))
    value_groups = jnp.transpose(value_rows, (1, 0, 2))

    def attend(pieces):
        query_g, key_g, value_g = pieces
        scores = low_back(jnp.einsum('rqd,kd->rqk', query_g, key_g, precision=highest) * HEAD_SIZE ** (-0.5))
        scores = jnp.where(allowed[None], scores, -1e+30)
        top_value = lax.optimization_barrier(jnp.max(scores, axis=-1, keepdims=True))
        expd = jnp.exp(scores - top_value)
        probs = low(expd / lax.optimization_barrier(jnp.sum(expd, axis=-1, keepdims=True)))
        return jnp.einsum('rqk,kd->rqd', probs, value_g, precision=highest)
    mixed = lax.map(jax.checkpoint(attend), (query_groups, key_groups, value_groups))
    attended = jnp.transpose(mixed, (2, 0, 1, 3)).reshape(token_length, query_columns)
    attended = low(low_back(attended))
    branch = low_back(jnp.dot(attended, w_out.T, precision=highest))
    middle = inputs + branch
    normed_two = low(middle * rms_scale(middle) * gain_mlp)
    gate_up = low_back(jnp.dot(normed_two, w_gateup, precision=highest))
    gate = gate_up[:, :FF]
    upper = gate_up[:, FF:]
    hidden = low(gate * jax.nn.sigmoid(gate) * upper)
    return middle + low_back(jnp.dot(hidden, w_down.T, precision=highest))

def adam(weight, grad, moment, second, rate, decay):
    moment_new = beta_one * moment + (1.0 - beta_one) * grad
    second_new = beta_two * second + (1.0 - beta_two) * grad * grad
    scaled_m = moment_new / (1.0 - beta_one ** ADAM_STEP)
    scaled_v = second_new / (1.0 - beta_two ** ADAM_STEP)
    weight_new = weight * (1.0 - rate * decay) - rate * scaled_m / (jnp.sqrt(scaled_v) + adam_eps)
    return (weight_new, moment_new, second_new)

def reference(tokens, cotangent, positions, weights, norm_gains, moment_weights, second_weights, moment_gains, second_gains):
    weight_all = weights.astype(jnp.float32)
    gain_all = norm_gains.astype(jnp.float32)
    seq_tokens = tokens.reshape(SEQS, LEN, D)
    seq_backs = cotangent.reshape(SEQS, LEN, D)
    seq_places = positions.reshape(SEQS, LEN)

    def one_sequence(carry, pieces):
        inputs, backs, places = pieces

        def layer(inputs_in, weight_in, gain_in):
            return forward(inputs_in, weight_in, gain_in, places)
        output, pull = jax.vjp(layer, inputs.astype(jnp.float32), weight_all, gain_all)
        grad_in, grad_w, grad_g = pull(backs.astype(jnp.float32))
        return ((carry[0] + grad_w, carry[1] + grad_g), (output, grad_in))
    start = (jnp.zeros(weight_all.shape, jnp.float32), jnp.zeros(gain_all.shape, jnp.float32))
    (grad_w, grad_g), (outputs, grad_inputs) = lax.scan(one_sequence, start, (seq_tokens, seq_backs, seq_places))
    total = jnp.sum(grad_w * grad_w) + jnp.sum(grad_g * grad_g)
    norm_all = jnp.sqrt(total)
    factor = jnp.minimum(1.0, clip_limit / (norm_all + 1e-06))
    column = jnp.arange(WCOLS)
    rates = jnp.where((column >= QKVC) & (column < QKVC + QUERY_HEADS * HEAD_SIZE), rate_output, rate_matrix)
    new_w, new_mw, new_vw = adam(weight_all, grad_w * factor, moment_weights, second_weights, rates[None, :], decay_rate)
    new_g, new_mg, new_vg = adam(gain_all, grad_g * factor, moment_gains, second_gains, rate_gain, 0.0)
    outputs = outputs.reshape(N_DP, ROWS_GROUP, D)
    grad_inputs = grad_inputs.reshape(N_DP, ROWS_GROUP, D)
    return (outputs, grad_inputs, norm_all.reshape(1), new_w, new_mw, new_vw, new_g, new_mg, new_vg)
```

```python
import math

import jax
import jax.numpy as jnp
from jax import lax
from jax.sharding import Mesh
from jax.sharding import PartitionSpec as P

D = 1024
FF = 3072
QUERY_HEADS = 16
KEY_VALUE_HEADS = 8
HEAD_SIZE = 128
ADAM_STEP = 10
QKVC = 4096
TP = 8
QW = 256
KW = 128
FW = FF // TP

ALL = ("ylo", "z", "yhi", "x", "core")

eps_norm = 1e-06
rope_base = 1000000.0
clip_limit = 1.0
beta_one = 0.9
beta_two = 0.95
adam_eps = 1e-08
decay_rate = 0.1
rate_matrix = 0.06
rate_output = 2.0
rate_gain = 1.0
contract_rows = (((0,), (0,)), ((), ()))
contract_cols = (((1,), (1,)), ((), ()))
f32 = jnp.float32
bf16 = jnp.bfloat16


def dot(a, b, dims=(((1,), (0,)), ((), ()))):
    return lax.dot_general(a, b, dims, preferred_element_type=f32)


def rms_scale(value_rows):
    return lax.rsqrt(jnp.mean(value_rows * value_rows, axis=-1, keepdims=True) + eps_norm)


def norm_back(value_rows, scale, gain, grad_out):
    gain_grad = jnp.sum(grad_out * value_rows * scale, axis=tuple(range(value_rows.ndim - 1)))
    weighted = grad_out * gain
    grad_in = scale * weighted - value_rows * scale * scale * scale * jnp.mean(
        weighted * value_rows, axis=-1, keepdims=True
    )
    return (grad_in, gain_grad)


def angles(places, width):
    half_width = width // 2
    inverse = jnp.exp(jnp.arange(half_width, dtype=f32) * (-2.0 / width) * math.log(rope_base))
    turned = places.astype(f32)[:, None] * inverse[None, :]
    return (jnp.cos(turned), jnp.sin(turned))


def rotate(value_rows, cosine_table, sine_table):
    half_width = value_rows.shape[-1] // 2
    front_half = value_rows[..., :half_width]
    back_half = value_rows[..., half_width:]
    cos_part = cosine_table[:, None, :]
    sin_part = sine_table[:, None, :]
    return jnp.concatenate(
        [
            front_half * cos_part - back_half * sin_part,
            back_half * cos_part + front_half * sin_part,
        ],
        axis=-1,
    )


def swap_core(v):
    return lax.ppermute(v, "core", [(0, 1), (1, 0)])


def swap_yhi(v):
    return lax.ppermute(v, "yhi", [(0, 1), (1, 0)])


def shift_x(v, k):
    return lax.ppermute(v, "x", [(i, (i + k) % 4) for i in range(4)])


def group_gather(v):
    near = jnp.concatenate([v, shift_x(v, -1), shift_x(v, -2), shift_x(v, -3)], axis=0)
    return jnp.concatenate([near, swap_core(near)], axis=0)


def group_scatter(left, right, dims):
    half = left.shape[0] // 2
    piece = half // 4
    away = swap_core(dot(left[half:], right, dims).astype(bf16))
    near = dot(left[:half], right, dims) + away.astype(f32)
    low = near.astype(bf16)
    total = near[:piece]
    for k in (1, 2, 3):
        total = total + shift_x(low[k * piece : (k + 1) * piece], k).astype(f32)
    return total


def spread(columns):
    n = columns.shape[2]
    owned = jnp.transpose(columns, (1, 0, 2)).reshape(64, n)
    sent = jnp.broadcast_to(owned[None], (16, 64, n)).reshape(1024, n)
    return lax.all_to_all(sent, ALL, 0, 0, tiled=True)


def collect(grad):
    n = grad.shape[1]
    got = lax.all_to_all(grad.astype(bf16), ALL, 0, 0, tiled=True)
    return jnp.sum(got.reshape(16, 8, 8, n).astype(f32), axis=0)


def to_columns(v):
    return jnp.transpose(v, (1, 0, 2)).reshape(8, -1)


def adam(weight, grad, moment, second, rate, decay):
    moment_new = beta_one * moment + (1.0 - beta_one) * grad
    second_new = beta_two * second + (1.0 - beta_two) * grad * grad
    scaled_m = moment_new / (1.0 - beta_one**ADAM_STEP)
    scaled_v = second_new / (1.0 - beta_two**ADAM_STEP)
    weight_new = weight * (1.0 - rate * decay) - rate * scaled_m / (jnp.sqrt(scaled_v) + adam_eps)
    return (weight_new, moment_new, second_new)


def slot_places(positions):
    seq = lax.axis_index("ylo") * 4 + lax.axis_index("z")
    table = lax.dynamic_index_in_dim(positions, seq, 0, keepdims=False).reshape(2, 4, 2, 128)
    xi = lax.axis_index("x")
    table = lax.dynamic_slice_in_dim(jnp.concatenate([table, table], axis=1), xi, 4, axis=1)
    table = jnp.transpose(table, (0, 2, 1, 3))
    table = jnp.where(lax.axis_index("core") == 0, table, table[:, ::-1])
    table = jnp.where(lax.axis_index("yhi") == 0, table, table[::-1])
    return table.reshape(2048)


def body(
    tokens,
    cotangent,
    positions,
    weights,
    norm_gains,
    moment_weights,
    second_weights,
    moment_gains,
    second_gains,
):
    scale = HEAD_SIZE ** (-0.5)
    o_q, o_k, o_v, o_o = 0, 2048, 3072, 4096
    o_g, o_u, o_d = 6144, 6144 + FF, 6144 + 2 * FF
    w_q = weights[:, o_q:o_k].reshape(8, 8, QW)
    w_k = weights[:, o_k:o_v].reshape(8, 8, KW)
    w_v = weights[:, o_v:o_o].reshape(8, 8, KW)
    w_o = weights[:, o_o:o_g].reshape(8, 8, QW)
    w_g = weights[:, o_g:o_u].reshape(8, 8, FW)
    w_u = weights[:, o_u:o_d].reshape(8, 8, FW)
    w_d = weights[:, o_d:].reshape(8, 8, FW)
    gain_all = (
        lax.all_to_all(
            jnp.broadcast_to(norm_gains[None], (128, 18)), ALL, 0, 0, tiled=True
        )
        .reshape(2304)
        .astype(f32)
    )
    w_qkv = spread(jnp.concatenate([w_q, w_k, w_v], axis=2))
    w_rest = spread(jnp.concatenate([w_o, w_g, w_u, w_d], axis=2))
    w_out = w_rest[:, :QW]
    w_gateup = w_rest[:, QW : QW + 2 * FW]
    w_down = w_rest[:, QW + 2 * FW :]
    gain_attn = gain_all[:D]
    gain_mlp = gain_all[D : 2 * D]
    gain_query = gain_all[2 * D : 2 * D + HEAD_SIZE]
    gain_key = gain_all[2 * D + HEAD_SIZE :]

    places_all = slot_places(positions)
    places = places_all[:1024]
    cosine_table, sine_table = angles(places, HEAD_SIZE)

    own = tokens[0].astype(f32)
    own_back = cotangent[0].astype(f32)
    inputs = group_gather(tokens[0]).astype(f32)
    backs_low = group_gather(cotangent[0])

    scale_one = rms_scale(inputs)
    normed = (inputs * scale_one * gain_attn).astype(bf16)
    projected = dot(normed, w_qkv)
    query_raw = projected[:, :QW].reshape(1024, 2, HEAD_SIZE)
    key_raw = projected[:, QW : QW + KW].reshape(1024, 1, HEAD_SIZE)
    scale_q = rms_scale(query_raw)
    scale_k = rms_scale(key_raw)
    query_rows = rotate(query_raw * scale_q * gain_query, cosine_table, sine_table).astype(bf16)
    key_rows = rotate(key_raw * scale_k * gain_key, cosine_table, sine_table).astype(bf16)
    pair = jnp.concatenate(
        [key_rows.reshape(1024, HEAD_SIZE), projected[:, QW + KW :].astype(bf16)], axis=1
    )
    pair_all = jnp.concatenate([pair, swap_yhi(pair)], axis=0)
    key_all = pair_all[:, :HEAD_SIZE]
    value_all = pair_all[:, HEAD_SIZE:]
    query_heads = jnp.transpose(query_rows, (1, 0, 2))
    allowed = places_all[None, :] <= places[:, None]

    def attend(query_h):
        scores = dot(query_h, key_all, contract_cols) * scale
        scores = jnp.where(allowed, scores, -1e30)
        top = jnp.max(scores, axis=-1, keepdims=True)
        expd = jnp.exp(scores - top)
        total = jnp.sum(expd, axis=-1, keepdims=True)
        probs = (expd / total).astype(bf16)
        return (dot(probs, value_all), top[..., 0] + jnp.log(total[..., 0]))

    mixed, logsum = lax.map(attend, query_heads)
    attended = jnp.transpose(mixed, (1, 0, 2)).reshape(1024, QW).astype(bf16)

    middle = own + group_scatter(attended, w_out, contract_cols)
    scale_two = rms_scale(middle)
    normed_two = group_gather((middle * scale_two * gain_mlp).astype(bf16))
    gate_up = dot(normed_two, w_gateup)
    gate = gate_up[:, :FW]
    upper = gate_up[:, FW:]
    sigma = jax.nn.sigmoid(gate)
    hidden = (gate * sigma * upper).astype(bf16)
    grad_hidden = dot(backs_low, w_down)
    grad_gate = grad_hidden * upper * sigma * (1.0 + gate * (1.0 - sigma))
    grad_up = grad_hidden * gate * sigma
    grad_gu = jnp.concatenate([grad_gate, grad_up], axis=1).astype(bf16)
    grad_normed_two = group_scatter(grad_gu, w_gateup, contract_cols)
    output = middle + group_scatter(hidden, w_down, contract_cols)
    term_mlp = jnp.concatenate(
        [dot(normed_two, grad_gu, contract_rows), dot(backs_low, hidden, contract_rows)], axis=1
    )
    share_mlp = collect(term_mlp)

    grad_mid_part, gain_mlp_grad = norm_back(middle, scale_two, gain_mlp, grad_normed_two)
    grad_mid = own_back + grad_mid_part
    grad_mid_low = group_gather(grad_mid.astype(bf16))
    term_out = dot(grad_mid_low, attended, contract_rows)
    share_out = collect(term_out)
    grad_att = dot(grad_mid_low, w_out).astype(bf16)
    grad_heads = jnp.transpose(grad_att.reshape(1024, 2, HEAD_SIZE), (1, 0, 2))

    def attend_back(carry, pieces):
        query_h, grad_h, logsum_h = pieces
        scores = dot(query_h, key_all, contract_cols) * scale
        probs = jnp.where(allowed, jnp.exp(scores - logsum_h[:, None]), 0.0)
        grad_p = dot(grad_h, value_all, contract_cols)
        inner = jnp.sum(probs * grad_p, axis=-1, keepdims=True)
        grad_s = (probs * (grad_p - inner)).astype(bf16)
        grad_q = dot(grad_s, key_all) * scale
        grad_k = dot(grad_s, query_h, contract_rows) * scale
        grad_v = dot(probs.astype(bf16), grad_h, contract_rows)
        return ((carry[0] + grad_k, carry[1] + grad_v), grad_q)

    start = (jnp.zeros((2048, HEAD_SIZE), f32), jnp.zeros((2048, HEAD_SIZE), f32))
    (grad_key, grad_value), grad_qh = lax.scan(
        attend_back, start, (query_heads, grad_heads, logsum)
    )
    grad_pair = jnp.concatenate([grad_key, grad_value], axis=1)
    grad_pair = grad_pair[:1024] + swap_yhi(grad_pair[1024:].astype(bf16)).astype(f32)
    grad_query = jnp.transpose(grad_qh, (1, 0, 2))

    grad_query_raw, gain_q_grad = norm_back(
        query_raw, scale_q, gain_query, rotate(grad_query, cosine_table, -sine_table)
    )
    grad_key_raw, gain_k_grad = norm_back(
        key_raw,
        scale_k,
        gain_key,
        rotate(grad_pair[:, :HEAD_SIZE].reshape(1024, 1, HEAD_SIZE), cosine_table, -sine_table),
    )
    grad_proj = jnp.concatenate(
        [
            grad_query_raw.reshape(1024, QW),
            grad_key_raw.reshape(1024, KW),
            grad_pair[:, HEAD_SIZE:],
        ],
        axis=1,
    ).astype(bf16)
    term_qkv = dot(normed, grad_proj, contract_rows)
    share_qkv = collect(term_qkv)

    grad_normed = group_scatter(grad_proj, w_qkv, contract_cols)
    own_scale = rms_scale(own)
    grad_in_part, gain_attn_grad = norm_back(own, own_scale, gain_attn, grad_normed)
    grad_inputs = grad_mid + grad_in_part

    gain_term = jnp.concatenate([gain_attn_grad, gain_mlp_grad, gain_q_grad, gain_k_grad])
    gain_grad = jnp.sum(
        lax.all_to_all(gain_term.reshape(128, 18), ALL, 0, 0, tiled=True), axis=0
    )
    grad_share = jnp.concatenate(
        [
            to_columns(share_qkv[:, :, :QW]),
            to_columns(share_qkv[:, :, QW : QW + KW]),
            to_columns(share_qkv[:, :, QW + KW :]),
            to_columns(share_out),
            to_columns(share_mlp[:, :, :FW]),
            to_columns(share_mlp[:, :, FW : 2 * FW]),
            to_columns(share_mlp[:, :, 2 * FW :]),
        ],
        axis=1,
    )
    squares = jnp.sum(grad_share * grad_share) + jnp.sum(gain_grad * gain_grad)
    shared = lax.all_to_all(jnp.broadcast_to(squares, (128, 128)), ALL, 0, 0, tiled=True)
    norm_all = jnp.sqrt(jnp.sum(shared[:, 0]))
    factor = jnp.minimum(1.0, clip_limit / (norm_all + 1e-06))
    column = jnp.arange(grad_share.shape[1])
    rates = jnp.where(
        (column >= QKVC) & (column < QKVC + QUERY_HEADS * HEAD_SIZE), rate_output, rate_matrix
    )
    new_w, new_mw, new_vw = adam(
        weights.astype(f32),
        grad_share * factor,
        moment_weights,
        second_weights,
        rates[None, :],
        decay_rate,
    )
    new_g, new_mg, new_vg = adam(
        norm_gains.astype(f32),
        gain_grad * factor,
        moment_gains,
        second_gains,
        rate_gain,
        0.0,
    )
    return (
        output[None],
        grad_inputs[None],
        norm_all.reshape(1),
        new_w,
        new_mw,
        new_vw,
        new_g,
        new_mg,
        new_vg,
    )


def solution(mesh):
    parts = Mesh(mesh.devices.reshape(2, 4, 2, 4, 2), ALL)
    rows = P(("ylo", "z"), ("yhi", "x", "core"), None)
    owned = P(ALL, None)
    small = P(ALL)
    return jax.shard_map(
        body,
        mesh=parts,
        in_specs=(rows, rows, P(), owned, small, owned, owned, small, small),
        out_specs=(rows, rows, P(), owned, owned, owned, small, small, small),
        check_vma=False,
    )
```

```python
import functools
import math

import jax
import jax.numpy as jnp
from jax import lax
from jax.experimental import pallas as pl
from jax.experimental.pallas import tpu as pltpu
from jax.sharding import Mesh
from jax.sharding import PartitionSpec as P

D = 1024
FF = 3072
QUERY_HEADS = 16
KEY_VALUE_HEADS = 8
HEAD_SIZE = 128
ADAM_STEP = 10
QKVC = 4096
TP = 8
QW = 256
KW = 128
FW = FF // TP
BLK = 64
TILE = 256

ALL = ("ylo", "z", "yhi", "x", "core")
PLANE = ("ylo", "z", "yhi")
GROUP = ("x", "core")

eps_norm = 1e-06
rope_base = 1000000.0
clip_limit = 1.0
beta_one = 0.9
beta_two = 0.95
adam_eps = 1e-08
decay_rate = 0.1
rate_matrix = 0.06
rate_output = 2.0
rate_gain = 1.0
contract_rows = (((0,), (0,)), ((), ()))
contract_cols = (((1,), (1,)), ((), ()))
f32 = jnp.float32
bf16 = jnp.bfloat16


def dot(a, b, dims=(((1,), (0,)), ((), ()))):
    return lax.dot_general(a, b, dims, preferred_element_type=f32)


def rms_scale(value_rows):
    return lax.rsqrt(jnp.mean(value_rows * value_rows, axis=-1, keepdims=True) + eps_norm)


def norm_back(value_rows, scale, gain, grad_out):
    gain_grad = jnp.sum(grad_out * value_rows * scale, axis=tuple(range(value_rows.ndim - 1)))
    weighted = grad_out * gain
    grad_in = scale * weighted - value_rows * scale * scale * scale * jnp.mean(
        weighted * value_rows, axis=-1, keepdims=True
    )
    return (grad_in, gain_grad)


def turn_tables(blocks):
    half = HEAD_SIZE // 2
    inverse = jnp.exp(jnp.arange(half, dtype=f32) * (-2.0 / HEAD_SIZE) * math.log(rope_base))
    inverse = jnp.concatenate([inverse, inverse])
    coarse = (blocks * BLK).astype(f32)[:, None] * inverse[None, :]
    fine = jnp.arange(BLK, dtype=f32)[:, None] * inverse[None, :]
    sign = jnp.where(jnp.arange(HEAD_SIZE) < half, -1.0, 1.0)
    cos_a, sin_a, cos_b, sin_b = lax.optimization_barrier(
        (jnp.cos(coarse), jnp.sin(coarse), jnp.cos(fine), jnp.sin(fine))
    )
    cos_a, sin_a = cos_a[:, None, :], sin_a[:, None, :]
    cosine = cos_a * cos_b - sin_a * sin_b
    sine = (sin_a * cos_b + cos_a * sin_b) * sign
    return (cosine.reshape(-1, HEAD_SIZE), sine.reshape(-1, HEAD_SIZE))


def swap_core(v):
    return lax.ppermute(v, "core", [(0, 1), (1, 0)])


def swap_yhi(v):
    return lax.ppermute(v, "yhi", [(0, 1), (1, 0)])


def shift_x(v, k):
    return lax.ppermute(v, "x", [(i, (i + k) % 4) for i in range(4)])


def y_index(p):
    return (p % 2) * 2 + p // 2


def shift_y(v, k):
    return lax.ppermute(v, ("ylo", "yhi"), [(y_index(i), y_index((i + k) % 4)) for i in range(4)])


def shift_z(v, k):
    return lax.ppermute(v, "z", [(i, (i + k) % 4) for i in range(4)])


def idle_kernel(*refs):
    pass


def after(v, *waits):
    return pl.pallas_call(
        idle_kernel,
        out_shape=jax.ShapeDtypeStruct(v.shape, v.dtype),
        in_specs=[pl.BlockSpec(memory_space=pl.ANY)] * (1 + len(waits)),
        out_specs=pl.BlockSpec(memory_space=pl.ANY),
        input_output_aliases={0: 0},
        cost_estimate=pl.CostEstimate(flops=0, bytes_accessed=0, transcendentals=0),
        name="after",
    )(v, *waits)


def near_gather(v):
    return jnp.concatenate([v, shift_x(v, -1), shift_x(v, -2), shift_x(v, -3)], axis=0)


def group_gather(v):
    near = near_gather(v)
    return jnp.concatenate([near, swap_core(near)], axis=0)


def group_scatter(left, right, dims):
    half = left.shape[0] // 2
    away = dot(left[half:], right, dims).astype(bf16)
    return group_fold(dot(left[:half], right, dims), away)


def group_fold(near, away):
    piece = near.shape[0] // 4
    near = near + swap_core(away).astype(f32)
    low = near.astype(bf16)
    total = near[:piece]
    for k in (1, 2, 3):
        total = total + shift_x(low[k * piece : (k + 1) * piece], k).astype(f32)
    return total


def to_owners(columns):
    return jnp.transpose(columns, (1, 0, 2)).reshape(64, columns.shape[2])


def to_all(columns):
    n = columns.shape[2]
    return jnp.broadcast_to(to_owners(columns)[None], (16, 64, n)).reshape(1024, n)


def plane_sum(grad):
    n = grad.shape[1]
    got = lax.all_to_all(grad.astype(bf16), PLANE, 0, 0, tiled=True)
    return jnp.sum(got.reshape(16, 64, n).astype(f32), axis=0)


def adam(weight, grad, moment, second, rate, decay):
    moment_new = beta_one * moment + (1.0 - beta_one) * grad
    second_new = beta_two * second + (1.0 - beta_two) * grad * grad
    scaled_m = moment_new / (1.0 - beta_one**ADAM_STEP)
    scaled_v = second_new / (1.0 - beta_two**ADAM_STEP)
    weight_new = weight * (1.0 - rate * decay) - rate * scaled_m / (jnp.sqrt(scaled_v) + adam_eps)
    return (weight_new, moment_new, second_new)


def sort_blocks(table, pair, keys, values):
    for i in range(32):
        spot = pl.ds(pl.multiple_of(table[i] * BLK, BLK), BLK)
        keys[spot, :] = pair[i * BLK : (i + 1) * BLK, :HEAD_SIZE]
        values[spot, :] = pair[i * BLK : (i + 1) * BLK, HEAD_SIZE:]


def flip(v):
    return jnp.transpose(v.astype(f32)).astype(bf16)


def stack_heads(ref, rows):
    return jnp.concatenate([ref[rows, :HEAD_SIZE], ref[rows, HEAD_SIZE:]], axis=0)


def seen(place, first, count):
    key_place = first + lax.broadcasted_iota(jnp.int32, (count, 2 * BLK), 0)
    lane = lax.broadcasted_iota(jnp.int32, (count, 2 * BLK), 1)
    return key_place <= place * BLK + lax.rem(lane, BLK)


def attend_kernel(table, query, pair, out, logsum, keys, values, values_t):
    scale = HEAD_SIZE ** (-0.5)
    sort_blocks(table, pair, keys, values)
    for t in range(8):
        values_t[:, t * TILE : (t + 1) * TILE] = flip(values[t * TILE : (t + 1) * TILE, :])

    def block(i, carry):
        place = table[i]
        rows = pl.ds(pl.multiple_of(i * BLK, BLK), BLK)

        def run(count):
            full = count - TILE
            stacked = stack_heads(query, rows)
            tail = dot(keys[full:count, :], stacked, contract_cols)
            tail = jnp.where(seen(place, full, TILE), tail, -1e30)
            top = jnp.max(tail, axis=0, keepdims=True)
            if full:
                head = dot(keys[:full, :], stacked, contract_cols)
                top = jnp.maximum(top, jnp.max(head, axis=0, keepdims=True))
            tail = jnp.exp((tail - top) * scale)
            total = jnp.sum(tail, axis=0, keepdims=True)
            mixed = dot(values_t[:, full:count], tail.astype(bf16))
            if full:
                head = jnp.exp((head - top) * scale)
                total = total + jnp.sum(head, axis=0, keepdims=True)
                mixed = mixed + dot(values_t[:, :full], head.astype(bf16))
            mixed = jnp.transpose(mixed / total).astype(bf16)
            out[rows, :HEAD_SIZE] = mixed[:BLK]
            out[rows, HEAD_SIZE:] = mixed[BLK:]
            logsum[pl.ds(i, 1), :] = top * scale + jnp.log(total)

        for step in range(8):
            pl.when(lax.div(place, 4) == step)(functools.partial(run, (step + 1) * TILE))
        return carry

    lax.fori_loop(0, 16, block, 0)


def turn(v):
    return jnp.concatenate([v[:, HEAD_SIZE // 2 :], v[:, : HEAD_SIZE // 2]], axis=1)


def head_back(raw, grad, gain, cosine, sine):
    grad = grad * cosine - turn(grad) * sine
    scale = lax.rsqrt(jnp.mean(raw * raw, axis=-1, keepdims=True) + eps_norm)
    gain_grad = jnp.sum(grad * raw * scale, axis=0, keepdims=True)
    weighted = grad * gain
    mean = jnp.mean(weighted * raw, axis=-1, keepdims=True)
    return (scale * weighted - raw * (scale * scale * scale * mean), gain_grad)


def attend_back_kernel(
    table, query, pair, out, logsum,
    query_raw, key_raw, cosine, sine, gains, gain_mlp, plain, mid_near, mid_far, weight_out, idle,
    last, grad_query, grad_own, grad_away,
    keys, values, keys_t, acc_key, acc_value, pair_near, pair_far, query_acc, grad,
):
    scale = HEAD_SIZE ** (-0.5)
    grad[:512, :] = dot(mid_near[...], weight_out[...]).astype(bf16)
    grad[512:, :] = dot(mid_far[...], weight_out[...]).astype(bf16)
    sort_blocks(table, pair, keys, values)
    acc_key[...] = jnp.zeros_like(acc_key)
    acc_value[...] = jnp.zeros_like(acc_value)
    for t in range(8):
        keys_t[:, t * TILE : (t + 1) * TILE] = flip(keys[t * TILE : (t + 1) * TILE, :])

    def block(i, carry):
        place = table[i]
        rows = pl.ds(pl.multiple_of(i * BLK, BLK), BLK)

        def run(count):
            stacked = stack_heads(query, rows)
            back = stack_heads(grad, rows)
            made = stack_heads(out, rows)
            inner = jnp.sum(
                jnp.transpose(back.astype(f32) * made.astype(f32)), axis=0, keepdims=True
            )
            level = logsum[pl.ds(i, 1), :]
            total = jnp.zeros((HEAD_SIZE, 2 * BLK), f32)
            for first in range(0, count, TILE):
                span = slice(first, first + TILE)
                probs = jnp.exp(dot(keys[span, :], stacked, contract_cols) * scale - level)
                if first + TILE == count:
                    probs = jnp.where(seen(place, first, TILE), probs, 0.0)
                grad_p = dot(values[span, :], back, contract_cols)
                grad_s = (probs * (grad_p - inner)).astype(bf16)
                acc_key[span, :] += dot(grad_s, stacked)
                acc_value[span, :] += dot(probs.astype(bf16), back)
                total = total + dot(keys_t[:, span], grad_s)
            total = jnp.transpose(total) * scale
            query_acc[rows, :HEAD_SIZE] = total[:BLK]
            query_acc[rows, HEAD_SIZE:] = total[BLK:]

        for step in range(8):
            pl.when(lax.div(place, 4) == step)(functools.partial(run, (step + 1) * TILE))
        return carry

    lax.fori_loop(0, 16, block, 0)
    for i in range(16):
        rows = slice(i * BLK, (i + 1) * BLK)
        near = pl.ds(pl.multiple_of(table[i] * BLK, BLK), BLK)
        grad_own[rows, :HEAD_SIZE] = acc_key[near, :] * scale
        grad_own[rows, HEAD_SIZE:] = acc_value[near, :]
        far = pl.ds(pl.multiple_of(table[16 + i] * BLK, BLK), BLK)
        pair_far[rows, :HEAD_SIZE] = acc_key[far, :] * scale
        pair_far[rows, HEAD_SIZE:] = acc_value[far, :]
    grad_away[...] = pair_far[...].astype(bf16)

    gain_q = gains[0:1, :]
    gain_k = gains[1:2, :]
    sum_q = jnp.zeros((1, HEAD_SIZE), f32)
    sum_k = jnp.zeros((1, HEAD_SIZE), f32)
    for t in range(4):
        rows = slice(t * TILE, (t + 1) * TILE)
        rows_far = slice(1024 + t * TILE, 1024 + (t + 1) * TILE)
        for h in range(2):
            cols = slice(h * HEAD_SIZE, (h + 1) * HEAD_SIZE)
            made, part = head_back(
                query_raw[rows, cols], query_acc[rows, cols], gain_q, cosine[rows, :], sine[rows, :]
            )
            grad_query[rows, cols] = made.astype(bf16)
            sum_q = sum_q + part
        made, part = head_back(
            key_raw[rows, :], grad_own[rows, :HEAD_SIZE], gain_k, cosine[rows, :], sine[rows, :]
        )
        pair_near[rows, :HEAD_SIZE] = made
        pair_near[rows, HEAD_SIZE:] = grad_own[rows, HEAD_SIZE:]
        sum_k = sum_k + part
        made, part = head_back(
            key_raw[rows_far, :], pair_far[rows, :HEAD_SIZE], gain_k,
            cosine[rows_far, :], sine[rows_far, :],
        )
        pair_far[rows, :HEAD_SIZE] = made
        sum_k = sum_k + part

    def down(ref):
        return jnp.transpose(ref[...].astype(f32)).astype(bf16)

    query_t = down(grad_query)
    near_t = down(pair_near)
    far_t = down(pair_far)
    out_t = down(out)
    for t in range(4):
        rows = slice(t * TILE, (t + 1) * TILE)
        made = dot(query_t, plain[:1024, rows])
        last[rows, :QW] = jnp.transpose(made).astype(bf16)
        made = dot(near_t, plain[:1024, rows]) + dot(far_t, plain[1024:, rows])
        last[rows, QW : 2 * QW] = jnp.transpose(made).astype(bf16)
        made = dot(out_t[:, :512], mid_near[:, rows]) + dot(out_t[:, 512:], mid_far[:, rows])
        last[rows, 2 * QW : 3 * QW] = jnp.transpose(made).astype(bf16)
    last[:, 3 * QW :] = jnp.zeros((1024, 128), bf16)
    lines = [gain_mlp[k : k + 1, :] for k in range(8)] + [sum_q, sum_k]
    row = lax.broadcasted_iota(jnp.int32, (16, HEAD_SIZE), 0)
    for k in range(5):
        made = jnp.zeros((16, HEAD_SIZE), f32)
        for at, line in ((0, lines[2 * k]), (8, lines[2 * k + 1])):
            high = line.astype(bf16).astype(f32)
            made = jnp.where(row == at, high, made)
            made = jnp.where(row == at + 1, line - high, made)
        last[16 * k : 16 * k + 16, 3 * QW :] = made.astype(bf16)


def in_vmem():
    return pl.BlockSpec(memory_space=pltpu.VMEM)


def in_smem():
    return pl.BlockSpec(memory_space=pltpu.SMEM)


def project_kernel(
    tokens, gain, weight_q, weight_kv, gains, cosine, sine, idle,
    plain, query, query_raw, pair, key_raw,
):
    rows = tokens[...].astype(f32)
    scaled = rows * lax.rsqrt(jnp.mean(rows * rows, axis=-1, keepdims=True) + eps_norm)
    plain[...] = scaled.astype(bf16)
    normed = (scaled * gain[...]).astype(bf16)

    def head(raw, head_gain):
        scale = lax.rsqrt(jnp.mean(raw * raw, axis=-1, keepdims=True) + eps_norm)
        made = raw * scale * head_gain
        return (made * cosine[...] + turn(made) * sine[...]).astype(bf16)

    made = dot(normed, weight_kv[...])
    key_raw[...] = made[:, :KW]
    pair[:, :KW] = head(made[:, :KW], gains[1:2, :])
    pair[:, KW:] = made[:, KW:].astype(bf16)

    @pl.when(pl.program_id(0) < 4)
    def _():
        made = dot(normed, weight_q[...])
        query_raw[...] = made
        for h in range(2):
            cols = slice(h * HEAD_SIZE, (h + 1) * HEAD_SIZE)
            query[:, cols] = head(made[:, cols], gains[0:1, :])


def project(tokens, gain, weight_q, weight_kv, gains, cosine, sine, idle):
    def rows(width):
        return pl.BlockSpec((TILE, width), lambda t: (t, 0))

    def first(width):
        return pl.BlockSpec((TILE, width), lambda t: (jnp.minimum(t, 3), 0))

    def whole(v):
        return pl.BlockSpec(v.shape, lambda t: (0, 0))

    return pl.pallas_call(
        project_kernel,
        grid=(8,),
        out_shape=[
            jax.ShapeDtypeStruct((2048, D), bf16),
            jax.ShapeDtypeStruct((1024, QW), bf16),
            jax.ShapeDtypeStruct((1024, QW), f32),
            jax.ShapeDtypeStruct((2048, QW), bf16),
            jax.ShapeDtypeStruct((2048, KW), f32),
        ],
        in_specs=[
            rows(D), whole(gain), whole(weight_q), whole(weight_kv), whole(gains),
            rows(HEAD_SIZE), rows(HEAD_SIZE), pl.BlockSpec(memory_space=pl.ANY),
        ],
        out_specs=[rows(D), first(QW), first(QW), rows(QW), rows(KW)],
        compiler_params=pltpu.CompilerParams(vmem_limit_bytes=32 * 2**20),
        name="project",
    )(tokens, gain, weight_q, weight_kv, gains, cosine, sine, idle)


def mlp_kernel(
    near, far, backs, weight, down, normed, hidden, grad_gu, low, total
):
    step = pl.program_id(0)
    rows = jnp.where(step < 2, far[...], near[...])
    normed[...] = rows
    made = dot(rows, weight[...])
    gate = made[:, :FW]
    upper = made[:, FW:]
    sigma = jax.nn.sigmoid(gate)
    acted = gate * sigma
    hidden[...] = (acted * upper).astype(bf16)
    grad = dot(backs[...], down[...])
    grad_gu[:, :FW] = (grad * upper * sigma * (1.0 + gate * (1.0 - sigma))).astype(bf16)
    grad_gu[:, FW:] = (grad * acted).astype(bf16)
    part = dot(grad_gu[...], weight[...], contract_cols)

    @pl.when(step < 2)
    def _():
        low[...] = part.astype(bf16)

    @pl.when(step >= 2)
    def _():
        total[...] = part


def mlp(near, far, backs, weight, down):
    def rows(width):
        return pl.BlockSpec((TILE, width), lambda t: (lax.rem(t + 2, 4), 0))

    def early(width):
        return pl.BlockSpec((TILE, width), lambda t: (jnp.minimum(t, 1), 0))

    def late(width):
        return pl.BlockSpec((TILE, width), lambda t: (jnp.maximum(t - 2, 0), 0))

    def whole(v):
        return pl.BlockSpec(v.shape, lambda t: (0, 0))

    return pl.pallas_call(
        mlp_kernel,
        grid=(4,),
        out_shape=[
            jax.ShapeDtypeStruct((1024, D), bf16),
            jax.ShapeDtypeStruct((1024, FW), bf16),
            jax.ShapeDtypeStruct((1024, 2 * FW), bf16),
            jax.ShapeDtypeStruct((512, D), bf16),
            jax.ShapeDtypeStruct((512, D), f32),
        ],
        in_specs=[late(D), early(D), rows(D), whole(weight), whole(down)],
        out_specs=[rows(D), rows(FW), rows(2 * FW), early(D), late(D)],
        compiler_params=pltpu.CompilerParams(vmem_limit_bytes=40 * 2**20),
        name="mlp",
    )(near, far, backs, weight, down)


def attend(table, query, pair, *idle):
    return pl.pallas_call(
        lambda table, query, pair, *refs: attend_kernel(table, query, pair, *refs[len(idle) :]),
        out_shape=[
            jax.ShapeDtypeStruct((1024, QW), bf16),
            jax.ShapeDtypeStruct((16, 2 * BLK), f32),
        ],
        in_specs=[in_smem()]
        + [in_vmem()] * 2
        + [pl.BlockSpec(memory_space=pl.ANY)] * len(idle),
        out_specs=[in_vmem()] * 2,
        scratch_shapes=[
            pltpu.VMEM((2048, HEAD_SIZE), bf16),
            pltpu.VMEM((2048, HEAD_SIZE), bf16),
            pltpu.VMEM((HEAD_SIZE, 2048), bf16),
        ],
        compiler_params=pltpu.CompilerParams(vmem_limit_bytes=48 * 2**20),
        cost_estimate=pl.CostEstimate(flops=1000000, bytes_accessed=100000, transcendentals=0),
        name="attend",
    )(table, query, pair, *idle)


def attend_back(*args):
    return pl.pallas_call(
        attend_back_kernel,
        out_shape=[
            jax.ShapeDtypeStruct((1024, 3 * QW + 128), bf16),
            jax.ShapeDtypeStruct((1024, QW), bf16),
            jax.ShapeDtypeStruct((1024, QW), f32),
            jax.ShapeDtypeStruct((1024, QW), bf16),
        ],
        in_specs=[in_smem()]
        + [in_vmem()] * (len(args) - 2)
        + [pl.BlockSpec(memory_space=pl.ANY)],
        out_specs=[in_vmem()] * 4,
        scratch_shapes=[
            pltpu.VMEM((2048, HEAD_SIZE), bf16),
            pltpu.VMEM((2048, HEAD_SIZE), bf16),
            pltpu.VMEM((HEAD_SIZE, 2048), bf16),
            pltpu.VMEM((2048, HEAD_SIZE), f32),
            pltpu.VMEM((2048, HEAD_SIZE), f32),
            pltpu.VMEM((1024, QW), f32),
            pltpu.VMEM((1024, QW), f32),
            pltpu.VMEM((1024, QW), f32),
            pltpu.VMEM((1024, QW), bf16),
        ],
        compiler_params=pltpu.CompilerParams(vmem_limit_bytes=48 * 2**20),
        cost_estimate=pl.CostEstimate(
            flops=3100000000, bytes_accessed=6000000, transcendentals=2400000
        ),
        name="attend_back",
    )(*args)


def collect_kernel(got, mlp, weights, own_gain, share, stats):
    total = got[0:64, :].astype(f32)
    for k in range(1, 16):
        total = total + got[64 * k : 64 * k + 64, :].astype(f32)
    gain_sum = total[0:1, 3 * QW :] + total[1:2, 3 * QW :]
    squares = jnp.zeros((8, HEAD_SIZE), f32)
    for j in range(1, 8):
        gain_sum = gain_sum + total[8 * j : 8 * j + 1, 3 * QW :]
        gain_sum = gain_sum + total[8 * j + 1 : 8 * j + 2, 3 * QW :]
    gain_part = jnp.zeros((8, HEAD_SIZE), f32)
    gain = own_gain[...]
    at_mlp = QKVC + 8 * QW

    def fold(v):
        made = v[:, :HEAD_SIZE]
        for k in range(1, v.shape[1] // HEAD_SIZE):
            made = made + v[:, k * HEAD_SIZE : (k + 1) * HEAD_SIZE]
        return made

    for j in range(8):
        rows = slice(8 * j, 8 * j + 8)
        for at, width, base in ((0, QW, 0), (QW, KW, 2048), (QW + KW, KW, 3072)):
            spot = slice(base + j * width, base + (j + 1) * width)
            plain = total[rows, at : at + width]
            gain_part = gain_part + fold(plain * weights[:, spot].astype(f32))
            made = plain * gain
            share[:, spot] = made
            squares = squares + fold(made * made)
        made = total[rows, 2 * QW : 3 * QW]
        share[:, QKVC + j * QW : QKVC + (j + 1) * QW] = made
        squares = squares + fold(made * made)
        for part in range(3):
            made = mlp[rows, part * FW : (part + 1) * FW]
            first = at_mlp + part * FF + j * FW
            share[:, first : first + FW] = made
            squares = squares + fold(made * made)
    attn = jnp.sum(gain_part, axis=1, keepdims=True)
    whole = jnp.sum(squares) + jnp.sum(gain_sum * gain_sum) + jnp.sum(attn * attn)
    row = lax.broadcasted_iota(jnp.int32, (8, HEAD_SIZE), 0)
    lane = lax.broadcasted_iota(jnp.int32, (8, HEAD_SIZE), 1)
    own_attn = jnp.sum(jnp.where(lane == row, attn, 0.0), axis=0, keepdims=True)
    first = lax.broadcasted_iota(jnp.int32, (1, HEAD_SIZE), 1)
    stats[:, :HEAD_SIZE] = gain_sum
    stats[:, HEAD_SIZE:] = jnp.where(first == 8, whole, own_attn)


def collect(got, mlp, weights, own_gain):
    return pl.pallas_call(
        collect_kernel,
        out_shape=[
            jax.ShapeDtypeStruct((8, 15360), f32),
            jax.ShapeDtypeStruct((1, 2 * HEAD_SIZE), f32),
        ],
        in_specs=[in_vmem()] * 4,
        out_specs=[in_vmem()] * 2,
        compiler_params=pltpu.CompilerParams(vmem_limit_bytes=32 * 2**20),
        name="collect",
    )(got, mlp, weights, own_gain)


def slot_places(positions):
    seq = lax.axis_index("ylo") * 4 + lax.axis_index("z")
    table = lax.dynamic_index_in_dim(positions, seq, 0, keepdims=False).reshape(2, 4, 2, 128)
    xi = lax.axis_index("x")
    table = lax.dynamic_slice_in_dim(jnp.concatenate([table, table], axis=1), xi, 4, axis=1)
    table = jnp.transpose(table, (0, 2, 1, 3))
    table = jnp.where(lax.axis_index("core") == 0, table, table[:, ::-1])
    table = jnp.where(lax.axis_index("yhi") == 0, table, table[::-1])
    return table.reshape(2048)


def body(
    tokens,
    cotangent,
    positions,
    weights,
    norm_gains,
    moment_weights,
    second_weights,
    moment_gains,
    second_gains,
):
    o_q, o_k, o_v, o_o = 0, 2048, 3072, 4096
    o_g, o_u, o_d = 6144, 6144 + FF, 6144 + 2 * FF
    w_q = weights[:, o_q:o_k].reshape(8, 8, QW)
    w_k = weights[:, o_k:o_v].reshape(8, 8, KW)
    w_v = weights[:, o_v:o_o].reshape(8, 8, KW)
    w_o = weights[:, o_o:o_g].reshape(8, 8, QW)
    w_g = weights[:, o_g:o_u].reshape(8, 8, FW)
    w_u = weights[:, o_u:o_d].reshape(8, 8, FW)
    w_d = weights[:, o_d:].reshape(8, 8, FW)
    rank = lax.axis_index("ylo")
    for name, size in (("z", 4), ("yhi", 2), ("x", 4), ("core", 2)):
        rank = rank * size + lax.axis_index(name)
    own = tokens[0].astype(f32)
    own_back = cotangent[0].astype(f32)

    w_gains = jnp.pad(norm_gains.reshape(1, 1, 18), ((0, 7), (0, 0), (0, 110)))
    sent = to_all(jnp.concatenate([w_q, w_k, w_v, w_o, jnp.broadcast_to(w_gains, (8, 8, 128))], axis=2))
    w_first = lax.all_to_all(sent, ALL, 0, 0, tiled=True)
    both = jnp.stack([tokens[0], swap_yhi(tokens[0])]).reshape(256, D)
    near = near_gather(both)
    tokens_all = jnp.transpose(
        jnp.concatenate([near, swap_core(near)], axis=0).reshape(8, 2, 128, D), (1, 0, 2, 3)
    ).reshape(2048, D)
    rest = to_owners(jnp.concatenate([w_g, w_u, w_d], axis=2))
    rest = lax.all_to_all(rest, GROUP, 0, 0, tiled=True)
    rest_sent = jnp.broadcast_to(rest[None], (16, 64, 3 * FW)).reshape(1024, 3 * FW)
    table = slot_places(positions)[::BLK] // BLK
    cosine, sine = turn_tables(table)

    w_qkv = w_first[:, : 2 * QW]
    w_out = w_first[:, 2 * QW : 3 * QW]
    gain_all = w_first[:, 3 * QW :].reshape(128, 8, 128)[:, 0, :18].reshape(2304).astype(f32)
    gain_attn = gain_all[:D]
    gain_mlp = gain_all[D : 2 * D]
    head_gains = gain_all[2 * D :].reshape(2, HEAD_SIZE)
    plain, query, query_raw, pair, key_raw = project(
        tokens_all, gain_attn[None], w_first[:, :QW], w_first[:, QW : 2 * QW],
        head_gains, cosine, sine, rest_sent,
    )
    w_rest = lax.all_to_all(rest_sent, PLANE, 0, 0, tiled=True)
    w_gateup = w_rest[:, : 2 * FW]
    w_down = w_rest[:, 2 * FW :]
    backs_low = group_gather(cotangent[0])
    attended, logsum = attend(table, query, pair, backs_low)

    middle = own + group_scatter(attended, w_out, contract_cols)
    scale_two = rms_scale(middle)
    normed_two = near_gather((middle * scale_two * gain_mlp).astype(bf16))
    normed_two = after(normed_two, w_rest)
    normed_all, hidden, grad_gu, low, total = mlp(
        normed_two, swap_core(normed_two), backs_low, w_gateup, w_down
    )
    grad_normed_two = group_fold(total, low)
    term_mlp = jnp.concatenate(
        [dot(normed_all, grad_gu, contract_rows), dot(backs_low, hidden, contract_rows)], axis=1
    )
    plane_mlp = plane_sum(term_mlp)

    grad_mid_part, gain_mlp_grad = norm_back(middle, scale_two, gain_mlp, grad_normed_two)
    grad_mid = own_back + grad_mid_part
    mid_near = near_gather(grad_mid.astype(bf16))
    last, grad_q_low, grad_pair, grad_pair_away = attend_back(
        table, query, pair, attended, logsum, query_raw, key_raw, cosine, sine, head_gains,
        gain_mlp_grad.reshape(8, HEAD_SIZE), plain, mid_near, swap_core(mid_near), w_out, plane_mlp,
    )
    got = lax.all_to_all(last, ALL, 0, 0, tiled=True)
    share_mlp = lax.all_to_all(after(plane_mlp, last), GROUP, 0, 0, tiled=True)
    own_gain = lax.dynamic_slice_in_dim(gain_attn, rank * 8, 8)
    grad_share, stats = collect(got, share_mlp, weights, own_gain[:, None])
    shared = lax.all_to_all(
        jnp.broadcast_to(stats, (128, 2 * HEAD_SIZE)), ALL, 0, 0, tiled=True
    )

    output = middle + group_scatter(hidden, w_down, contract_cols)
    grad_pair_sum = grad_pair + swap_yhi(grad_pair_away).astype(f32)
    grad_key = grad_pair_sum[:, :KW]
    grad_key = grad_key * cosine[:1024] - jnp.roll(grad_key, HEAD_SIZE // 2, axis=1) * sine[:1024]
    key_near = key_raw[:1024]
    grad_key_raw, _ = norm_back(key_near, rms_scale(key_near), head_gains[1], grad_key)
    grad_proj = jnp.concatenate(
        [grad_q_low, grad_key_raw.astype(bf16), grad_pair_sum[:, KW:].astype(bf16)], axis=1
    )
    grad_normed = group_scatter(grad_proj, w_qkv, contract_cols)
    grad_in_part, _ = norm_back(own, rms_scale(own), gain_attn, grad_normed)
    grad_inputs = grad_mid + grad_in_part

    norm_all = jnp.sqrt(jnp.sum(shared[:, HEAD_SIZE + 8]))
    gain_whole = jnp.concatenate(
        [shared[:, HEAD_SIZE : HEAD_SIZE + 8].reshape(D), shared[:10, :HEAD_SIZE].reshape(1280)]
    )
    gain_grad = lax.dynamic_slice_in_dim(gain_whole, rank * 18, 18)
    factor = jnp.minimum(1.0, clip_limit / (norm_all + 1e-06))
    column = jnp.arange(grad_share.shape[1])
    rates = jnp.where(
        (column >= QKVC) & (column < QKVC + QUERY_HEADS * HEAD_SIZE), rate_output, rate_matrix
    )
    new_w, new_mw, new_vw = adam(
        weights.astype(f32),
        grad_share * factor,
        moment_weights,
        second_weights,
        rates[None, :],
        decay_rate,
    )
    new_g, new_mg, new_vg = adam(
        norm_gains.astype(f32),
        gain_grad * factor,
        moment_gains,
        second_gains,
        rate_gain,
        0.0,
    )
    return (
        output[None],
        grad_inputs[None],
        norm_all.reshape(1),
        new_w,
        new_mw,
        new_vw,
        new_g,
        new_mg,
        new_vg,
    )


def solution(mesh):
    parts = Mesh(mesh.devices.reshape(2, 4, 2, 4, 2), ALL)
    rows = P(("ylo", "z"), ("yhi", "x", "core"), None)
    owned = P(ALL, None)
    small = P(ALL)
    return jax.shard_map(
        body,
        mesh=parts,
        in_specs=(rows, rows, P(), owned, small, owned, owned, small, small),
        out_specs=(rows, rows, P(), owned, owned, owned, small, small, small),
        check_vma=False,
    )
```

```python
import functools
import math

import jax
import jax.numpy as jnp
from jax import lax
from jax.experimental import pallas as pl
from jax.experimental.pallas import tpu as pltpu
from jax.sharding import Mesh
from jax.sharding import PartitionSpec as P

D = 1024
FF = 3072
QUERY_HEADS = 16
KEY_VALUE_HEADS = 8
HEAD_SIZE = 128
ADAM_STEP = 10
QKVC = 4096
TP = 8
QW = 256
KW = 128
FW = FF // TP
BLK = 64
TILE = 256

ALL = ("ylo", "z", "yhi", "x", "core")
PLANE = ("ylo", "z", "yhi")

eps_norm = 1e-06
rope_base = 1000000.0
clip_limit = 1.0
beta_one = 0.9
beta_two = 0.95
adam_eps = 1e-08
decay_rate = 0.1
rate_matrix = 0.06
rate_output = 2.0
rate_gain = 1.0
contract_rows = (((0,), (0,)), ((), ()))
contract_cols = (((1,), (1,)), ((), ()))
f32 = jnp.float32
bf16 = jnp.bfloat16


def dot(a, b, dims=(((1,), (0,)), ((), ()))):
    return lax.dot_general(a, b, dims, preferred_element_type=f32)


def rms_scale(value_rows):
    return lax.rsqrt(jnp.mean(value_rows * value_rows, axis=-1, keepdims=True) + eps_norm)


def norm_back(value_rows, scale, gain, grad_out):
    gain_grad = jnp.sum(grad_out * value_rows * scale, axis=tuple(range(value_rows.ndim - 1)))
    weighted = grad_out * gain
    grad_in = scale * weighted - value_rows * scale * scale * scale * jnp.mean(
        weighted * value_rows, axis=-1, keepdims=True
    )
    return (grad_in, gain_grad)


def turn_tables(blocks):
    half = HEAD_SIZE // 2
    inverse = jnp.exp(jnp.arange(half, dtype=f32) * (-2.0 / HEAD_SIZE) * math.log(rope_base))
    inverse = jnp.concatenate([inverse, inverse])
    coarse = (blocks * BLK).astype(f32)[:, None] * inverse[None, :]
    fine = jnp.arange(BLK, dtype=f32)[:, None] * inverse[None, :]
    sign = jnp.where(jnp.arange(HEAD_SIZE) < half, -1.0, 1.0)
    cos_a, sin_a, cos_b, sin_b = lax.optimization_barrier(
        (jnp.cos(coarse), jnp.sin(coarse), jnp.cos(fine), jnp.sin(fine))
    )
    cos_a, sin_a = cos_a[:, None, :], sin_a[:, None, :]
    cosine = cos_a * cos_b - sin_a * sin_b
    sine = (sin_a * cos_b + cos_a * sin_b) * sign
    return (cosine.reshape(-1, HEAD_SIZE), sine.reshape(-1, HEAD_SIZE))


def swap_core(v):
    return lax.ppermute(v, "core", [(0, 1), (1, 0)])


def swap_yhi(v):
    return lax.ppermute(v, "yhi", [(0, 1), (1, 0)])


def shift_x(v, k):
    return lax.ppermute(v, "x", [(i, (i + k) % 4) for i in range(4)])


def y_index(p):
    return (p % 2) * 2 + p // 2


def shift_y(v, k):
    return lax.ppermute(v, ("ylo", "yhi"), [(y_index(i), y_index((i + k) % 4)) for i in range(4)])


def shift_z(v, k):
    return lax.ppermute(v, "z", [(i, (i + k) % 4) for i in range(4)])


def idle_kernel(*refs):
    pass


def after(v, *waits):
    return pl.pallas_call(
        idle_kernel,
        out_shape=jax.ShapeDtypeStruct(v.shape, v.dtype),
        in_specs=[pl.BlockSpec(memory_space=pl.ANY)] * (1 + len(waits)),
        out_specs=pl.BlockSpec(memory_space=pl.ANY),
        input_output_aliases={0: 0},
        cost_estimate=pl.CostEstimate(flops=0, bytes_accessed=0, transcendentals=0),
        name="after",
    )(v, *waits)


def turned(v, start):
    return lax.dynamic_slice_in_dim(jnp.concatenate([v, v], axis=0), start, 4, axis=0)


def group_exchange(v):
    xi, core = lax.axis_index("x"), lax.axis_index("core")
    n = v.shape[2]
    v = turned(v.reshape(4, 2, 8, n), xi)
    kept = jnp.where(core == 0, v[:, 0], v[:, 1])
    got = swap_core(jnp.where(core == 0, v[:, 1], v[:, 0]))
    v = jnp.stack([kept, got], axis=1)
    v = jnp.stack([v[0], shift_x(v[3], 3), shift_x(v[2], 2), shift_x(v[1], 1)])
    v = jnp.where(core == 0, v, v[:, ::-1])
    return turned(v, lax.rem(4 - xi, 4)).reshape(8, 8, n)


def near_gather(v):
    return jnp.concatenate([v] + [shift_x(v, -k) for k in (1, 2, 3)], axis=0)


def group_gather(v):
    near = near_gather(v)
    return jnp.concatenate([near, swap_core(near)], axis=0)


def group_scatter(left, right, dims):
    half = left.shape[0] // 2
    away = dot(left[half:], right, dims).astype(bf16)
    return group_fold(dot(left[:half], right, dims), away)


def core_fold(near, away):
    near = near + swap_core(away).astype(f32)
    return near[:128], near.astype(bf16)


def x_fold(total, low):
    for k in (1, 2, 3):
        total = total + shift_x(low[k * 128 : (k + 1) * 128], k).astype(f32)
    return total


def group_fold(near, away):
    return x_fold(*core_fold(near, away))


def adam(weight, grad, moment, second, rate, decay):
    moment_new = beta_one * moment + (1.0 - beta_one) * grad
    second_new = beta_two * second + (1.0 - beta_two) * grad * grad
    scaled_m = moment_new / (1.0 - beta_one**ADAM_STEP)
    scaled_v = second_new / (1.0 - beta_two**ADAM_STEP)
    weight_new = weight * (1.0 - rate * decay) - rate * scaled_m / (jnp.sqrt(scaled_v) + adam_eps)
    return (weight_new, moment_new, second_new)


def sort_blocks(table, pair, keys, values):
    for i in range(32):
        spot = pl.ds(pl.multiple_of(table[i] * BLK, BLK), BLK)
        keys[spot, :] = pair[i * BLK : (i + 1) * BLK, :HEAD_SIZE]
        values[spot, :] = pair[i * BLK : (i + 1) * BLK, HEAD_SIZE:]


def flip(v):
    return jnp.transpose(v.astype(f32)).astype(bf16)


def stack_heads(ref, rows):
    return jnp.concatenate([ref[rows, :HEAD_SIZE], ref[rows, HEAD_SIZE:]], axis=0)


def seen(place, first, count):
    key_place = first + lax.broadcasted_iota(jnp.int32, (count, 2 * BLK), 0)
    lane = lax.broadcasted_iota(jnp.int32, (count, 2 * BLK), 1)
    return key_place <= place * BLK + lax.rem(lane, BLK)


def attend_kernel(table, query, pair, out, logsum, keys, values, values_t):
    scale = HEAD_SIZE ** (-0.5)
    sort_blocks(table, pair, keys, values)
    for t in range(8):
        values_t[:, t * TILE : (t + 1) * TILE] = flip(values[t * TILE : (t + 1) * TILE, :])

    def block(i, carry):
        place = table[i]
        rows = pl.ds(pl.multiple_of(i * BLK, BLK), BLK)

        def run(count):
            full = count - TILE
            stacked = stack_heads(query, rows)
            tail = dot(keys[full:count, :], stacked, contract_cols)
            tail = jnp.where(seen(place, full, TILE), tail, -1e30)
            top = jnp.max(tail, axis=0, keepdims=True)
            if full:
                head = dot(keys[:full, :], stacked, contract_cols)
                top = jnp.maximum(top, jnp.max(head, axis=0, keepdims=True))
            tail = jnp.exp((tail - top) * scale)
            total = jnp.sum(tail, axis=0, keepdims=True)
            mixed = dot(values_t[:, full:count], tail.astype(bf16))
            if full:
                head = jnp.exp((head - top) * scale)
                total = total + jnp.sum(head, axis=0, keepdims=True)
                mixed = mixed + dot(values_t[:, :full], head.astype(bf16))
            mixed = jnp.transpose(mixed / total).astype(bf16)
            out[rows, :HEAD_SIZE] = mixed[:BLK]
            out[rows, HEAD_SIZE:] = mixed[BLK:]
            logsum[pl.ds(i, 1), :] = top * scale + jnp.log(total)

        for step in range(8):
            pl.when(lax.div(place, 4) == step)(functools.partial(run, (step + 1) * TILE))
        return carry

    lax.fori_loop(0, 16, block, 0)


def turn(v):
    return jnp.concatenate([v[:, HEAD_SIZE // 2 :], v[:, : HEAD_SIZE // 2]], axis=1)


def head_back(raw, grad, gain, cosine, sine):
    grad = grad * cosine - turn(grad) * sine
    scale = lax.rsqrt(jnp.mean(raw * raw, axis=-1, keepdims=True) + eps_norm)
    gain_grad = jnp.sum(grad * raw * scale, axis=0, keepdims=True)
    weighted = grad * gain
    mean = jnp.mean(weighted * raw, axis=-1, keepdims=True)
    return (scale * weighted - raw * (scale * scale * scale * mean), gain_grad)


def attend_back_kernel(
    table, query, pair, out, logsum,
    query_raw, key_raw, cosine, sine, gains, gain_mlp, plain, mid_near, mid_far,
    weight_out, idle, last, grad_query, grad_own, grad_away,
    keys, values, keys_t, acc_key, acc_value, pair_near, pair_far, query_acc, grad,
):
    scale = HEAD_SIZE ** (-0.5)
    grad[:512, :] = dot(mid_near[...], weight_out[...]).astype(bf16)
    grad[512:, :] = dot(mid_far[...], weight_out[...]).astype(bf16)
    sort_blocks(table, pair, keys, values)
    acc_key[...] = jnp.zeros_like(acc_key)
    acc_value[...] = jnp.zeros_like(acc_value)
    for t in range(8):
        keys_t[:, t * TILE : (t + 1) * TILE] = flip(keys[t * TILE : (t + 1) * TILE, :])

    def block(i, carry):
        place = table[i]
        rows = pl.ds(pl.multiple_of(i * BLK, BLK), BLK)

        def run(count):
            stacked = stack_heads(query, rows)
            back = stack_heads(grad, rows)
            made = stack_heads(out, rows)
            inner = jnp.sum(
                jnp.transpose(back.astype(f32) * made.astype(f32)), axis=0, keepdims=True
            )
            level = logsum[pl.ds(i, 1), :]
            total = jnp.zeros((HEAD_SIZE, 2 * BLK), f32)
            for first in range(0, count, TILE):
                span = slice(first, first + TILE)
                probs = jnp.exp(dot(keys[span, :], stacked, contract_cols) * scale - level)
                if first + TILE == count:
                    probs = jnp.where(seen(place, first, TILE), probs, 0.0)
                grad_p = dot(values[span, :], back, contract_cols)
                grad_s = (probs * (grad_p - inner)).astype(bf16)
                acc_key[span, :] += dot(grad_s, stacked)
                acc_value[span, :] += dot(probs.astype(bf16), back)
                total = total + dot(keys_t[:, span], grad_s)
            total = jnp.transpose(total) * scale
            query_acc[rows, :HEAD_SIZE] = total[:BLK]
            query_acc[rows, HEAD_SIZE:] = total[BLK:]

        for step in range(8):
            pl.when(lax.div(place, 4) == step)(functools.partial(run, (step + 1) * TILE))
        return carry

    lax.fori_loop(0, 16, block, 0)
    for i in range(16):
        rows = slice(i * BLK, (i + 1) * BLK)
        near = pl.ds(pl.multiple_of(table[i] * BLK, BLK), BLK)
        pair_near[rows, :HEAD_SIZE] = acc_key[near, :] * scale
        pair_near[rows, HEAD_SIZE:] = acc_value[near, :]
        far = pl.ds(pl.multiple_of(table[16 + i] * BLK, BLK), BLK)
        pair_far[rows, :HEAD_SIZE] = acc_key[far, :] * scale
        pair_far[rows, HEAD_SIZE:] = acc_value[far, :]

    gain_q = gains[0:1, :]
    gain_k = gains[1:2, :]
    sum_q = jnp.zeros((1, HEAD_SIZE), f32)
    sum_k = jnp.zeros((1, HEAD_SIZE), f32)
    for t in range(4):
        rows = slice(t * TILE, (t + 1) * TILE)
        rows_far = slice(1024 + t * TILE, 1024 + (t + 1) * TILE)
        for h in range(2):
            cols = slice(h * HEAD_SIZE, (h + 1) * HEAD_SIZE)
            made, part = head_back(
                query_raw[rows, cols], query_acc[rows, cols], gain_q, cosine[rows, :], sine[rows, :]
            )
            grad_query[rows, cols] = made.astype(bf16)
            sum_q = sum_q + part
        made, part = head_back(
            key_raw[rows, :], pair_near[rows, :HEAD_SIZE], gain_k, cosine[rows, :], sine[rows, :]
        )
        pair_near[rows, :HEAD_SIZE] = made
        sum_k = sum_k + part
        made, part = head_back(
            key_raw[rows_far, :], pair_far[rows, :HEAD_SIZE], gain_k,
            cosine[rows_far, :], sine[rows_far, :],
        )
        pair_far[rows, :HEAD_SIZE] = made
        sum_k = sum_k + part
    grad_own[...] = pair_near[...]
    grad_away[...] = pair_far[...].astype(bf16)

    def down(ref):
        return jnp.transpose(ref[...].astype(f32)).astype(bf16)

    query_t = down(grad_query)
    near_t = down(pair_near)
    far_t = down(pair_far)
    out_t = down(out)
    for t in range(4):
        rows = slice(t * TILE, (t + 1) * TILE)
        made = dot(query_t, plain[:1024, rows])
        last[rows, :QW] = jnp.transpose(made).astype(bf16)
        made = dot(near_t, plain[:1024, rows]) + dot(far_t, plain[1024:, rows])
        last[rows, QW : 2 * QW] = jnp.transpose(made).astype(bf16)
        made = dot(out_t[:, :512], mid_near[:, rows]) + dot(out_t[:, 512:], mid_far[:, rows])
        last[rows, 2 * QW : 3 * QW] = jnp.transpose(made).astype(bf16)
    last[:, 3 * QW :] = jnp.zeros((1024, 128), bf16)
    lines = [gain_mlp[k : k + 1, :] for k in range(8)] + [sum_q, sum_k]
    row = lax.broadcasted_iota(jnp.int32, (16, HEAD_SIZE), 0)
    for k in range(5):
        made = jnp.zeros((16, HEAD_SIZE), f32)
        for at, line in ((0, lines[2 * k]), (8, lines[2 * k + 1])):
            high = line.astype(bf16).astype(f32)
            made = jnp.where(row == at, high, made)
            made = jnp.where(row == at + 1, line - high, made)
        last[16 * k : 16 * k + 16, 3 * QW :] = made.astype(bf16)


def in_vmem():
    return pl.BlockSpec(memory_space=pltpu.VMEM)


def in_smem():
    return pl.BlockSpec(memory_space=pltpu.SMEM)


def project_kernel(
    near, far, weight_q, weight_kv, gain_cols, pick, cosine, sine,
    plain, query, query_raw, pair, key_raw, gains,
):
    step = pl.program_id(0)

    @pl.when(step == 0)
    def _():
        gains[...] = dot(pick[...], gain_cols[...])

    is_near = lax.rem(lax.div(step, 2), 2) == 0
    rows = jnp.where(is_near, near[...].reshape(TILE, D), far[...].reshape(TILE, D)).astype(f32)
    scaled = rows * lax.rsqrt(jnp.mean(rows * rows, axis=-1, keepdims=True) + eps_norm)
    plain[...] = scaled.astype(bf16)
    gain = jnp.concatenate([gains[k : k + 1, :] for k in range(8)], axis=1)
    normed = (scaled * gain).astype(bf16)

    def head(raw, head_gain):
        scale = lax.rsqrt(jnp.mean(raw * raw, axis=-1, keepdims=True) + eps_norm)
        made = raw * scale * head_gain
        return (made * cosine[...] + turn(made) * sine[...]).astype(bf16)

    made = dot(normed, weight_kv[...])
    key_raw[...] = made[:, :KW]
    pair[:, :KW] = head(made[:, :KW], gains[17:18, :])
    pair[:, KW:] = made[:, KW:].astype(bf16)

    @pl.when(step < 4)
    def _():
        made = dot(normed, weight_q[...])
        query_raw[...] = made
        for h in range(2):
            cols = slice(h * HEAD_SIZE, (h + 1) * HEAD_SIZE)
            query[:, cols] = head(made[:, cols], gains[16:17, :])


def gain_picker():
    row = jnp.arange(1024)
    line = (row // 8 * 18) // 128 + row % 8
    return ((jnp.arange(24)[:, None] == line[None, :]) & (row % 8 < 2)[None, :]).astype(bf16)


def tiles(width):
    return pl.BlockSpec((TILE, width), lambda t: (t, 0))


def columns(width, at):
    return pl.BlockSpec((1024, width), lambda t: (0, at))


def early_tiles(width):
    return pl.BlockSpec((TILE, width), lambda t: (jnp.minimum(t, 1), 0))


def late_tiles(width):
    return pl.BlockSpec((TILE, width), lambda t: (jnp.maximum(t - 2, 0), 0))


def project(near, far, w_first, cosine, sine):
    def first(width):
        return pl.BlockSpec((TILE, width), lambda t: (jnp.minimum(t, 3), 0))

    def near_at(t):
        core = lax.rem(lax.div(t, 2), 2)
        return (jnp.where(core == 0, lax.rem(t, 2), 1), lax.div(t, 4), 0, 0)

    def far_at(t):
        core = lax.rem(lax.div(t, 2), 2)
        return (jnp.where(core == 0, 0, lax.rem(t, 2)), lax.div(t, 4), 0, 0)

    return pl.pallas_call(
        project_kernel,
        grid=(8,),
        out_shape=[
            jax.ShapeDtypeStruct((2048, D), bf16),
            jax.ShapeDtypeStruct((1024, QW), bf16),
            jax.ShapeDtypeStruct((1024, QW), f32),
            jax.ShapeDtypeStruct((2048, QW), bf16),
            jax.ShapeDtypeStruct((2048, KW), f32),
            jax.ShapeDtypeStruct((24, HEAD_SIZE), f32),
        ],
        in_specs=[
            pl.BlockSpec((2, 1, 128, D), near_at),
            pl.BlockSpec((2, 1, 128, D), far_at),
            columns(QW, 0),
            columns(QW, 1),
            columns(128, 6),
            pl.BlockSpec((24, 1024), lambda t: (0, 0)),
            tiles(HEAD_SIZE),
            tiles(HEAD_SIZE),
        ],
        out_specs=[
            tiles(D), first(QW), first(QW), tiles(QW), tiles(KW),
            pl.BlockSpec((24, HEAD_SIZE), lambda t: (0, 0)),
        ],
        compiler_params=pltpu.CompilerParams(vmem_limit_bytes=32 * 2**20),
        cost_estimate=pl.CostEstimate(
            flops=8000000000, bytes_accessed=20000000, transcendentals=0
        ),
        name="project",
    )(near, far, w_first, w_first, w_first, gain_picker(), cosine, sine)


def mlp_kernel(
    near, far, backs_near, backs_far, weight, down, normed, backs, hidden, grad_gu, low, total, low_out, total_out
):
    step = pl.program_id(0)
    rows = jnp.where(step < 2, far[...], near[...])
    normed[...] = rows
    made = dot(rows, weight[...])
    gate = made[:, :FW]
    upper = made[:, FW:]
    sigma = jax.nn.sigmoid(gate)
    acted = gate * sigma
    hidden[...] = (acted * upper).astype(bf16)
    back = jnp.where(step < 2, backs_far[...], backs_near[...])
    backs[...] = back
    grad = dot(back, down[...])
    grad_gu[:, :FW] = (grad * upper * sigma * (1.0 + gate * (1.0 - sigma))).astype(bf16)
    grad_gu[:, FW:] = (grad * acted).astype(bf16)
    part = dot(grad_gu[...], weight[...], contract_cols)
    part_out = dot(hidden[...], down[...], contract_cols)

    @pl.when(step < 2)
    def _():
        low[...] = part.astype(bf16)
        low_out[...] = part_out.astype(bf16)

    @pl.when(step >= 2)
    def _():
        total[...] = part
        total_out[...] = part_out


def mlp(near, far, backs_near, backs_far, w_rest):
    def rows(width):
        return pl.BlockSpec((TILE, width), lambda t: (lax.rem(t + 2, 4), 0))

    return pl.pallas_call(
        mlp_kernel,
        grid=(4,),
        out_shape=[
            jax.ShapeDtypeStruct((1024, D), bf16),
            jax.ShapeDtypeStruct((1024, D), bf16),
            jax.ShapeDtypeStruct((1024, FW), bf16),
            jax.ShapeDtypeStruct((1024, 2 * FW), bf16),
            jax.ShapeDtypeStruct((512, D), bf16),
            jax.ShapeDtypeStruct((512, D), f32),
            jax.ShapeDtypeStruct((512, D), bf16),
            jax.ShapeDtypeStruct((512, D), f32),
        ],
        in_specs=[
            late_tiles(D),
            early_tiles(D),
            late_tiles(D),
            early_tiles(D),
            columns(2 * FW, 0),
            columns(FW, 2),
        ],
        out_specs=[
            rows(D), rows(D), rows(FW), rows(2 * FW),
            early_tiles(D), late_tiles(D), early_tiles(D), late_tiles(D),
        ],
        compiler_params=pltpu.CompilerParams(vmem_limit_bytes=40 * 2**20),
        cost_estimate=pl.CostEstimate(flops=1000000, bytes_accessed=100000, transcendentals=0),
        name="mlp",
    )(near, far, backs_near, backs_far, w_rest, w_rest)


def attend(table, query, pair):
    return pl.pallas_call(
        attend_kernel,
        out_shape=[
            jax.ShapeDtypeStruct((1024, QW), bf16),
            jax.ShapeDtypeStruct((16, 2 * BLK), f32),
        ],
        in_specs=[in_smem()]
        + [in_vmem()] * 2,
        out_specs=[in_vmem()] * 2,
        scratch_shapes=[
            pltpu.VMEM((2048, HEAD_SIZE), bf16),
            pltpu.VMEM((2048, HEAD_SIZE), bf16),
            pltpu.VMEM((HEAD_SIZE, 2048), bf16),
        ],
        compiler_params=pltpu.CompilerParams(vmem_limit_bytes=48 * 2**20),
        cost_estimate=pl.CostEstimate(flops=12000000000, bytes_accessed=20000000, transcendentals=0),
        name="attend",
    )(table, query, pair)


def attend_back(*args):
    return pl.pallas_call(
        attend_back_kernel,
        out_shape=[
            jax.ShapeDtypeStruct((1024, 3 * QW + 128), bf16),
            jax.ShapeDtypeStruct((1024, QW), bf16),
            jax.ShapeDtypeStruct((1024, QW), f32),
            jax.ShapeDtypeStruct((1024, QW), bf16),
        ],
        in_specs=[in_smem()]
        + [in_vmem()] * (len(args) - 2)
        + [pl.BlockSpec(memory_space=pl.ANY)],
        out_specs=[in_vmem()] * 4,
        scratch_shapes=[
            pltpu.VMEM((2048, HEAD_SIZE), bf16),
            pltpu.VMEM((2048, HEAD_SIZE), bf16),
            pltpu.VMEM((HEAD_SIZE, 2048), bf16),
            pltpu.VMEM((2048, HEAD_SIZE), f32),
            pltpu.VMEM((2048, HEAD_SIZE), f32),
            pltpu.VMEM((1024, QW), f32),
            pltpu.VMEM((1024, QW), f32),
            pltpu.VMEM((1024, QW), f32),
            pltpu.VMEM((1024, QW), bf16),
        ],
        compiler_params=pltpu.CompilerParams(vmem_limit_bytes=48 * 2**20),
        cost_estimate=pl.CostEstimate(
            flops=25000000000, bytes_accessed=30000000, transcendentals=0
        ),
        name="attend_back",
    )(*args)


def collect_kernel(got, mlp, weights, own_gain, idle, share, stats):
    total = got[0:64, :].astype(f32)
    for k in range(1, 16):
        total = total + got[64 * k : 64 * k + 64, :].astype(f32)
    gain_sum = total[0:1, 3 * QW :] + total[1:2, 3 * QW :]
    squares = jnp.zeros((8, HEAD_SIZE), f32)
    for j in range(1, 8):
        gain_sum = gain_sum + total[8 * j : 8 * j + 1, 3 * QW :]
        gain_sum = gain_sum + total[8 * j + 1 : 8 * j + 2, 3 * QW :]
    gain_part = jnp.zeros((8, HEAD_SIZE), f32)
    gain = own_gain[...]
    at_mlp = QKVC + 8 * QW

    def fold(v):
        made = v[:, :HEAD_SIZE]
        for k in range(1, v.shape[1] // HEAD_SIZE):
            made = made + v[:, k * HEAD_SIZE : (k + 1) * HEAD_SIZE]
        return made

    for j in range(8):
        rows = slice(8 * j, 8 * j + 8)
        for at, width, base in ((0, QW, 0), (QW, KW, 2048), (QW + KW, KW, 3072)):
            spot = slice(base + j * width, base + (j + 1) * width)
            plain = total[rows, at : at + width]
            gain_part = gain_part + fold(plain * weights[:, spot].astype(f32))
            made = plain * gain
            share[:, spot] = made
            squares = squares + fold(made * made)
        made = total[rows, 2 * QW : 3 * QW]
        share[:, QKVC + j * QW : QKVC + (j + 1) * QW] = made
        squares = squares + fold(made * made)
        for part in range(3):
            made = mlp[rows, part * FW : (part + 1) * FW]
            first = at_mlp + part * FF + j * FW
            share[:, first : first + FW] = made
            squares = squares + fold(made * made)
    attn = jnp.sum(gain_part, axis=1, keepdims=True)
    whole = jnp.sum(squares) + jnp.sum(gain_sum * gain_sum) + jnp.sum(attn * attn)
    row = lax.broadcasted_iota(jnp.int32, (8, HEAD_SIZE), 0)
    lane = lax.broadcasted_iota(jnp.int32, (8, HEAD_SIZE), 1)
    own_attn = jnp.sum(jnp.where(lane == row, attn, 0.0), axis=0, keepdims=True)
    first = lax.broadcasted_iota(jnp.int32, (1, HEAD_SIZE), 1)
    stats[:, :HEAD_SIZE] = gain_sum
    stats[:, HEAD_SIZE:] = jnp.where(first == 8, whole, own_attn)


def collect(got, mlp, weights, own_gain, idle):
    return pl.pallas_call(
        collect_kernel,
        out_shape=[
            jax.ShapeDtypeStruct((8, 15360), f32),
            jax.ShapeDtypeStruct((1, 2 * HEAD_SIZE), f32),
        ],
        in_specs=[in_vmem()] * 4 + [pl.BlockSpec(memory_space=pl.ANY)],
        out_specs=[in_vmem()] * 2,
        compiler_params=pltpu.CompilerParams(vmem_limit_bytes=32 * 2**20),
        name="collect",
    )(got, mlp, weights, own_gain, idle)


def slot_places(positions):
    seq = lax.axis_index("ylo") * 4 + lax.axis_index("z")
    table = lax.dynamic_index_in_dim(positions, seq, 0, keepdims=False).reshape(2, 4, 2, 128)
    xi = lax.axis_index("x")
    table = lax.dynamic_slice_in_dim(jnp.concatenate([table, table], axis=1), xi, 4, axis=1)
    table = jnp.transpose(table, (0, 2, 1, 3))
    table = jnp.where(lax.axis_index("core") == 0, table, table[:, ::-1])
    table = jnp.where(lax.axis_index("yhi") == 0, table, table[::-1])
    return table.reshape(2048)


def body(
    tokens,
    cotangent,
    positions,
    weights,
    norm_gains,
    moment_weights,
    second_weights,
    moment_gains,
    second_gains,
):
    o_q, o_k, o_v, o_o = 0, 2048, 3072, 4096
    o_g, o_u, o_d = 6144, 6144 + FF, 6144 + 2 * FF
    w_q = weights[:, o_q:o_k].reshape(8, 8, QW)
    w_k = weights[:, o_k:o_v].reshape(8, 8, KW)
    w_v = weights[:, o_v:o_o].reshape(8, 8, KW)
    w_o = weights[:, o_o:o_g].reshape(8, 8, QW)
    w_g = weights[:, o_g:o_u].reshape(8, 8, FW)
    w_u = weights[:, o_u:o_d].reshape(8, 8, FW)
    w_d = weights[:, o_d:].reshape(8, 8, FW)
    rank = lax.axis_index("ylo")
    for name, size in (("z", 4), ("yhi", 2), ("x", 4), ("core", 2)):
        rank = rank * size + lax.axis_index(name)
    own = tokens[0].astype(f32)
    own_back = cotangent[0].astype(f32)

    ready = positions[0, 0] >= 0

    def region(run, *args):
        made = jax.eval_shape(run, *args)

        def never(*args):
            return jax.tree.map(lambda v: jnp.zeros(v.shape, v.dtype), made)

        return lax.cond(ready, run, never, *args)

    gain_row = jnp.concatenate([norm_gains, jnp.zeros(238, bf16)])
    gain_row = jnp.roll(gain_row, lax.rem(rank * 18, 128)).reshape(1, 2, 128)
    w_gains = jnp.broadcast_to(jnp.pad(gain_row, ((0, 0), (0, 6), (0, 0))), (8, 8, 128))
    w_gains = jnp.transpose(w_gains, (1, 0, 2))

    def spread(v):
        n = v.shape[1]
        return jnp.broadcast_to(v[None], (16, 64, n)).reshape(1024, n)

    def pack(tokens, *parts):
        mine = jnp.transpose(jnp.concatenate(parts, axis=2), (1, 0, 2))
        mine = group_exchange(mine).reshape(64, 2048)
        more = jnp.concatenate([tokens, swap_yhi(tokens)], axis=0)
        return more, spread(mine[:, : 3 * QW + 128]), spread(mine[:, 3 * QW + 128 :])

    more, first_sent, rest_sent = region(
        pack, tokens[0], w_q, w_k, w_v, w_o, w_gains, w_g, w_u, w_d
    )
    w_first = lax.all_to_all(first_sent, PLANE, 0, 0, tiled=True)

    def fetch(more, positions):
        near = near_gather(more)
        table = slot_places(positions)[::BLK] // BLK
        far = swap_core(near).reshape(4, 2, 128, D)
        return (near.reshape(4, 2, 128, D), far, table, *turn_tables(table))

    near, far, table, cosine, sine = region(fetch, more, positions)
    w_rest = lax.all_to_all(after(rest_sent, w_first, far), PLANE, 0, 0, tiled=True)

    def mix(near, far, w_first, cosine, sine, table, back, own):
        back_parts = [shift_x(back, -k) for k in (1, 2, 3)]
        plain, query, query_raw, pair, key_raw, gains = project(near, far, w_first, cosine, sine)
        attended, logsum = attend(table, query, pair)
        attended = after(attended, *back_parts)
        back_near = jnp.concatenate([back] + back_parts, axis=0)
        w_out = w_first[:, 2 * QW : 3 * QW]
        middle = own + group_scatter(attended, w_out, contract_cols)
        normed_two = middle * rms_scale(middle) * gains[8:16].reshape(D)
        normed_two = near_gather(normed_two.astype(bf16))
        return (
            plain, query, query_raw, pair, key_raw, gains, attended, logsum,
            back_near, swap_core(back_near), middle, normed_two, swap_core(normed_two),
        )

    (
        plain, query, query_raw, pair, key_raw, gains, attended, logsum,
        back_near, back_far, middle, two_near, two_far,
    ) = region(mix, near, far, w_first, cosine, sine, table, cotangent[0], own)
    w_qkv = w_first[:, : 2 * QW]
    w_out = w_first[:, 2 * QW : 3 * QW]
    gain_attn = gains[:8].reshape(D)
    gain_mlp = gains[8:16].reshape(D)
    head_gains = gains[16:18]
    normed_all, backs_low, hidden, grad_gu, low, total, low_out, total_out = mlp(
        two_near, two_far, back_near, back_far, w_rest
    )

    def weigh(total, low, normed_all, grad_gu, backs_low, hidden):
        term_gu = dot(normed_all, grad_gu, contract_rows)
        term_down = dot(backs_low, hidden, contract_rows)
        term = jnp.concatenate([term_gu, term_down], axis=1).astype(bf16)
        return *core_fold(total, low), term

    total, low, term_mlp = region(weigh, total, low, normed_all, grad_gu, backs_low, hidden)
    got_mlp = lax.all_to_all(term_mlp, PLANE, 0, 0, tiled=True)

    def turn_back(total, low, middle, own_back, gain_mlp, total_out, low_out):
        grad_normed_two = x_fold(total, low)
        grad_mid_part, gain_grad = norm_back(middle, rms_scale(middle), gain_mlp, grad_normed_two)
        grad_mid = own_back + grad_mid_part
        mid_near = near_gather(grad_mid.astype(bf16))
        gain_grad = gain_grad.reshape(8, HEAD_SIZE)
        total_out, low_out = core_fold(total_out, low_out)
        return (
            grad_mid, gain_grad, mid_near, swap_core(mid_near), middle + total_out, low_out
        )

    grad_mid, gain_mlp_grad, mid_near, mid_far, output, out_low = region(
        turn_back, total, low, middle, own_back, gain_mlp, total_out, low_out
    )

    def back(output, out_low, *args):
        made = attend_back(*args)
        for k in (1, 2, 3):
            part = after(shift_x(out_low[k * 128 : k * 128 + 128], k), made[0])
            output = output + part.astype(f32)
        return (output, *made)

    output, last, grad_q_low, grad_pair, grad_pair_away = region(
        back, output, out_low,
        table, query, pair, attended, logsum, query_raw, key_raw,
        cosine, sine, head_gains, gain_mlp_grad, plain, mid_near, mid_far, w_out,
        got_mlp,
    )
    got = lax.all_to_all(last, ALL, 0, 0, tiled=True)

    away = swap_yhi(grad_pair_away)

    def share(got_mlp):
        plane_mlp = jnp.sum(got_mlp.reshape(16, 64, 3 * FW).astype(f32), axis=0)
        return group_exchange(plane_mlp.reshape(8, 8, 3 * FW)).reshape(64, 3 * FW)

    share_mlp = region(share, after(got_mlp, last))

    def finish(grad_q_low, grad_pair, away, w_qkv):
        grad_pair = (grad_pair + away.astype(f32)).astype(bf16)
        grad_proj = jnp.concatenate([grad_q_low, grad_pair], axis=1)
        half = dot(grad_proj[512:], w_qkv, contract_cols).astype(bf16)
        return core_fold(dot(grad_proj[:512], w_qkv, contract_cols), half)

    total, low = region(finish, after(grad_q_low, share_mlp), grad_pair, away, w_qkv)
    own_gain = lax.dynamic_slice_in_dim(gain_attn, rank * 8, 8)
    grad_share, stats = collect(got, share_mlp, weights, own_gain[:, None], low)
    shared = lax.all_to_all(
        jnp.broadcast_to(stats, (128, 2 * HEAD_SIZE)), ALL, 0, 0, tiled=True
    )


    grad_normed = region(x_fold, total, after(low, stats))
    grad_in_part, _ = norm_back(own, rms_scale(own), gain_attn, grad_normed)
    grad_inputs = grad_mid + grad_in_part
    shared = after(shared, grad_normed)

    norm_all = jnp.sqrt(jnp.sum(shared[:, HEAD_SIZE + 8]))
    gain_whole = jnp.concatenate(
        [shared[:, HEAD_SIZE : HEAD_SIZE + 8].reshape(D), shared[:10, :HEAD_SIZE].reshape(1280)]
    )
    gain_grad = lax.dynamic_slice_in_dim(gain_whole, rank * 18, 18)
    factor = jnp.minimum(1.0, clip_limit / (norm_all + 1e-06))
    column = jnp.arange(grad_share.shape[1])
    rates = jnp.where(
        (column >= QKVC) & (column < QKVC + QUERY_HEADS * HEAD_SIZE), rate_output, rate_matrix
    )
    new_w, new_mw, new_vw = adam(
        weights.astype(f32),
        grad_share * factor,
        moment_weights,
        second_weights,
        rates[None, :],
        decay_rate,
    )
    new_g, new_mg, new_vg = adam(
        norm_gains.astype(f32),
        gain_grad * factor,
        moment_gains,
        second_gains,
        rate_gain,
        0.0,
    )
    return (
        output[None],
        grad_inputs[None],
        norm_all.reshape(1),
        new_w,
        new_mw,
        new_vw,
        new_g,
        new_mg,
        new_vg,
    )


def solution(mesh):
    parts = Mesh(mesh.devices.reshape(2, 4, 2, 4, 2), ALL)
    rows = P(("ylo", "z"), ("yhi", "x", "core"), None)
    owned = P(ALL, None)
    small = P(ALL)
    return jax.shard_map(
        body,
        mesh=parts,
        in_specs=(rows, rows, P(), owned, small, owned, owned, small, small),
        out_specs=(rows, rows, P(), owned, owned, owned, small, small, small),
        check_vma=False,
    )
```

```python
import functools
import math

import jax
import jax.numpy as jnp
from jax import lax
from jax.experimental import pallas as pl
from jax.experimental.pallas import tpu as pltpu
from jax.sharding import Mesh
from jax.sharding import PartitionSpec as P

D = 1024
FF = 3072
QUERY_HEADS = 16
KEY_VALUE_HEADS = 8
HEAD_SIZE = 128
ADAM_STEP = 10
QKVC = 4096
TP = 8
QW = 256
KW = 128
FW = FF // TP
BLK = 64
TILE = 256

ALL = ("ylo", "z", "yhi", "x", "core")
PLANE = ("ylo", "z", "yhi")

eps_norm = 1e-06
rope_base = 1000000.0
clip_limit = 1.0
beta_one = 0.9
beta_two = 0.95
adam_eps = 1e-08
decay_rate = 0.1
rate_matrix = 0.06
rate_output = 2.0
rate_gain = 1.0
contract_rows = (((0,), (0,)), ((), ()))
contract_cols = (((1,), (1,)), ((), ()))
f32 = jnp.float32
bf16 = jnp.bfloat16


def dot(a, b, dims=(((1,), (0,)), ((), ()))):
    return lax.dot_general(a, b, dims, preferred_element_type=f32)


def rms_scale(value_rows):
    return lax.rsqrt(jnp.mean(value_rows * value_rows, axis=-1, keepdims=True) + eps_norm)


def norm_back(value_rows, scale, gain, grad_out):
    gain_grad = jnp.sum(grad_out * value_rows * scale, axis=tuple(range(value_rows.ndim - 1)))
    weighted = grad_out * gain
    grad_in = scale * weighted - value_rows * scale * scale * scale * jnp.mean(
        weighted * value_rows, axis=-1, keepdims=True
    )
    return (grad_in, gain_grad)


def turn_tables(blocks):
    half = HEAD_SIZE // 2
    inverse = jnp.exp(jnp.arange(half, dtype=f32) * (-2.0 / HEAD_SIZE) * math.log(rope_base))
    inverse = jnp.concatenate([inverse, inverse])
    coarse = (blocks * BLK).astype(f32)[:, None] * inverse[None, :]
    fine = jnp.arange(BLK, dtype=f32)[:, None] * inverse[None, :]
    sign = jnp.where(jnp.arange(HEAD_SIZE) < half, -1.0, 1.0)
    cos_a, sin_a, cos_b, sin_b = lax.optimization_barrier(
        (jnp.cos(coarse), jnp.sin(coarse), jnp.cos(fine), jnp.sin(fine))
    )
    cos_a, sin_a = cos_a[:, None, :], sin_a[:, None, :]
    cosine = cos_a * cos_b - sin_a * sin_b
    sine = (sin_a * cos_b + cos_a * sin_b) * sign
    return (cosine.reshape(-1, HEAD_SIZE), sine.reshape(-1, HEAD_SIZE))


def swap_core(v):
    return lax.ppermute(v, "core", [(0, 1), (1, 0)])


def swap_yhi(v):
    return lax.ppermute(v, "yhi", [(0, 1), (1, 0)])


def shift_x(v, k):
    return lax.ppermute(v, "x", [(i, (i + k) % 4) for i in range(4)])


def y_index(p):
    return (p % 2) * 2 + p // 2


def shift_y(v, k):
    return lax.ppermute(v, ("ylo", "yhi"), [(y_index(i), y_index((i + k) % 4)) for i in range(4)])


def shift_z(v, k):
    return lax.ppermute(v, "z", [(i, (i + k) % 4) for i in range(4)])


def idle_kernel(*refs):
    pass


def after(v, *waits):
    return pl.pallas_call(
        idle_kernel,
        out_shape=jax.ShapeDtypeStruct(v.shape, v.dtype),
        in_specs=[pl.BlockSpec(memory_space=pl.ANY)] * (1 + len(waits)),
        out_specs=pl.BlockSpec(memory_space=pl.ANY),
        input_output_aliases={0: 0},
        cost_estimate=pl.CostEstimate(flops=0, bytes_accessed=0, transcendentals=0),
        name="after",
    )(v, *waits)


def turned(v, start):
    return lax.dynamic_slice_in_dim(jnp.concatenate([v, v], axis=0), start, 4, axis=0)


def group_exchange(v):
    xi, core = lax.axis_index("x"), lax.axis_index("core")
    n = v.shape[2]
    v = turned(v.reshape(4, 2, 8, n), xi)
    kept = jnp.where(core == 0, v[:, 0], v[:, 1])
    got = swap_core(jnp.where(core == 0, v[:, 1], v[:, 0]))
    v = jnp.stack([kept, got], axis=1)
    v = jnp.stack([v[0], shift_x(v[3], 3), shift_x(v[2], 2), shift_x(v[1], 1)])
    v = jnp.where(core == 0, v, v[:, ::-1])
    return turned(v, lax.rem(4 - xi, 4)).reshape(8, 8, n)


def flip_x(v, mask):
    return lax.ppermute(v, "x", [(i, i ^ mask) for i in range(4)])


def near_gather(v):
    return jnp.concatenate([v] + [flip_x(v, mask) for mask in (1, 3, 2)], axis=0)


def near_gather_halves(v):
    half = v.shape[0] // 2
    a, b = v[:half], v[half:]
    a_one, b_two = flip_x(a, 1), flip_x(b, 3)
    a_rest = flip_x(jnp.concatenate([a, a_one], axis=0), 3)
    b_rest = flip_x(jnp.concatenate([b, b_two], axis=0), 1)
    return jnp.concatenate(
        [v, a_one, b_rest[:half], a_rest[:half], b_two, a_rest[half:], b_rest[half:]], axis=0
    )


def group_gather(v):
    near = near_gather(v)
    return jnp.concatenate([near, swap_core(near)], axis=0)


def group_scatter(left, right, dims):
    half = left.shape[0] // 2
    away = dot(left[half:], right, dims).astype(bf16)
    return group_fold(dot(left[:half], right, dims), away)


def core_fold(near, away):
    near = near + swap_core(away).astype(f32)
    return near[:128], near.astype(bf16)


def x_fold(total, low):
    for k, mask in ((1, 1), (2, 3), (3, 2)):
        total = total + flip_x(low[k * 128 : (k + 1) * 128], mask).astype(f32)
    return total


def group_fold(near, away):
    return x_fold(*core_fold(near, away))


def adam(weight, grad, moment, second, rate, decay):
    moment_new = beta_one * moment + (1.0 - beta_one) * grad
    second_new = beta_two * second + (1.0 - beta_two) * grad * grad
    scaled_m = moment_new / (1.0 - beta_one**ADAM_STEP)
    scaled_v = second_new / (1.0 - beta_two**ADAM_STEP)
    weight_new = weight * (1.0 - rate * decay) - rate * scaled_m / (jnp.sqrt(scaled_v) + adam_eps)
    return (weight_new, moment_new, second_new)


def sort_blocks(table, pair, keys, values):
    for i in range(32):
        spot = pl.ds(pl.multiple_of(table[i] * BLK, BLK), BLK)
        keys[spot, :] = pair[i * BLK : (i + 1) * BLK, :HEAD_SIZE]
        values[spot, :] = pair[i * BLK : (i + 1) * BLK, HEAD_SIZE:]


def flip(v):
    return jnp.transpose(v.astype(f32)).astype(bf16)


def stack_heads(ref, rows):
    return jnp.concatenate([ref[rows, :HEAD_SIZE], ref[rows, HEAD_SIZE:]], axis=0)


def seen(place, first, count):
    key_place = first + lax.broadcasted_iota(jnp.int32, (count, 2 * BLK), 0)
    lane = lax.broadcasted_iota(jnp.int32, (count, 2 * BLK), 1)
    return key_place <= place * BLK + lax.rem(lane, BLK)


def attend_kernel(table, query, pair, out, logsum, keys, values, values_t):
    scale = HEAD_SIZE ** (-0.5)
    sort_blocks(table, pair, keys, values)
    for t in range(8):
        values_t[:, t * TILE : (t + 1) * TILE] = flip(values[t * TILE : (t + 1) * TILE, :])

    def block(i, carry):
        place = table[i]
        rows = pl.ds(pl.multiple_of(i * BLK, BLK), BLK)

        def run(count):
            full = count - TILE
            stacked = stack_heads(query, rows)
            tail = dot(keys[full:count, :], stacked, contract_cols)
            tail = jnp.where(seen(place, full, TILE), tail, -1e30)
            top = jnp.max(tail, axis=0, keepdims=True)
            if full:
                head = dot(keys[:full, :], stacked, contract_cols)
                top = jnp.maximum(top, jnp.max(head, axis=0, keepdims=True))
            tail = jnp.exp((tail - top) * scale)
            total = jnp.sum(tail, axis=0, keepdims=True)
            mixed = dot(values_t[:, full:count], tail.astype(bf16))
            if full:
                head = jnp.exp((head - top) * scale)
                total = total + jnp.sum(head, axis=0, keepdims=True)
                mixed = mixed + dot(values_t[:, :full], head.astype(bf16))
            mixed = jnp.transpose(mixed / total).astype(bf16)
            out[rows, :HEAD_SIZE] = mixed[:BLK]
            out[rows, HEAD_SIZE:] = mixed[BLK:]
            logsum[pl.ds(i, 1), :] = top * scale + jnp.log(total)

        for step in range(8):
            pl.when(lax.div(place, 4) == step)(functools.partial(run, (step + 1) * TILE))
        return carry

    lax.fori_loop(0, 16, block, 0)


def turn(v):
    return jnp.concatenate([v[:, HEAD_SIZE // 2 :], v[:, : HEAD_SIZE // 2]], axis=1)


def head_back(raw, grad, gain, cosine, sine):
    grad = grad * cosine - turn(grad) * sine
    scale = lax.rsqrt(jnp.mean(raw * raw, axis=-1, keepdims=True) + eps_norm)
    gain_grad = jnp.sum(grad * raw * scale, axis=0, keepdims=True)
    weighted = grad * gain
    mean = jnp.mean(weighted * raw, axis=-1, keepdims=True)
    return (scale * weighted - raw * (scale * scale * scale * mean), gain_grad)


def attend_back_kernel(
    table, query, pair, out, logsum,
    query_raw, key_raw, cosine, sine, gains, gain_mlp, plain, mid_near, mid_far,
    weight, idle, last, grad_query, grad_own, grad_away,
    keys, values, keys_t, acc_key, acc_value, pair_near, pair_far, query_acc, grad,
):
    scale = HEAD_SIZE ** (-0.5)
    columns_out = slice(2 * QW, 3 * QW)
    grad[:512, :] = dot(mid_near[...], weight[:, columns_out]).astype(bf16)
    grad[512:, :] = dot(mid_far[...], weight[:, columns_out]).astype(bf16)
    sort_blocks(table, pair, keys, values)
    acc_key[...] = jnp.zeros_like(acc_key)
    acc_value[...] = jnp.zeros_like(acc_value)
    for t in range(8):
        keys_t[:, t * TILE : (t + 1) * TILE] = flip(keys[t * TILE : (t + 1) * TILE, :])

    def block(i, carry):
        place = table[i]
        rows = pl.ds(pl.multiple_of(i * BLK, BLK), BLK)

        def run(count):
            stacked = stack_heads(query, rows)
            back = stack_heads(grad, rows)
            made = stack_heads(out, rows)
            inner = jnp.sum(
                jnp.transpose(back.astype(f32) * made.astype(f32)), axis=0, keepdims=True
            )
            level = logsum[pl.ds(i, 1), :]
            total = jnp.zeros((HEAD_SIZE, 2 * BLK), f32)
            for first in range(0, count, TILE):
                span = slice(first, first + TILE)
                probs = jnp.exp(dot(keys[span, :], stacked, contract_cols) * scale - level)
                if first + TILE == count:
                    probs = jnp.where(seen(place, first, TILE), probs, 0.0)
                grad_p = dot(values[span, :], back, contract_cols)
                grad_s = (probs * (grad_p - inner)).astype(bf16)
                acc_key[span, :] += dot(grad_s, stacked)
                acc_value[span, :] += dot(probs.astype(bf16), back)
                total = total + dot(keys_t[:, span], grad_s)
            total = jnp.transpose(total) * scale
            query_acc[rows, :HEAD_SIZE] = total[:BLK]
            query_acc[rows, HEAD_SIZE:] = total[BLK:]

        for step in range(8):
            pl.when(lax.div(place, 4) == step)(functools.partial(run, (step + 1) * TILE))
        return carry

    lax.fori_loop(0, 16, block, 0)
    for i in range(16):
        rows = slice(i * BLK, (i + 1) * BLK)
        near = pl.ds(pl.multiple_of(table[i] * BLK, BLK), BLK)
        pair_near[rows, :HEAD_SIZE] = acc_key[near, :] * scale
        pair_near[rows, HEAD_SIZE:] = acc_value[near, :]
        far = pl.ds(pl.multiple_of(table[16 + i] * BLK, BLK), BLK)
        pair_far[rows, :HEAD_SIZE] = acc_key[far, :] * scale
        pair_far[rows, HEAD_SIZE:] = acc_value[far, :]

    gain_q = gains[0:1, :]
    gain_k = gains[1:2, :]
    sum_q = jnp.zeros((1, HEAD_SIZE), f32)
    sum_k = jnp.zeros((1, HEAD_SIZE), f32)
    for t in range(4):
        rows = slice(t * TILE, (t + 1) * TILE)
        rows_far = slice(1024 + t * TILE, 1024 + (t + 1) * TILE)
        for h in range(2):
            cols = slice(h * HEAD_SIZE, (h + 1) * HEAD_SIZE)
            made, part = head_back(
                query_raw[rows, cols], query_acc[rows, cols], gain_q, cosine[rows, :], sine[rows, :]
            )
            grad_query[rows, cols] = made.astype(bf16)
            sum_q = sum_q + part
        made, part = head_back(
            key_raw[rows, :], pair_near[rows, :HEAD_SIZE], gain_k, cosine[rows, :], sine[rows, :]
        )
        pair_near[rows, :HEAD_SIZE] = made
        sum_k = sum_k + part
        made, part = head_back(
            key_raw[rows_far, :], pair_far[rows, :HEAD_SIZE], gain_k,
            cosine[rows_far, :], sine[rows_far, :],
        )
        pair_far[rows, :HEAD_SIZE] = made
        sum_k = sum_k + part
    grad_own[...] = pair_near[...]
    grad_away[...] = pair_far[...].astype(bf16)

    def down(ref):
        return jnp.transpose(ref[...].astype(f32)).astype(bf16)

    query_t = down(grad_query)
    near_t = down(pair_near)
    far_t = down(pair_far)
    out_t = down(out)
    for t in range(4):
        rows = slice(t * TILE, (t + 1) * TILE)
        made = dot(query_t, plain[:1024, rows])
        last[rows, :QW] = jnp.transpose(made).astype(bf16)
        made = dot(near_t, plain[:1024, rows]) + dot(far_t, plain[1024:, rows])
        last[rows, QW : 2 * QW] = jnp.transpose(made).astype(bf16)
        made = dot(out_t[:, :512], mid_near[:, rows]) + dot(out_t[:, 512:], mid_far[:, rows])
        last[rows, 2 * QW : 3 * QW] = jnp.transpose(made).astype(bf16)
    last[:, 3 * QW :] = jnp.zeros((1024, 128), bf16)
    lines = [gain_mlp[k : k + 1, :] for k in range(8)] + [sum_q, sum_k]
    row = lax.broadcasted_iota(jnp.int32, (16, HEAD_SIZE), 0)
    for k in range(5):
        made = jnp.zeros((16, HEAD_SIZE), f32)
        for at, line in ((0, lines[2 * k]), (8, lines[2 * k + 1])):
            high = line.astype(bf16).astype(f32)
            made = jnp.where(row == at, high, made)
            made = jnp.where(row == at + 1, line - high, made)
        last[16 * k : 16 * k + 16, 3 * QW :] = made.astype(bf16)


def in_vmem():
    return pl.BlockSpec(memory_space=pltpu.VMEM)


def in_smem():
    return pl.BlockSpec(memory_space=pltpu.SMEM)


def project_kernel(
    near, far, weight_q, weight_kv, gain_cols, pick, cosine, sine,
    plain, query, query_raw, pair, key_raw, gains,
):
    step = pl.program_id(0)

    @pl.when(step == 0)
    def _():
        gains[...] = dot(pick[...], gain_cols[...])

    is_near = lax.rem(lax.div(step, 2), 2) == 0
    rows = jnp.where(is_near, near[...].reshape(TILE, D), far[...].reshape(TILE, D)).astype(f32)
    scaled = rows * lax.rsqrt(jnp.mean(rows * rows, axis=-1, keepdims=True) + eps_norm)
    plain[...] = scaled.astype(bf16)
    gain = jnp.concatenate([gains[k : k + 1, :] for k in range(8)], axis=1)
    normed = (scaled * gain).astype(bf16)

    def head(raw, head_gain):
        scale = lax.rsqrt(jnp.mean(raw * raw, axis=-1, keepdims=True) + eps_norm)
        made = raw * scale * head_gain
        return (made * cosine[...] + turn(made) * sine[...]).astype(bf16)

    made = dot(normed, weight_kv[...])
    key_raw[...] = made[:, :KW]
    pair[:, :KW] = head(made[:, :KW], gains[17:18, :])
    pair[:, KW:] = made[:, KW:].astype(bf16)

    @pl.when(step < 4)
    def _():
        made = dot(normed, weight_q[...])
        query_raw[...] = made
        for h in range(2):
            cols = slice(h * HEAD_SIZE, (h + 1) * HEAD_SIZE)
            query[:, cols] = head(made[:, cols], gains[16:17, :])


def gain_picker():
    row = jnp.arange(1024)
    line = (row // 8 * 18) // 128 + row % 8
    return ((jnp.arange(24)[:, None] == line[None, :]) & (row % 8 < 2)[None, :]).astype(bf16)


def tiles(width):
    return pl.BlockSpec((TILE, width), lambda t: (t, 0))


def columns(width, at):
    return pl.BlockSpec((1024, width), lambda t: (0, at))


def early_tiles(width):
    return pl.BlockSpec((TILE, width), lambda t: (jnp.minimum(t, 1), 0))


def late_tiles(width):
    return pl.BlockSpec((TILE, width), lambda t: (jnp.maximum(t - 2, 0), 0))


def project(near, far, w_first, cosine, sine):
    def first(width):
        return pl.BlockSpec((TILE, width), lambda t: (jnp.minimum(t, 3), 0))

    def near_at(t):
        core = lax.rem(lax.div(t, 2), 2)
        return (jnp.where(core == 0, lax.rem(t, 2), 1), lax.div(t, 4), 0, 0)

    def far_at(t):
        core = lax.rem(lax.div(t, 2), 2)
        return (jnp.where(core == 0, 0, lax.rem(t, 2)), lax.div(t, 4), 0, 0)

    return pl.pallas_call(
        project_kernel,
        grid=(8,),
        out_shape=[
            jax.ShapeDtypeStruct((2048, D), bf16),
            jax.ShapeDtypeStruct((1024, QW), bf16),
            jax.ShapeDtypeStruct((1024, QW), f32),
            jax.ShapeDtypeStruct((2048, QW), bf16),
            jax.ShapeDtypeStruct((2048, KW), f32),
            jax.ShapeDtypeStruct((24, HEAD_SIZE), f32),
        ],
        in_specs=[
            pl.BlockSpec((2, 1, 128, D), near_at),
            pl.BlockSpec((2, 1, 128, D), far_at),
            columns(QW, 0),
            columns(QW, 1),
            columns(128, 6),
            pl.BlockSpec((24, 1024), lambda t: (0, 0)),
            tiles(HEAD_SIZE),
            tiles(HEAD_SIZE),
        ],
        out_specs=[
            tiles(D), first(QW), first(QW), tiles(QW), tiles(KW),
            pl.BlockSpec((24, HEAD_SIZE), lambda t: (0, 0)),
        ],
        compiler_params=pltpu.CompilerParams(vmem_limit_bytes=32 * 2**20),
        cost_estimate=pl.CostEstimate(
            flops=8000000000, bytes_accessed=20000000, transcendentals=0
        ),
        name="project",
    )(near, far, w_first, w_first, w_first, gain_picker(), cosine, sine)


def mlp_kernel(
    near, far, backs_near, backs_far, weight, down, normed, backs, hidden, grad_gu, low, total, low_out, total_out
):
    step = pl.program_id(0)
    rows = jnp.where(step < 2, far[...], near[...])
    normed[...] = rows
    made = dot(rows, weight[...])
    gate = made[:, :FW]
    upper = made[:, FW:]
    sigma = jax.nn.sigmoid(gate)
    acted = gate * sigma
    hidden[...] = (acted * upper).astype(bf16)
    back = jnp.where(step < 2, backs_far[...], backs_near[...])
    backs[...] = back
    grad = dot(back, down[...])
    grad_gu[:, :FW] = (grad * upper * sigma * (1.0 + gate * (1.0 - sigma))).astype(bf16)
    grad_gu[:, FW:] = (grad * acted).astype(bf16)
    part = dot(grad_gu[...], weight[...], contract_cols)
    part_out = dot(hidden[...], down[...], contract_cols)

    @pl.when(step < 2)
    def _():
        low[...] = part.astype(bf16)
        low_out[...] = part_out.astype(bf16)

    @pl.when(step >= 2)
    def _():
        total[...] = part
        total_out[...] = part_out


def mlp(near, far, backs_near, backs_far, w_rest):
    def rows(width):
        return pl.BlockSpec((TILE, width), lambda t: (lax.rem(t + 2, 4), 0))

    return pl.pallas_call(
        mlp_kernel,
        grid=(4,),
        out_shape=[
            jax.ShapeDtypeStruct((1024, D), bf16),
            jax.ShapeDtypeStruct((1024, D), bf16),
            jax.ShapeDtypeStruct((1024, FW), bf16),
            jax.ShapeDtypeStruct((1024, 2 * FW), bf16),
            jax.ShapeDtypeStruct((512, D), bf16),
            jax.ShapeDtypeStruct((512, D), f32),
            jax.ShapeDtypeStruct((512, D), bf16),
            jax.ShapeDtypeStruct((512, D), f32),
        ],
        in_specs=[
            late_tiles(D),
            early_tiles(D),
            late_tiles(D),
            early_tiles(D),
            columns(2 * FW, 0),
            columns(FW, 2),
        ],
        out_specs=[
            rows(D), rows(D), rows(FW), rows(2 * FW),
            early_tiles(D), late_tiles(D), early_tiles(D), late_tiles(D),
        ],
        compiler_params=pltpu.CompilerParams(vmem_limit_bytes=40 * 2**20),
        cost_estimate=pl.CostEstimate(flops=1000000, bytes_accessed=100000, transcendentals=0),
        name="mlp",
    )(near, far, backs_near, backs_far, w_rest, w_rest)


def attend(table, query, pair):
    return pl.pallas_call(
        attend_kernel,
        out_shape=[
            jax.ShapeDtypeStruct((1024, QW), bf16),
            jax.ShapeDtypeStruct((16, 2 * BLK), f32),
        ],
        in_specs=[in_smem()]
        + [in_vmem()] * 2,
        out_specs=[in_vmem()] * 2,
        scratch_shapes=[
            pltpu.VMEM((2048, HEAD_SIZE), bf16),
            pltpu.VMEM((2048, HEAD_SIZE), bf16),
            pltpu.VMEM((HEAD_SIZE, 2048), bf16),
        ],
        compiler_params=pltpu.CompilerParams(vmem_limit_bytes=48 * 2**20),
        cost_estimate=pl.CostEstimate(flops=12000000000, bytes_accessed=20000000, transcendentals=0),
        name="attend",
    )(table, query, pair)


def attend_back(*args):
    return pl.pallas_call(
        attend_back_kernel,
        out_shape=[
            jax.ShapeDtypeStruct((1024, 3 * QW + 128), bf16),
            jax.ShapeDtypeStruct((1024, QW), bf16),
            jax.ShapeDtypeStruct((1024, QW), f32),
            jax.ShapeDtypeStruct((1024, QW), bf16),
        ],
        in_specs=[in_smem()]
        + [in_vmem()] * (len(args) - 2)
        + [pl.BlockSpec(memory_space=pl.ANY)],
        out_specs=[in_vmem()] * 4,
        scratch_shapes=[
            pltpu.VMEM((2048, HEAD_SIZE), bf16),
            pltpu.VMEM((2048, HEAD_SIZE), bf16),
            pltpu.VMEM((HEAD_SIZE, 2048), bf16),
            pltpu.VMEM((2048, HEAD_SIZE), f32),
            pltpu.VMEM((2048, HEAD_SIZE), f32),
            pltpu.VMEM((1024, QW), f32),
            pltpu.VMEM((1024, QW), f32),
            pltpu.VMEM((1024, QW), f32),
            pltpu.VMEM((1024, QW), bf16),
        ],
        compiler_params=pltpu.CompilerParams(vmem_limit_bytes=48 * 2**20),
        cost_estimate=pl.CostEstimate(
            flops=25000000000, bytes_accessed=30000000, transcendentals=0
        ),
        name="attend_back",
    )(*args)


def collect_kernel(got, mlp, weights, own_gain, idle, share, stats):
    total = got[0:64, :].astype(f32)
    for k in range(1, 16):
        total = total + got[64 * k : 64 * k + 64, :].astype(f32)
    gain_sum = total[0:1, 3 * QW :] + total[1:2, 3 * QW :]
    squares = jnp.zeros((8, HEAD_SIZE), f32)
    for j in range(1, 8):
        gain_sum = gain_sum + total[8 * j : 8 * j + 1, 3 * QW :]
        gain_sum = gain_sum + total[8 * j + 1 : 8 * j + 2, 3 * QW :]
    gain_part = jnp.zeros((8, HEAD_SIZE), f32)
    gain = own_gain[...]
    at_mlp = QKVC + 8 * QW

    def fold(v):
        made = v[:, :HEAD_SIZE]
        for k in range(1, v.shape[1] // HEAD_SIZE):
            made = made + v[:, k * HEAD_SIZE : (k + 1) * HEAD_SIZE]
        return made

    for j in range(8):
        rows = slice(8 * j, 8 * j + 8)
        for at, width, base in ((0, QW, 0), (QW, KW, 2048), (QW + KW, KW, 3072)):
            spot = slice(base + j * width, base + (j + 1) * width)
            plain = total[rows, at : at + width]
            gain_part = gain_part + fold(plain * weights[:, spot].astype(f32))
            made = plain * gain
            share[:, spot] = made
            squares = squares + fold(made * made)
        made = total[rows, 2 * QW : 3 * QW]
        share[:, QKVC + j * QW : QKVC + (j + 1) * QW] = made
        squares = squares + fold(made * made)
        for part in range(3):
            made = mlp[rows, part * FW : (part + 1) * FW]
            first = at_mlp + part * FF + j * FW
            share[:, first : first + FW] = made
            squares = squares + fold(made * made)
    attn = jnp.sum(gain_part, axis=1, keepdims=True)
    whole = jnp.sum(squares) + jnp.sum(gain_sum * gain_sum) + jnp.sum(attn * attn)
    row = lax.broadcasted_iota(jnp.int32, (8, HEAD_SIZE), 0)
    lane = lax.broadcasted_iota(jnp.int32, (8, HEAD_SIZE), 1)
    own_attn = jnp.sum(jnp.where(lane == row, attn, 0.0), axis=0, keepdims=True)
    first = lax.broadcasted_iota(jnp.int32, (1, HEAD_SIZE), 1)
    stats[:, :HEAD_SIZE] = jnp.broadcast_to(gain_sum, (128, HEAD_SIZE))
    stats[:, HEAD_SIZE:] = jnp.broadcast_to(
        jnp.where(first == 8, whole, own_attn), (128, HEAD_SIZE)
    )


def collect(got, mlp, weights, own_gain, idle):
    return pl.pallas_call(
        collect_kernel,
        out_shape=[
            jax.ShapeDtypeStruct((8, 15360), f32),
            jax.ShapeDtypeStruct((128, 2 * HEAD_SIZE), f32),
        ],
        in_specs=[in_vmem()] * 4 + [pl.BlockSpec(memory_space=pl.ANY)],
        out_specs=[in_vmem()] * 2,
        compiler_params=pltpu.CompilerParams(vmem_limit_bytes=32 * 2**20),
        name="collect",
    )(got, mlp, weights, own_gain, idle)


def slot_places(positions):
    seq = lax.axis_index("ylo") * 4 + lax.axis_index("z")
    table = lax.dynamic_index_in_dim(positions, seq, 0, keepdims=False).reshape(2, 4, 2, 128)
    xi = lax.axis_index("x")
    table = jnp.stack(
        [
            lax.dynamic_index_in_dim(table, jnp.bitwise_xor(xi, mask), 1, keepdims=False)
            for mask in (0, 1, 3, 2)
        ],
        axis=1,
    )
    table = jnp.transpose(table, (0, 2, 1, 3))
    table = jnp.where(lax.axis_index("core") == 0, table, table[:, ::-1])
    table = jnp.where(lax.axis_index("yhi") == 0, table, table[::-1])
    return table.reshape(2048)


def body(
    tokens,
    cotangent,
    positions,
    weights,
    norm_gains,
    moment_weights,
    second_weights,
    moment_gains,
    second_gains,
):
    o_q, o_k, o_v, o_o = 0, 2048, 3072, 4096
    o_g, o_u, o_d = 6144, 6144 + FF, 6144 + 2 * FF
    w_q = weights[:, o_q:o_k].reshape(8, 8, QW)
    w_k = weights[:, o_k:o_v].reshape(8, 8, KW)
    w_v = weights[:, o_v:o_o].reshape(8, 8, KW)
    w_o = weights[:, o_o:o_g].reshape(8, 8, QW)
    w_g = weights[:, o_g:o_u].reshape(8, 8, FW)
    w_u = weights[:, o_u:o_d].reshape(8, 8, FW)
    w_d = weights[:, o_d:].reshape(8, 8, FW)
    rank = lax.axis_index("ylo")
    for name, size in (("z", 4), ("yhi", 2), ("x", 4), ("core", 2)):
        rank = rank * size + lax.axis_index(name)
    own = tokens[0].astype(f32)
    own_back = cotangent[0].astype(f32)

    ready = positions[0, 0] >= 0

    def region(run, *args):
        made = jax.eval_shape(run, *args)

        def never(*args):
            return jax.tree.map(lambda v: jnp.zeros(v.shape, v.dtype), made)

        return lax.cond(ready, run, never, *args)

    gain_row = jnp.concatenate([norm_gains, jnp.zeros(238, bf16)])
    gain_row = jnp.roll(gain_row, lax.rem(rank * 18, 128)).reshape(1, 2, 128)
    w_gains = jnp.broadcast_to(jnp.pad(gain_row, ((0, 0), (0, 6), (0, 0))), (8, 8, 128))
    w_gains = jnp.transpose(w_gains, (1, 0, 2))

    def spread(v):
        n = v.shape[1]
        return jnp.broadcast_to(v[None], (16, 64, n)).reshape(1024, n)

    def pack(tokens, *parts):
        mine = jnp.transpose(jnp.concatenate(parts, axis=2), (1, 0, 2))
        mine = group_exchange(mine).reshape(64, 2048)
        more = jnp.concatenate([tokens, swap_yhi(tokens)], axis=0)
        return more, spread(mine[:, : 3 * QW + 128]), spread(mine[:, 3 * QW + 128 :])

    more, first_sent, rest_sent = region(
        pack, tokens[0], w_q, w_k, w_v, w_o, w_gains, w_g, w_u, w_d
    )
    w_first = lax.all_to_all(first_sent, PLANE, 0, 0, tiled=True)

    def fetch(more, positions):
        near = near_gather_halves(more)
        table = slot_places(positions)[::BLK] // BLK
        far = swap_core(near).reshape(4, 2, 128, D)
        return (near.reshape(4, 2, 128, D), far, table, *turn_tables(table))

    near, far, table, cosine, sine = region(fetch, more, positions)
    w_rest = lax.all_to_all(after(rest_sent, w_first, far), PLANE, 0, 0, tiled=True)

    def mix(near, far, w_first, cosine, sine, table, back, own):
        back_parts = [flip_x(back, mask) for mask in (1, 3, 2)]
        plain, query, query_raw, pair, key_raw, gains = project(near, far, w_first, cosine, sine)
        attended, logsum = attend(table, query, pair)
        attended = after(attended, *back_parts)
        back_near = jnp.concatenate([back] + back_parts, axis=0)
        w_out = w_first[:, 2 * QW : 3 * QW]
        middle = own + group_scatter(attended, w_out, contract_cols)
        normed_two = middle * rms_scale(middle) * gains[8:16].reshape(D)
        normed_two = near_gather(normed_two.astype(bf16))
        return (
            plain, query, query_raw, pair, key_raw, gains, attended, logsum,
            back_near, swap_core(back_near), middle, normed_two, swap_core(normed_two),
        )

    (
        plain, query, query_raw, pair, key_raw, gains, attended, logsum,
        back_near, back_far, middle, two_near, two_far,
    ) = region(mix, near, far, w_first, cosine, sine, table, cotangent[0], own)
    w_qkv = w_first[:, : 2 * QW]
    gain_attn = gains[:8].reshape(D)
    gain_mlp = gains[8:16].reshape(D)
    head_gains = gains[16:18]
    normed_all, backs_low, hidden, grad_gu, low, total, low_out, total_out = mlp(
        two_near, two_far, back_near, back_far, w_rest
    )

    def weigh(total, low, normed_all, grad_gu, backs_low, hidden):
        term_gu = dot(normed_all, grad_gu, contract_rows)
        term_down = dot(backs_low, hidden, contract_rows)
        term = jnp.concatenate([term_gu, term_down], axis=1).astype(bf16)
        return *core_fold(total, low), term

    total, low, term_mlp = region(weigh, total, low, normed_all, grad_gu, backs_low, hidden)
    got_mlp = lax.all_to_all(term_mlp, PLANE, 0, 0, tiled=True)

    def turn_back(total, low, middle, own_back, gain_mlp, total_out, low_out):
        grad_normed_two = x_fold(total, low)
        grad_mid_part, gain_grad = norm_back(middle, rms_scale(middle), gain_mlp, grad_normed_two)
        grad_mid = own_back + grad_mid_part
        mid_near = near_gather(grad_mid.astype(bf16))
        gain_grad = gain_grad.reshape(8, HEAD_SIZE)
        total_out, low_out = core_fold(total_out, low_out)
        return (
            grad_mid, gain_grad, mid_near, swap_core(mid_near), middle + total_out,
            low_out[128:256], low_out[256:384], low_out[384:],
        )

    grad_mid, gain_mlp_grad, mid_near, mid_far, output, *out_low = region(
        turn_back, total, low, middle, own_back, gain_mlp, total_out, low_out
    )

    def back(low_1, low_2, low_3, *args):
        made = attend_back(*args)
        parts = [after(flip_x(v, m), made[0]) for v, m in ((low_1, 1), (low_2, 3), (low_3, 2))]
        return (*parts, *made)

    part_1, part_2, part_3, last, grad_q_low, grad_pair, grad_pair_away = region(
        back, *out_low,
        table, query, pair, attended, logsum, query_raw, key_raw,
        cosine, sine, head_gains, gain_mlp_grad, plain, mid_near, mid_far, w_first,
        got_mlp,
    )
    got = lax.all_to_all(last, ALL, 0, 0, tiled=True)

    away = swap_yhi(grad_pair_away)

    def share(got_mlp, output, *parts):
        for part in parts:
            output = output + part.astype(f32)
        plane_mlp = jnp.sum(got_mlp.reshape(16, 64, 3 * FW).astype(f32), axis=0)
        return group_exchange(plane_mlp.reshape(8, 8, 3 * FW)).reshape(64, 3 * FW), output

    share_mlp, output = region(share, after(got_mlp, last), output, part_1, part_2, part_3)

    def finish(grad_q_low, grad_pair, away, w_qkv):
        grad_pair = (grad_pair + away.astype(f32)).astype(bf16)
        grad_proj = jnp.concatenate([grad_q_low, grad_pair], axis=1)
        half = dot(grad_proj[512:], w_qkv, contract_cols).astype(bf16)
        return core_fold(dot(grad_proj[:512], w_qkv, contract_cols), half)

    total, low = region(finish, after(grad_q_low, share_mlp), grad_pair, away, w_qkv)
    own_gain = lax.dynamic_slice_in_dim(gain_attn, rank * 8, 8)
    grad_share, stats = collect(got, share_mlp, weights, own_gain[:, None], low)
    shared = lax.all_to_all(stats, ALL, 0, 0, tiled=True)


    grad_normed = region(x_fold, total, after(low, stats))
    grad_in_part, _ = norm_back(own, rms_scale(own), gain_attn, grad_normed)
    grad_inputs = grad_mid + grad_in_part
    shared = after(shared, grad_normed)

    norm_all = jnp.sqrt(jnp.sum(shared[:, HEAD_SIZE + 8]))
    gain_whole = jnp.concatenate(
        [shared[:, HEAD_SIZE : HEAD_SIZE + 8].reshape(D), shared[:10, :HEAD_SIZE].reshape(1280)]
    )
    gain_grad = lax.dynamic_slice_in_dim(gain_whole, rank * 18, 18)
    factor = jnp.minimum(1.0, clip_limit / (norm_all + 1e-06))
    column = jnp.arange(grad_share.shape[1])
    rates = jnp.where(
        (column >= QKVC) & (column < QKVC + QUERY_HEADS * HEAD_SIZE), rate_output, rate_matrix
    )
    new_w, new_mw, new_vw = adam(
        weights.astype(f32),
        grad_share * factor,
        moment_weights,
        second_weights,
        rates[None, :],
        decay_rate,
    )
    new_g, new_mg, new_vg = adam(
        norm_gains.astype(f32),
        gain_grad * factor,
        moment_gains,
        second_gains,
        rate_gain,
        0.0,
    )
    return (
        output[None],
        grad_inputs[None],
        norm_all.reshape(1),
        new_w,
        new_mw,
        new_vw,
        new_g,
        new_mg,
        new_vg,
    )


def solution(mesh):
    parts = Mesh(mesh.devices.reshape(2, 4, 2, 4, 2), ALL)
    rows = P(("ylo", "z"), ("yhi", "x", "core"), None)
    owned = P(ALL, None)
    small = P(ALL)
    return jax.shard_map(
        body,
        mesh=parts,
        in_specs=(rows, rows, P(), owned, small, owned, owned, small, small),
        out_specs=(rows, rows, P(), owned, owned, owned, small, small, small),
        check_vma=False,
    )
```

```python
import functools
import math

import jax
import jax.numpy as jnp
from jax import lax
from jax.experimental import pallas as pl
from jax.experimental.pallas import tpu as pltpu
from jax.sharding import Mesh
from jax.sharding import PartitionSpec as P

D = 1024
FF = 3072
QUERY_HEADS = 16
KEY_VALUE_HEADS = 8
HEAD_SIZE = 128
ADAM_STEP = 10
QKVC = 4096
TP = 8
QW = 256
KW = 128
FW = FF // TP
BLK = 64
TILE = 256

ALL = ("ylo", "z", "yhi", "x", "core")
PLANE = ("ylo", "z", "yhi")

eps_norm = 1e-06
rope_base = 1000000.0
clip_limit = 1.0
beta_one = 0.9
beta_two = 0.95
adam_eps = 1e-08
decay_rate = 0.1
rate_matrix = 0.06
rate_output = 2.0
rate_gain = 1.0
contract_rows = (((0,), (0,)), ((), ()))
contract_cols = (((1,), (1,)), ((), ()))
f32 = jnp.float32
bf16 = jnp.bfloat16


def dot(a, b, dims=(((1,), (0,)), ((), ()))):
    return lax.dot_general(a, b, dims, preferred_element_type=f32)


def rms_scale(value_rows):
    return lax.rsqrt(jnp.mean(value_rows * value_rows, axis=-1, keepdims=True) + eps_norm)


def norm_back(value_rows, scale, gain, grad_out):
    gain_grad = jnp.sum(grad_out * value_rows * scale, axis=tuple(range(value_rows.ndim - 1)))
    weighted = grad_out * gain
    grad_in = scale * weighted - value_rows * scale * scale * scale * jnp.mean(
        weighted * value_rows, axis=-1, keepdims=True
    )
    return (grad_in, gain_grad)


def turn_tables(blocks):
    half = HEAD_SIZE // 2
    inverse = jnp.exp(jnp.arange(half, dtype=f32) * (-2.0 / HEAD_SIZE) * math.log(rope_base))
    inverse = jnp.concatenate([inverse, inverse])
    coarse = (blocks * BLK).astype(f32)[:, None] * inverse[None, :]
    fine = jnp.arange(BLK, dtype=f32)[:, None] * inverse[None, :]
    sign = jnp.where(jnp.arange(HEAD_SIZE) < half, -1.0, 1.0)
    cos_a, sin_a, cos_b, sin_b = lax.optimization_barrier(
        (jnp.cos(coarse), jnp.sin(coarse), jnp.cos(fine), jnp.sin(fine))
    )
    cos_a, sin_a = cos_a[:, None, :], sin_a[:, None, :]
    cosine = cos_a * cos_b - sin_a * sin_b
    sine = (sin_a * cos_b + cos_a * sin_b) * sign
    return (cosine.reshape(-1, HEAD_SIZE), sine.reshape(-1, HEAD_SIZE))


def swap_core(v):
    return lax.ppermute(v, "core", [(0, 1), (1, 0)])


def swap_yhi(v):
    return lax.ppermute(v, "yhi", [(0, 1), (1, 0)])


def shift_x(v, k):
    return lax.ppermute(v, "x", [(i, (i + k) % 4) for i in range(4)])


def y_index(p):
    return (p % 2) * 2 + p // 2


def shift_y(v, k):
    return lax.ppermute(v, ("ylo", "yhi"), [(y_index(i), y_index((i + k) % 4)) for i in range(4)])


def shift_z(v, k):
    return lax.ppermute(v, "z", [(i, (i + k) % 4) for i in range(4)])


def idle_kernel(*refs):
    pass


def after(v, *waits):
    return pl.pallas_call(
        idle_kernel,
        out_shape=jax.ShapeDtypeStruct(v.shape, v.dtype),
        in_specs=[pl.BlockSpec(memory_space=pl.ANY)] * (1 + len(waits)),
        out_specs=pl.BlockSpec(memory_space=pl.ANY),
        input_output_aliases={0: 0},
        cost_estimate=pl.CostEstimate(flops=0, bytes_accessed=0, transcendentals=0),
        name="after",
    )(v, *waits)


def turned(v, start):
    return lax.dynamic_slice_in_dim(jnp.concatenate([v, v], axis=0), start, 4, axis=0)


def group_exchange(v):
    xi, core = lax.axis_index("x"), lax.axis_index("core")
    n = v.shape[2]
    v = turned(v.reshape(4, 2, 8, n), xi)
    kept = jnp.where(core == 0, v[:, 0], v[:, 1])
    got = swap_core(jnp.where(core == 0, v[:, 1], v[:, 0]))
    v = jnp.stack([kept, got], axis=1)
    v = jnp.stack([v[0], shift_x(v[3], 3), shift_x(v[2], 2), shift_x(v[1], 1)])
    v = jnp.where(core == 0, v, v[:, ::-1])
    return turned(v, lax.rem(4 - xi, 4)).reshape(8, 8, n)


def flip_x(v, mask):
    return lax.ppermute(v, "x", [(i, i ^ mask) for i in range(4)])


def near_gather(v):
    return jnp.concatenate([v] + [flip_x(v, mask) for mask in (1, 3, 2)], axis=0)


def near_gather_halves(v):
    half = v.shape[0] // 2
    a, b = v[:half], v[half:]
    a_one, b_two = flip_x(a, 1), flip_x(b, 3)
    a_rest = flip_x(jnp.concatenate([a, a_one], axis=0), 3)
    b_rest = flip_x(jnp.concatenate([b, b_two], axis=0), 1)
    return jnp.concatenate(
        [v, a_one, b_rest[:half], a_rest[:half], b_two, a_rest[half:], b_rest[half:]], axis=0
    )


def group_gather(v):
    near = near_gather(v)
    return jnp.concatenate([near, swap_core(near)], axis=0)


def group_scatter(left, right, dims):
    half = left.shape[0] // 2
    away = dot(left[half:], right, dims).astype(bf16)
    return group_fold(dot(left[:half], right, dims), away)


def core_fold(near, away):
    near = near + swap_core(away).astype(f32)
    return near[:128], near.astype(bf16)


def x_fold(total, low):
    for k, mask in ((1, 1), (2, 3), (3, 2)):
        total = total + flip_x(low[k * 128 : (k + 1) * 128], mask).astype(f32)
    return total


def group_fold(near, away):
    return x_fold(*core_fold(near, away))


def adam(weight, grad, moment, second, rate, decay):
    moment_new = beta_one * moment + (1.0 - beta_one) * grad
    second_new = beta_two * second + (1.0 - beta_two) * grad * grad
    scaled_m = moment_new / (1.0 - beta_one**ADAM_STEP)
    scaled_v = second_new / (1.0 - beta_two**ADAM_STEP)
    weight_new = weight * (1.0 - rate * decay) - rate * scaled_m / (jnp.sqrt(scaled_v) + adam_eps)
    return (weight_new, moment_new, second_new)


def sort_blocks(table, pair, keys, values):
    for i in range(32):
        spot = pl.ds(pl.multiple_of(table[i] * BLK, BLK), BLK)
        keys[spot, :] = pair[i * BLK : (i + 1) * BLK, :HEAD_SIZE]
        values[spot, :] = pair[i * BLK : (i + 1) * BLK, HEAD_SIZE:]


def flip(v):
    return jnp.transpose(v.astype(f32)).astype(bf16)


def stack_heads(ref, rows):
    return jnp.concatenate([ref[rows, :HEAD_SIZE], ref[rows, HEAD_SIZE:]], axis=0)


def seen(place, first, count):
    key_place = first + lax.broadcasted_iota(jnp.int32, (count, 2 * BLK), 0)
    lane = lax.broadcasted_iota(jnp.int32, (count, 2 * BLK), 1)
    return key_place <= place * BLK + lax.rem(lane, BLK)


def attend_kernel(table, query, pair, out, logsum, keys, values, values_t):
    scale = HEAD_SIZE ** (-0.5)
    sort_blocks(table, pair, keys, values)
    for t in range(8):
        values_t[:, t * TILE : (t + 1) * TILE] = flip(values[t * TILE : (t + 1) * TILE, :])

    def block(i, carry):
        place = table[i]
        rows = pl.ds(pl.multiple_of(i * BLK, BLK), BLK)

        def run(count):
            full = count - TILE
            stacked = stack_heads(query, rows)
            tail = dot(keys[full:count, :], stacked, contract_cols)
            tail = jnp.where(seen(place, full, TILE), tail, -1e30)
            top = jnp.max(tail, axis=0, keepdims=True)
            if full:
                head = dot(keys[:full, :], stacked, contract_cols)
                top = jnp.maximum(top, jnp.max(head, axis=0, keepdims=True))
            tail = jnp.exp((tail - top) * scale)
            total = jnp.sum(tail, axis=0, keepdims=True)
            mixed = dot(values_t[:, full:count], tail.astype(bf16))
            if full:
                head = jnp.exp((head - top) * scale)
                total = total + jnp.sum(head, axis=0, keepdims=True)
                mixed = mixed + dot(values_t[:, :full], head.astype(bf16))
            mixed = jnp.transpose(mixed / total).astype(bf16)
            out[rows, :HEAD_SIZE] = mixed[:BLK]
            out[rows, HEAD_SIZE:] = mixed[BLK:]
            logsum[pl.ds(i, 1), :] = top * scale + jnp.log(total)

        for step in range(8):
            pl.when(lax.div(place, 4) == step)(functools.partial(run, (step + 1) * TILE))
        return carry

    lax.fori_loop(0, 16, block, 0)


def turn(v):
    return jnp.concatenate([v[:, HEAD_SIZE // 2 :], v[:, : HEAD_SIZE // 2]], axis=1)


def head_back(raw, grad, gain, cosine, sine):
    grad = grad * cosine - turn(grad) * sine
    scale = lax.rsqrt(jnp.mean(raw * raw, axis=-1, keepdims=True) + eps_norm)
    gain_grad = jnp.sum(grad * raw * scale, axis=0, keepdims=True)
    weighted = grad * gain
    mean = jnp.mean(weighted * raw, axis=-1, keepdims=True)
    return (scale * weighted - raw * (scale * scale * scale * mean), gain_grad)


def attend_back_kernel(
    table, query, pair, out, logsum,
    query_raw, key_raw, cosine, sine, gains, gain_mlp, plain, mid_near, mid_far,
    weight, idle, last, grad_query, grad_own, grad_away,
    keys, values, keys_t, acc_key, acc_value, pair_near, pair_far, query_acc, grad,
):
    scale = HEAD_SIZE ** (-0.5)
    columns_out = slice(2 * QW, 3 * QW)
    grad[:512, :] = dot(mid_near[...], weight[:, columns_out]).astype(bf16)
    grad[512:, :] = dot(mid_far[...], weight[:, columns_out]).astype(bf16)
    sort_blocks(table, pair, keys, values)
    acc_key[...] = jnp.zeros_like(acc_key)
    acc_value[...] = jnp.zeros_like(acc_value)
    for t in range(8):
        keys_t[:, t * TILE : (t + 1) * TILE] = flip(keys[t * TILE : (t + 1) * TILE, :])

    def block(i, carry):
        place = table[i]
        rows = pl.ds(pl.multiple_of(i * BLK, BLK), BLK)

        def run(count):
            stacked = stack_heads(query, rows)
            back = stack_heads(grad, rows)
            made = stack_heads(out, rows)
            inner = jnp.sum(
                jnp.transpose(back.astype(f32) * made.astype(f32)), axis=0, keepdims=True
            )
            level = logsum[pl.ds(i, 1), :]
            total = jnp.zeros((HEAD_SIZE, 2 * BLK), f32)
            for first in range(0, count, TILE):
                span = slice(first, first + TILE)
                probs = jnp.exp(dot(keys[span, :], stacked, contract_cols) * scale - level)
                if first + TILE == count:
                    probs = jnp.where(seen(place, first, TILE), probs, 0.0)
                grad_p = dot(values[span, :], back, contract_cols)
                grad_s = (probs * (grad_p - inner)).astype(bf16)
                acc_key[span, :] += dot(grad_s, stacked)
                acc_value[span, :] += dot(probs.astype(bf16), back)
                total = total + dot(keys_t[:, span], grad_s)
            total = jnp.transpose(total) * scale
            query_acc[rows, :HEAD_SIZE] = total[:BLK]
            query_acc[rows, HEAD_SIZE:] = total[BLK:]

        for step in range(8):
            pl.when(lax.div(place, 4) == step)(functools.partial(run, (step + 1) * TILE))
        return carry

    lax.fori_loop(0, 16, block, 0)
    for i in range(16):
        rows = slice(i * BLK, (i + 1) * BLK)
        near = pl.ds(pl.multiple_of(table[i] * BLK, BLK), BLK)
        pair_near[rows, :HEAD_SIZE] = acc_key[near, :] * scale
        pair_near[rows, HEAD_SIZE:] = acc_value[near, :]
        far = pl.ds(pl.multiple_of(table[16 + i] * BLK, BLK), BLK)
        pair_far[rows, :HEAD_SIZE] = acc_key[far, :] * scale
        pair_far[rows, HEAD_SIZE:] = acc_value[far, :]

    gain_q = gains[0:1, :]
    gain_k = gains[1:2, :]
    sum_q = jnp.zeros((1, HEAD_SIZE), f32)
    sum_k = jnp.zeros((1, HEAD_SIZE), f32)
    for t in range(4):
        rows = slice(t * TILE, (t + 1) * TILE)
        rows_far = slice(1024 + t * TILE, 1024 + (t + 1) * TILE)
        for h in range(2):
            cols = slice(h * HEAD_SIZE, (h + 1) * HEAD_SIZE)
            made, part = head_back(
                query_raw[rows, cols], query_acc[rows, cols], gain_q, cosine[rows, :], sine[rows, :]
            )
            grad_query[rows, cols] = made.astype(bf16)
            sum_q = sum_q + part
        made, part = head_back(
            key_raw[rows, :], pair_near[rows, :HEAD_SIZE], gain_k, cosine[rows, :], sine[rows, :]
        )
        pair_near[rows, :HEAD_SIZE] = made
        sum_k = sum_k + part
        made, part = head_back(
            key_raw[rows_far, :], pair_far[rows, :HEAD_SIZE], gain_k,
            cosine[rows_far, :], sine[rows_far, :],
        )
        pair_far[rows, :HEAD_SIZE] = made
        sum_k = sum_k + part
    grad_own[...] = pair_near[...]
    grad_away[...] = pair_far[...].astype(bf16)

    def down(ref):
        return jnp.transpose(ref[...].astype(f32)).astype(bf16)

    query_t = down(grad_query)
    near_t = down(pair_near)
    far_t = down(pair_far)
    out_t = down(out)
    for t in range(4):
        rows = slice(t * TILE, (t + 1) * TILE)
        made = dot(query_t, plain[:1024, rows])
        last[rows, :QW] = jnp.transpose(made).astype(bf16)
        made = dot(near_t, plain[:1024, rows]) + dot(far_t, plain[1024:, rows])
        last[rows, QW : 2 * QW] = jnp.transpose(made).astype(bf16)
        made = dot(out_t[:, :512], mid_near[:, rows]) + dot(out_t[:, 512:], mid_far[:, rows])
        last[rows, 2 * QW : 3 * QW] = jnp.transpose(made).astype(bf16)
    last[:, 3 * QW :] = jnp.zeros((1024, 128), bf16)
    lines = [gain_mlp[k : k + 1, :] for k in range(8)] + [sum_q, sum_k]
    row = lax.broadcasted_iota(jnp.int32, (16, HEAD_SIZE), 0)
    for k in range(5):
        made = jnp.zeros((16, HEAD_SIZE), f32)
        for at, line in ((0, lines[2 * k]), (8, lines[2 * k + 1])):
            high = line.astype(bf16).astype(f32)
            made = jnp.where(row == at, high, made)
            made = jnp.where(row == at + 1, line - high, made)
        last[16 * k : 16 * k + 16, 3 * QW :] = made.astype(bf16)


def in_vmem():
    return pl.BlockSpec(memory_space=pltpu.VMEM)


def in_smem():
    return pl.BlockSpec(memory_space=pltpu.SMEM)


def project_kernel(
    near, far, weight_q, weight_kv, gain_cols, pick, cosine, sine,
    plain, query, query_raw, pair, key_raw, gains,
):
    step = pl.program_id(0)

    @pl.when(step == 0)
    def _():
        gains[...] = dot(pick[...], gain_cols[...])

    is_near = lax.rem(lax.div(step, 2), 2) == 0
    rows = jnp.where(is_near, near[...].reshape(TILE, D), far[...].reshape(TILE, D)).astype(f32)
    scaled = rows * lax.rsqrt(jnp.mean(rows * rows, axis=-1, keepdims=True) + eps_norm)
    plain[...] = scaled.astype(bf16)
    gain = jnp.concatenate([gains[k : k + 1, :] for k in range(8)], axis=1)
    normed = (scaled * gain).astype(bf16)

    def head(raw, head_gain):
        scale = lax.rsqrt(jnp.mean(raw * raw, axis=-1, keepdims=True) + eps_norm)
        made = raw * scale * head_gain
        return (made * cosine[...] + turn(made) * sine[...]).astype(bf16)

    made = dot(normed, weight_kv[...])
    key_raw[...] = made[:, :KW]
    pair[:, :KW] = head(made[:, :KW], gains[17:18, :])
    pair[:, KW:] = made[:, KW:].astype(bf16)

    @pl.when(step < 4)
    def _():
        made = dot(normed, weight_q[...])
        query_raw[...] = made
        for h in range(2):
            cols = slice(h * HEAD_SIZE, (h + 1) * HEAD_SIZE)
            query[:, cols] = head(made[:, cols], gains[16:17, :])


def gain_picker():
    row = jnp.arange(1024)
    line = (row // 8 * 18) // 128 + row % 8
    return ((jnp.arange(24)[:, None] == line[None, :]) & (row % 8 < 2)[None, :]).astype(bf16)


def tiles(width):
    return pl.BlockSpec((TILE, width), lambda t: (t, 0))


def columns(width, at):
    return pl.BlockSpec((1024, width), lambda t: (0, at))


def early_tiles(width):
    return pl.BlockSpec((TILE, width), lambda t: (jnp.minimum(t, 1), 0))


def late_tiles(width):
    return pl.BlockSpec((TILE, width), lambda t: (jnp.maximum(t - 2, 0), 0))


def project(near, far, w_first, cosine, sine):
    def first(width):
        return pl.BlockSpec((TILE, width), lambda t: (jnp.minimum(t, 3), 0))

    def near_at(t):
        core = lax.rem(lax.div(t, 2), 2)
        return (jnp.where(core == 0, lax.rem(t, 2), 1), lax.div(t, 4), 0, 0)

    def far_at(t):
        core = lax.rem(lax.div(t, 2), 2)
        return (jnp.where(core == 0, 0, lax.rem(t, 2)), lax.div(t, 4), 0, 0)

    return pl.pallas_call(
        project_kernel,
        grid=(8,),
        out_shape=[
            jax.ShapeDtypeStruct((2048, D), bf16),
            jax.ShapeDtypeStruct((1024, QW), bf16),
            jax.ShapeDtypeStruct((1024, QW), f32),
            jax.ShapeDtypeStruct((2048, QW), bf16),
            jax.ShapeDtypeStruct((2048, KW), f32),
            jax.ShapeDtypeStruct((24, HEAD_SIZE), f32),
        ],
        in_specs=[
            pl.BlockSpec((2, 1, 128, D), near_at),
            pl.BlockSpec((2, 1, 128, D), far_at),
            columns(QW, 0),
            columns(QW, 1),
            columns(128, 6),
            pl.BlockSpec((24, 1024), lambda t: (0, 0)),
            tiles(HEAD_SIZE),
            tiles(HEAD_SIZE),
        ],
        out_specs=[
            tiles(D), first(QW), first(QW), tiles(QW), tiles(KW),
            pl.BlockSpec((24, HEAD_SIZE), lambda t: (0, 0)),
        ],
        compiler_params=pltpu.CompilerParams(vmem_limit_bytes=32 * 2**20),
        cost_estimate=pl.CostEstimate(
            flops=8000000000, bytes_accessed=20000000, transcendentals=0
        ),
        name="project",
    )(near, far, w_first, w_first, w_first, gain_picker(), cosine, sine)


def mlp_kernel(
    near, far, backs_near, backs_far, weight, down, normed, backs, hidden, grad_gu, low, total, low_out, total_out
):
    step = pl.program_id(0)
    rows = jnp.where(step < 2, far[...], near[...])
    normed[...] = rows
    made = dot(rows, weight[...])
    gate = made[:, :FW]
    upper = made[:, FW:]
    sigma = jax.nn.sigmoid(gate)
    acted = gate * sigma
    hidden[...] = (acted * upper).astype(bf16)
    back = jnp.where(step < 2, backs_far[...], backs_near[...])
    backs[...] = back
    grad = dot(back, down[...])
    grad_gu[:, :FW] = (grad * upper * sigma * (1.0 + gate * (1.0 - sigma))).astype(bf16)
    grad_gu[:, FW:] = (grad * acted).astype(bf16)
    part = dot(grad_gu[...], weight[...], contract_cols)
    part_out = dot(hidden[...], down[...], contract_cols)

    @pl.when(step < 2)
    def _():
        low[...] = part.astype(bf16)
        low_out[...] = part_out.astype(bf16)

    @pl.when(step >= 2)
    def _():
        total[...] = part
        total_out[...] = part_out


def mlp(near, far, backs_near, backs_far, w_rest):
    def rows(width):
        return pl.BlockSpec((TILE, width), lambda t: (lax.rem(t + 2, 4), 0))

    return pl.pallas_call(
        mlp_kernel,
        grid=(4,),
        out_shape=[
            jax.ShapeDtypeStruct((1024, D), bf16),
            jax.ShapeDtypeStruct((1024, D), bf16),
            jax.ShapeDtypeStruct((1024, FW), bf16),
            jax.ShapeDtypeStruct((1024, 2 * FW), bf16),
            jax.ShapeDtypeStruct((512, D), bf16),
            jax.ShapeDtypeStruct((512, D), f32),
            jax.ShapeDtypeStruct((512, D), bf16),
            jax.ShapeDtypeStruct((512, D), f32),
        ],
        in_specs=[
            late_tiles(D),
            early_tiles(D),
            late_tiles(D),
            early_tiles(D),
            columns(2 * FW, 0),
            columns(FW, 2),
        ],
        out_specs=[
            rows(D), rows(D), rows(FW), rows(2 * FW),
            early_tiles(D), late_tiles(D), early_tiles(D), late_tiles(D),
        ],
        compiler_params=pltpu.CompilerParams(vmem_limit_bytes=40 * 2**20),
        cost_estimate=pl.CostEstimate(flops=1000000, bytes_accessed=100000, transcendentals=0),
        name="mlp",
    )(near, far, backs_near, backs_far, w_rest, w_rest)


def attend(table, query, pair):
    return pl.pallas_call(
        attend_kernel,
        out_shape=[
            jax.ShapeDtypeStruct((1024, QW), bf16),
            jax.ShapeDtypeStruct((16, 2 * BLK), f32),
        ],
        in_specs=[in_smem()]
        + [in_vmem()] * 2,
        out_specs=[in_vmem()] * 2,
        scratch_shapes=[
            pltpu.VMEM((2048, HEAD_SIZE), bf16),
            pltpu.VMEM((2048, HEAD_SIZE), bf16),
            pltpu.VMEM((HEAD_SIZE, 2048), bf16),
        ],
        compiler_params=pltpu.CompilerParams(vmem_limit_bytes=48 * 2**20),
        cost_estimate=pl.CostEstimate(flops=12000000000, bytes_accessed=20000000, transcendentals=0),
        name="attend",
    )(table, query, pair)


def attend_back(*args):
    return pl.pallas_call(
        attend_back_kernel,
        out_shape=[
            jax.ShapeDtypeStruct((1024, 3 * QW + 128), bf16),
            jax.ShapeDtypeStruct((1024, QW), bf16),
            jax.ShapeDtypeStruct((1024, QW), f32),
            jax.ShapeDtypeStruct((1024, QW), bf16),
        ],
        in_specs=[in_smem()]
        + [in_vmem()] * (len(args) - 2)
        + [pl.BlockSpec(memory_space=pl.ANY)],
        out_specs=[in_vmem()] * 4,
        scratch_shapes=[
            pltpu.VMEM((2048, HEAD_SIZE), bf16),
            pltpu.VMEM((2048, HEAD_SIZE), bf16),
            pltpu.VMEM((HEAD_SIZE, 2048), bf16),
            pltpu.VMEM((2048, HEAD_SIZE), f32),
            pltpu.VMEM((2048, HEAD_SIZE), f32),
            pltpu.VMEM((1024, QW), f32),
            pltpu.VMEM((1024, QW), f32),
            pltpu.VMEM((1024, QW), f32),
            pltpu.VMEM((1024, QW), bf16),
        ],
        compiler_params=pltpu.CompilerParams(vmem_limit_bytes=48 * 2**20),
        cost_estimate=pl.CostEstimate(
            flops=25000000000, bytes_accessed=30000000, transcendentals=0
        ),
        name="attend_back",
    )(*args)


def collect_kernel(got, mlp, weights, own_gain, idle, share, stats):
    total = got[0:64, :].astype(f32)
    for k in range(1, 16):
        total = total + got[64 * k : 64 * k + 64, :].astype(f32)
    gain_sum = total[0:1, 3 * QW :] + total[1:2, 3 * QW :]
    squares = jnp.zeros((8, HEAD_SIZE), f32)
    for j in range(1, 8):
        gain_sum = gain_sum + total[8 * j : 8 * j + 1, 3 * QW :]
        gain_sum = gain_sum + total[8 * j + 1 : 8 * j + 2, 3 * QW :]
    gain_part = jnp.zeros((8, HEAD_SIZE), f32)
    gain = own_gain[...]
    at_mlp = QKVC + 8 * QW

    def fold(v):
        made = v[:, :HEAD_SIZE]
        for k in range(1, v.shape[1] // HEAD_SIZE):
            made = made + v[:, k * HEAD_SIZE : (k + 1) * HEAD_SIZE]
        return made

    for j in range(8):
        rows = slice(8 * j, 8 * j + 8)
        for at, width, base in ((0, QW, 0), (QW, KW, 2048), (QW + KW, KW, 3072)):
            spot = slice(base + j * width, base + (j + 1) * width)
            plain = total[rows, at : at + width]
            gain_part = gain_part + fold(plain * weights[:, spot].astype(f32))
            made = plain * gain
            share[:, spot] = made
            squares = squares + fold(made * made)
        made = total[rows, 2 * QW : 3 * QW]
        share[:, QKVC + j * QW : QKVC + (j + 1) * QW] = made
        squares = squares + fold(made * made)
        for part in range(3):
            made = mlp[rows, part * FW : (part + 1) * FW]
            first = at_mlp + part * FF + j * FW
            share[:, first : first + FW] = made
            squares = squares + fold(made * made)
    attn = jnp.sum(gain_part, axis=1, keepdims=True)
    whole = jnp.sum(squares) + jnp.sum(gain_sum * gain_sum) + jnp.sum(attn * attn)
    row = lax.broadcasted_iota(jnp.int32, (8, HEAD_SIZE), 0)
    lane = lax.broadcasted_iota(jnp.int32, (8, HEAD_SIZE), 1)
    own_attn = jnp.sum(jnp.where(lane == row, attn, 0.0), axis=0, keepdims=True)
    first = lax.broadcasted_iota(jnp.int32, (1, HEAD_SIZE), 1)
    stats[:, :HEAD_SIZE] = jnp.broadcast_to(gain_sum, (128, HEAD_SIZE))
    stats[:, HEAD_SIZE:] = jnp.broadcast_to(
        jnp.where(first == 8, whole, own_attn), (128, HEAD_SIZE)
    )


def collect(got, mlp, weights, own_gain, idle):
    return pl.pallas_call(
        collect_kernel,
        out_shape=[
            jax.ShapeDtypeStruct((8, 15360), f32),
            jax.ShapeDtypeStruct((128, 2 * HEAD_SIZE), f32),
        ],
        in_specs=[in_vmem()] * 4 + [pl.BlockSpec(memory_space=pl.ANY)],
        out_specs=[in_vmem()] * 2,
        compiler_params=pltpu.CompilerParams(vmem_limit_bytes=32 * 2**20),
        name="collect",
    )(got, mlp, weights, own_gain, idle)


def norm_step_kernel(total, one, two, three, rows, base, gain, out, low, gain_grad):
    grad = total[...] + one[...].astype(f32) + two[...].astype(f32) + three[...].astype(f32)
    v = rows[...]
    scale = lax.rsqrt(jnp.mean(v * v, axis=-1, keepdims=True) + eps_norm)
    line = jnp.sum(grad * v * scale, axis=0, keepdims=True)
    weighted = grad * gain[...]
    mean = jnp.mean(weighted * v, axis=-1, keepdims=True)
    made = base[...] + scale * weighted - v * (scale * scale * scale * mean)
    out[...] = made
    low[...] = made.astype(bf16)
    for k in range(8):
        gain_grad[k : k + 1, :] = line[:, k * HEAD_SIZE : (k + 1) * HEAD_SIZE]


def norm_step(*args):
    return pl.pallas_call(
        norm_step_kernel,
        out_shape=[
            jax.ShapeDtypeStruct((128, D), f32),
            jax.ShapeDtypeStruct((128, D), bf16),
            jax.ShapeDtypeStruct((8, HEAD_SIZE), f32),
        ],
        in_specs=[in_vmem()] * 7,
        out_specs=[in_vmem()] * 3,
        compiler_params=pltpu.CompilerParams(vmem_limit_bytes=16 * 2**20),
        cost_estimate=pl.CostEstimate(flops=1000000, bytes_accessed=100000, transcendentals=0),
        name="norm_step",
    )(*args)


def x_parts(low):
    return tuple(
        flip_x(low[k * 128 : (k + 1) * 128], mask) for k, mask in ((1, 1), (2, 3), (3, 2))
    )


def slot_places(positions):
    seq = lax.axis_index("ylo") * 4 + lax.axis_index("z")
    table = lax.dynamic_index_in_dim(positions, seq, 0, keepdims=False).reshape(2, 4, 2, 128)
    xi = lax.axis_index("x")
    table = jnp.stack(
        [
            lax.dynamic_index_in_dim(table, jnp.bitwise_xor(xi, mask), 1, keepdims=False)
            for mask in (0, 1, 3, 2)
        ],
        axis=1,
    )
    table = jnp.transpose(table, (0, 2, 1, 3))
    table = jnp.where(lax.axis_index("core") == 0, table, table[:, ::-1])
    table = jnp.where(lax.axis_index("yhi") == 0, table, table[::-1])
    return table.reshape(2048)


def body(
    tokens,
    cotangent,
    positions,
    weights,
    norm_gains,
    moment_weights,
    second_weights,
    moment_gains,
    second_gains,
):
    o_q, o_k, o_v, o_o = 0, 2048, 3072, 4096
    o_g, o_u, o_d = 6144, 6144 + FF, 6144 + 2 * FF
    w_q = weights[:, o_q:o_k].reshape(8, 8, QW)
    w_k = weights[:, o_k:o_v].reshape(8, 8, KW)
    w_v = weights[:, o_v:o_o].reshape(8, 8, KW)
    w_o = weights[:, o_o:o_g].reshape(8, 8, QW)
    w_g = weights[:, o_g:o_u].reshape(8, 8, FW)
    w_u = weights[:, o_u:o_d].reshape(8, 8, FW)
    w_d = weights[:, o_d:].reshape(8, 8, FW)
    rank = lax.axis_index("ylo")
    for name, size in (("z", 4), ("yhi", 2), ("x", 4), ("core", 2)):
        rank = rank * size + lax.axis_index(name)
    own = tokens[0].astype(f32)
    own_back = cotangent[0].astype(f32)

    ready = positions[0, 0] >= 0

    def region(run, *args):
        made = jax.eval_shape(run, *args)

        def never(*args):
            return jax.tree.map(lambda v: jnp.zeros(v.shape, v.dtype), made)

        return lax.cond(ready, run, never, *args)

    gain_row = jnp.concatenate([norm_gains, jnp.zeros(238, bf16)])
    gain_row = jnp.roll(gain_row, lax.rem(rank * 18, 128)).reshape(1, 2, 128)
    w_gains = jnp.broadcast_to(jnp.pad(gain_row, ((0, 0), (0, 6), (0, 0))), (8, 8, 128))
    w_gains = jnp.transpose(w_gains, (1, 0, 2))

    def spread(v):
        n = v.shape[1]
        return jnp.broadcast_to(v[None], (16, 64, n)).reshape(1024, n)

    def pack(tokens, *parts):
        mine = jnp.transpose(jnp.concatenate(parts, axis=2), (1, 0, 2))
        mine = group_exchange(mine).reshape(64, 2048)
        more = jnp.concatenate([tokens, swap_yhi(tokens)], axis=0)
        return more, spread(mine[:, : 3 * QW + 128]), spread(mine[:, 3 * QW + 128 :])

    more, first_sent, rest_sent = region(
        pack, tokens[0], w_q, w_k, w_v, w_o, w_gains, w_g, w_u, w_d
    )
    w_first = lax.all_to_all(first_sent, PLANE, 0, 0, tiled=True)

    def fetch(more, positions):
        near = near_gather_halves(more)
        table = slot_places(positions)[::BLK] // BLK
        far = swap_core(near).reshape(4, 2, 128, D)
        return (near.reshape(4, 2, 128, D), far, table, *turn_tables(table))

    near, far, table, cosine, sine = region(fetch, more, positions)
    w_rest = lax.all_to_all(after(rest_sent, w_first, far), PLANE, 0, 0, tiled=True)

    def mix(near, far, w_first, cosine, sine, table, back, own):
        back_parts = [flip_x(back, mask) for mask in (1, 3, 2)]
        plain, query, query_raw, pair, key_raw, gains = project(near, far, w_first, cosine, sine)
        attended, logsum = attend(table, query, pair)
        attended = after(attended, *back_parts)
        back_near = jnp.concatenate([back] + back_parts, axis=0)
        w_out = w_first[:, 2 * QW : 3 * QW]
        middle = own + group_scatter(attended, w_out, contract_cols)
        normed_two = middle * rms_scale(middle) * gains[8:16].reshape(D)
        normed_two = near_gather(normed_two.astype(bf16))
        return (
            plain, query, query_raw, pair, key_raw, gains, attended, logsum,
            back_near, swap_core(back_near), middle, normed_two, swap_core(normed_two),
        )

    (
        plain, query, query_raw, pair, key_raw, gains, attended, logsum,
        back_near, back_far, middle, two_near, two_far,
    ) = region(mix, near, far, w_first, cosine, sine, table, cotangent[0], own)
    w_qkv = w_first[:, : 2 * QW]
    gain_attn = gains[:8].reshape(D)
    gain_mlp = gains[8:16].reshape(D)
    head_gains = gains[16:18]
    normed_all, backs_low, hidden, grad_gu, low, total, low_out, total_out = mlp(
        two_near, two_far, back_near, back_far, w_rest
    )

    def weigh(total, low, normed_all, grad_gu, backs_low, hidden):
        term_gu = dot(normed_all, grad_gu, contract_rows)
        term_down = dot(backs_low, hidden, contract_rows)
        return *core_fold(total, low), term_gu.astype(bf16), term_down.astype(bf16)

    total, low, term_gu, term_down = region(
        weigh, total, low, normed_all, grad_gu, backs_low, hidden
    )
    term_mlp = jnp.concatenate([term_gu, term_down], axis=1)
    got_mlp = lax.all_to_all(term_mlp, PLANE, 0, 0, tiled=True)

    def turn_back(total, low, middle, own_back, gain_mlp, total_out, low_out):
        grad_mid, grad_mid_low, gain_grad = norm_step(
            total, *x_parts(low), middle, own_back, gain_mlp[None]
        )
        mid_near = near_gather(grad_mid_low)
        total_out, low_out = core_fold(total_out, low_out)
        return (
            grad_mid, gain_grad, mid_near, swap_core(mid_near), middle + total_out,
            low_out[128:256], low_out[256:384], low_out[384:],
        )

    grad_mid, gain_mlp_grad, mid_near, mid_far, output, *out_low = region(
        turn_back, total, low, middle, own_back, gain_mlp, total_out, low_out
    )

    def back(low_1, low_2, low_3, *args):
        made = attend_back(*args)
        parts = [after(flip_x(v, m), made[0]) for v, m in ((low_1, 1), (low_2, 3), (low_3, 2))]
        return (*parts, *made)

    part_1, part_2, part_3, last, grad_q_low, grad_pair, grad_pair_away = region(
        back, *out_low,
        table, query, pair, attended, logsum, query_raw, key_raw,
        cosine, sine, head_gains, gain_mlp_grad, plain, mid_near, mid_far, w_first,
        got_mlp,
    )
    got = lax.all_to_all(last, ALL, 0, 0, tiled=True)

    away = swap_yhi(grad_pair_away)

    def share(got_mlp, output, *parts):
        for part in parts:
            output = output + part.astype(f32)
        plane_mlp = jnp.sum(got_mlp.reshape(16, 64, 3 * FW).astype(f32), axis=0)
        return group_exchange(plane_mlp.reshape(8, 8, 3 * FW)).reshape(64, 3 * FW), output

    share_mlp, output = region(share, after(got_mlp, last), output, part_1, part_2, part_3)

    def finish(grad_q_low, grad_pair, away, w_qkv):
        grad_pair = (grad_pair + away.astype(f32)).astype(bf16)
        grad_proj = jnp.concatenate([grad_q_low, grad_pair], axis=1)
        half = dot(grad_proj[512:], w_qkv, contract_cols).astype(bf16)
        return core_fold(dot(grad_proj[:512], w_qkv, contract_cols), half)

    total, low = region(finish, after(grad_q_low, share_mlp), grad_pair, away, w_qkv)
    own_gain = lax.dynamic_slice_in_dim(gain_attn, rank * 8, 8)
    grad_share, stats = collect(got, share_mlp, weights, own_gain[:, None], low)
    shared = lax.all_to_all(stats, ALL, 0, 0, tiled=True)


    parts = region(x_parts, after(low, stats))
    grad_inputs, _, _ = norm_step(total, *parts, own, grad_mid, gain_attn[None])
    shared = after(shared, *parts)

    norm_all = jnp.sqrt(jnp.sum(shared[:, HEAD_SIZE + 8]))
    gain_whole = jnp.concatenate(
        [shared[:, HEAD_SIZE : HEAD_SIZE + 8].reshape(D), shared[:10, :HEAD_SIZE].reshape(1280)]
    )
    gain_grad = lax.dynamic_slice_in_dim(gain_whole, rank * 18, 18)
    factor = jnp.minimum(1.0, clip_limit / (norm_all + 1e-06))
    column = jnp.arange(grad_share.shape[1])
    rates = jnp.where(
        (column >= QKVC) & (column < QKVC + QUERY_HEADS * HEAD_SIZE), rate_output, rate_matrix
    )
    new_w, new_mw, new_vw = adam(
        weights.astype(f32),
        grad_share * factor,
        moment_weights,
        second_weights,
        rates[None, :],
        decay_rate,
    )
    new_g, new_mg, new_vg = adam(
        norm_gains.astype(f32),
        gain_grad * factor,
        moment_gains,
        second_gains,
        rate_gain,
        0.0,
    )
    return (
        output[None],
        grad_inputs[None],
        norm_all.reshape(1),
        new_w,
        new_mw,
        new_vw,
        new_g,
        new_mg,
        new_vg,
    )


def solution(mesh):
    parts = Mesh(mesh.devices.reshape(2, 4, 2, 4, 2), ALL)
    rows = P(("ylo", "z"), ("yhi", "x", "core"), None)
    owned = P(ALL, None)
    small = P(ALL)
    return jax.shard_map(
        body,
        mesh=parts,
        in_specs=(rows, rows, P(), owned, small, owned, owned, small, small),
        out_specs=(rows, rows, P(), owned, owned, owned, small, small, small),
        check_vma=False,
    )
```

```python
import functools
import math

import jax
import jax.numpy as jnp
from jax import lax
from jax.experimental import pallas as pl
from jax.experimental.pallas import tpu as pltpu
from jax.sharding import Mesh
from jax.sharding import PartitionSpec as P

D = 1024
FF = 3072
QUERY_HEADS = 16
KEY_VALUE_HEADS = 8
HEAD_SIZE = 128
ADAM_STEP = 10
QKVC = 4096
TP = 8
QW = 256
KW = 128
FW = FF // TP
BLK = 64
TILE = 256

ALL = ("ylo", "z", "yhi", "x", "core")
PLANE = ("ylo", "z", "yhi")

eps_norm = 1e-06
rope_base = 1000000.0
clip_limit = 1.0
beta_one = 0.9
beta_two = 0.95
adam_eps = 1e-08
decay_rate = 0.1
rate_matrix = 0.06
rate_output = 2.0
rate_gain = 1.0
contract_rows = (((0,), (0,)), ((), ()))
contract_cols = (((1,), (1,)), ((), ()))
f32 = jnp.float32
bf16 = jnp.bfloat16


def dot(a, b, dims=(((1,), (0,)), ((), ()))):
    return lax.dot_general(a, b, dims, preferred_element_type=f32)


def rms_scale(value_rows):
    return lax.rsqrt(jnp.mean(value_rows * value_rows, axis=-1, keepdims=True) + eps_norm)


def norm_back(value_rows, scale, gain, grad_out):
    gain_grad = jnp.sum(grad_out * value_rows * scale, axis=tuple(range(value_rows.ndim - 1)))
    weighted = grad_out * gain
    grad_in = scale * weighted - value_rows * scale * scale * scale * jnp.mean(
        weighted * value_rows, axis=-1, keepdims=True
    )
    return (grad_in, gain_grad)


def turn_tables(blocks):
    half = HEAD_SIZE // 2
    inverse = jnp.exp(jnp.arange(half, dtype=f32) * (-2.0 / HEAD_SIZE) * math.log(rope_base))
    inverse = jnp.concatenate([inverse, inverse])
    coarse = (blocks * BLK).astype(f32)[:, None] * inverse[None, :]
    fine = jnp.arange(BLK, dtype=f32)[:, None] * inverse[None, :]
    sign = jnp.where(jnp.arange(HEAD_SIZE) < half, -1.0, 1.0)
    cos_a, sin_a, cos_b, sin_b = lax.optimization_barrier(
        (jnp.cos(coarse), jnp.sin(coarse), jnp.cos(fine), jnp.sin(fine))
    )
    cos_a, sin_a = cos_a[:, None, :], sin_a[:, None, :]
    cosine = cos_a * cos_b - sin_a * sin_b
    sine = (sin_a * cos_b + cos_a * sin_b) * sign
    return (cosine.reshape(-1, HEAD_SIZE), sine.reshape(-1, HEAD_SIZE))


def swap_core(v):
    return lax.ppermute(v, "core", [(0, 1), (1, 0)])


def swap_yhi(v):
    return lax.ppermute(v, "yhi", [(0, 1), (1, 0)])


def shift_x(v, k):
    return lax.ppermute(v, "x", [(i, (i + k) % 4) for i in range(4)])


def y_index(p):
    return (p % 2) * 2 + p // 2


def shift_y(v, k):
    return lax.ppermute(v, ("ylo", "yhi"), [(y_index(i), y_index((i + k) % 4)) for i in range(4)])


def shift_z(v, k):
    return lax.ppermute(v, "z", [(i, (i + k) % 4) for i in range(4)])


def idle_kernel(*refs):
    pass


def after(v, *waits):
    return pl.pallas_call(
        idle_kernel,
        out_shape=jax.ShapeDtypeStruct(v.shape, v.dtype),
        in_specs=[pl.BlockSpec(memory_space=pl.ANY)] * (1 + len(waits)),
        out_specs=pl.BlockSpec(memory_space=pl.ANY),
        input_output_aliases={0: 0},
        cost_estimate=pl.CostEstimate(flops=0, bytes_accessed=0, transcendentals=0),
        name="after",
    )(v, *waits)


def turned(v, start):
    return lax.dynamic_slice_in_dim(jnp.concatenate([v, v], axis=0), start, 4, axis=0)


def group_exchange(v):
    xi, core = lax.axis_index("x"), lax.axis_index("core")
    n = v.shape[2]
    v = turned(v.reshape(4, 2, 8, n), xi)
    kept = jnp.where(core == 0, v[:, 0], v[:, 1])
    got = swap_core(jnp.where(core == 0, v[:, 1], v[:, 0]))
    v = jnp.stack([kept, got], axis=1)
    v = jnp.stack([v[0], shift_x(v[3], 3), shift_x(v[2], 2), shift_x(v[1], 1)])
    v = jnp.where(core == 0, v, v[:, ::-1])
    return turned(v, lax.rem(4 - xi, 4)).reshape(8, 8, n)


def flip_x(v, mask):
    return lax.ppermute(v, "x", [(i, i ^ mask) for i in range(4)])


def near_gather(v):
    return jnp.concatenate([v] + [flip_x(v, mask) for mask in (1, 3, 2)], axis=0)


def near_gather_halves(v):
    half = v.shape[0] // 2
    a, b = v[:half], v[half:]
    a_one, b_two = flip_x(a, 1), flip_x(b, 3)
    a_rest = flip_x(jnp.concatenate([a, a_one], axis=0), 3)
    b_rest = flip_x(jnp.concatenate([b, b_two], axis=0), 1)
    return jnp.concatenate(
        [v, a_one, b_rest[:half], a_rest[:half], b_two, a_rest[half:], b_rest[half:]], axis=0
    )


def group_gather(v):
    near = near_gather(v)
    return jnp.concatenate([near, swap_core(near)], axis=0)


def group_scatter(left, right, dims):
    half = left.shape[0] // 2
    away = dot(left[half:], right, dims).astype(bf16)
    return group_fold(dot(left[:half], right, dims), away)


def core_fold(near, away):
    near = near + swap_core(away).astype(f32)
    return near[:128], near.astype(bf16)


def x_fold(total, low):
    for k, mask in ((1, 1), (2, 3), (3, 2)):
        total = total + flip_x(low[k * 128 : (k + 1) * 128], mask).astype(f32)
    return total


def group_fold(near, away):
    return x_fold(*core_fold(near, away))


def adam(weight, grad, moment, second, rate, decay):
    moment_new = beta_one * moment + (1.0 - beta_one) * grad
    second_new = beta_two * second + (1.0 - beta_two) * grad * grad
    scaled_m = moment_new / (1.0 - beta_one**ADAM_STEP)
    scaled_v = second_new / (1.0 - beta_two**ADAM_STEP)
    weight_new = weight * (1.0 - rate * decay) - rate * scaled_m / (jnp.sqrt(scaled_v) + adam_eps)
    return (weight_new, moment_new, second_new)


def sort_blocks(table, pair, keys, values):
    for i in range(32):
        spot = pl.ds(pl.multiple_of(table[i] * BLK, BLK), BLK)
        keys[spot, :] = pair[i * BLK : (i + 1) * BLK, :HEAD_SIZE]
        values[spot, :] = pair[i * BLK : (i + 1) * BLK, HEAD_SIZE:]


def flip(v):
    return jnp.transpose(v.astype(f32)).astype(bf16)


def stack_heads(ref, rows):
    return jnp.concatenate([ref[rows, :HEAD_SIZE], ref[rows, HEAD_SIZE:]], axis=0)


def seen(place, first, count):
    key_place = first + lax.broadcasted_iota(jnp.int32, (count, 2 * BLK), 0)
    lane = lax.broadcasted_iota(jnp.int32, (count, 2 * BLK), 1)
    return key_place <= place * BLK + lax.rem(lane, BLK)


def attend_kernel(table, query, pair, out, logsum, keys, values, values_t):
    scale = HEAD_SIZE ** (-0.5)
    sort_blocks(table, pair, keys, values)
    for t in range(8):
        values_t[:, t * TILE : (t + 1) * TILE] = flip(values[t * TILE : (t + 1) * TILE, :])

    def block(i, carry):
        place = table[i]
        rows = pl.ds(pl.multiple_of(i * BLK, BLK), BLK)

        def run(count):
            full = count - TILE
            stacked = stack_heads(query, rows)
            tail = dot(keys[full:count, :], stacked, contract_cols)
            tail = jnp.where(seen(place, full, TILE), tail, -1e30)
            top = jnp.max(tail, axis=0, keepdims=True)
            if full:
                head = dot(keys[:full, :], stacked, contract_cols)
                top = jnp.maximum(top, jnp.max(head, axis=0, keepdims=True))
            tail = jnp.exp((tail - top) * scale)
            total = jnp.sum(tail, axis=0, keepdims=True)
            mixed = dot(values_t[:, full:count], tail.astype(bf16))
            if full:
                head = jnp.exp((head - top) * scale)
                total = total + jnp.sum(head, axis=0, keepdims=True)
                mixed = mixed + dot(values_t[:, :full], head.astype(bf16))
            mixed = jnp.transpose(mixed / total).astype(bf16)
            out[rows, :HEAD_SIZE] = mixed[:BLK]
            out[rows, HEAD_SIZE:] = mixed[BLK:]
            logsum[pl.ds(i, 1), :] = top * scale + jnp.log(total)

        for step in range(8):
            pl.when(lax.div(place, 4) == step)(functools.partial(run, (step + 1) * TILE))
        return carry

    lax.fori_loop(0, 16, block, 0)


def turn(v):
    return jnp.concatenate([v[:, HEAD_SIZE // 2 :], v[:, : HEAD_SIZE // 2]], axis=1)


def head_back(raw, grad, gain, cosine, sine):
    grad = grad * cosine - turn(grad) * sine
    scale = lax.rsqrt(jnp.mean(raw * raw, axis=-1, keepdims=True) + eps_norm)
    gain_grad = jnp.sum(grad * raw * scale, axis=0, keepdims=True)
    weighted = grad * gain
    mean = jnp.mean(weighted * raw, axis=-1, keepdims=True)
    return (scale * weighted - raw * (scale * scale * scale * mean), gain_grad)


def attend_back_kernel(
    table, query, pair, out, logsum,
    query_raw, key_raw, cosine, sine, gains, gain_mlp, plain, mid_near, mid_far,
    weight, idle, last, grad_query, grad_own, grad_away,
    keys, values, keys_t, acc_key, acc_value, pair_near, pair_far, query_acc, grad,
):
    scale = HEAD_SIZE ** (-0.5)
    columns_out = slice(2 * QW, 3 * QW)
    grad[:512, :] = dot(mid_near[...], weight[:, columns_out]).astype(bf16)
    grad[512:, :] = dot(mid_far[...], weight[:, columns_out]).astype(bf16)
    sort_blocks(table, pair, keys, values)
    acc_key[...] = jnp.zeros_like(acc_key)
    acc_value[...] = jnp.zeros_like(acc_value)
    for t in range(8):
        keys_t[:, t * TILE : (t + 1) * TILE] = flip(keys[t * TILE : (t + 1) * TILE, :])

    def block(i, carry):
        place = table[i]
        rows = pl.ds(pl.multiple_of(i * BLK, BLK), BLK)

        def run(count):
            stacked = stack_heads(query, rows)
            back = stack_heads(grad, rows)
            made = stack_heads(out, rows)
            inner = jnp.sum(
                jnp.transpose(back.astype(f32) * made.astype(f32)), axis=0, keepdims=True
            )
            level = logsum[pl.ds(i, 1), :]
            total = jnp.zeros((HEAD_SIZE, 2 * BLK), f32)
            for first in range(0, count, TILE):
                span = slice(first, first + TILE)
                probs = jnp.exp(dot(keys[span, :], stacked, contract_cols) * scale - level)
                if first + TILE == count:
                    probs = jnp.where(seen(place, first, TILE), probs, 0.0)
                grad_p = dot(values[span, :], back, contract_cols)
                grad_s = (probs * (grad_p - inner)).astype(bf16)
                acc_key[span, :] += dot(grad_s, stacked)
                acc_value[span, :] += dot(probs.astype(bf16), back)
                total = total + dot(keys_t[:, span], grad_s)
            total = jnp.transpose(total) * scale
            query_acc[rows, :HEAD_SIZE] = total[:BLK]
            query_acc[rows, HEAD_SIZE:] = total[BLK:]

        for step in range(8):
            pl.when(lax.div(place, 4) == step)(functools.partial(run, (step + 1) * TILE))
        return carry

    lax.fori_loop(0, 16, block, 0)
    for i in range(16):
        rows = slice(i * BLK, (i + 1) * BLK)
        near = pl.ds(pl.multiple_of(table[i] * BLK, BLK), BLK)
        pair_near[rows, :HEAD_SIZE] = acc_key[near, :] * scale
        pair_near[rows, HEAD_SIZE:] = acc_value[near, :]
        far = pl.ds(pl.multiple_of(table[16 + i] * BLK, BLK), BLK)
        pair_far[rows, :HEAD_SIZE] = acc_key[far, :] * scale
        pair_far[rows, HEAD_SIZE:] = acc_value[far, :]

    gain_q = gains[0:1, :]
    gain_k = gains[1:2, :]
    sum_q = jnp.zeros((1, HEAD_SIZE), f32)
    sum_k = jnp.zeros((1, HEAD_SIZE), f32)
    for t in range(4):
        rows = slice(t * TILE, (t + 1) * TILE)
        rows_far = slice(1024 + t * TILE, 1024 + (t + 1) * TILE)
        for h in range(2):
            cols = slice(h * HEAD_SIZE, (h + 1) * HEAD_SIZE)
            made, part = head_back(
                query_raw[rows, cols], query_acc[rows, cols], gain_q, cosine[rows, :], sine[rows, :]
            )
            grad_query[rows, cols] = made.astype(bf16)
            sum_q = sum_q + part
        made, part = head_back(
            key_raw[rows, :], pair_near[rows, :HEAD_SIZE], gain_k, cosine[rows, :], sine[rows, :]
        )
        pair_near[rows, :HEAD_SIZE] = made
        sum_k = sum_k + part
        made, part = head_back(
            key_raw[rows_far, :], pair_far[rows, :HEAD_SIZE], gain_k,
            cosine[rows_far, :], sine[rows_far, :],
        )
        pair_far[rows, :HEAD_SIZE] = made
        sum_k = sum_k + part
    grad_own[...] = pair_near[...]
    grad_away[...] = pair_far[...].astype(bf16)

    def down(ref):
        return jnp.transpose(ref[...].astype(f32)).astype(bf16)

    query_t = down(grad_query)
    near_t = down(pair_near)
    far_t = down(pair_far)
    out_t = down(out)
    for t in range(4):
        rows = slice(t * TILE, (t + 1) * TILE)
        made = dot(query_t, plain[:1024, rows])
        last[rows, :QW] = jnp.transpose(made).astype(bf16)
        made = dot(near_t, plain[:1024, rows]) + dot(far_t, plain[1024:, rows])
        last[rows, QW : 2 * QW] = jnp.transpose(made).astype(bf16)
        made = dot(out_t[:, :512], mid_near[:, rows]) + dot(out_t[:, 512:], mid_far[:, rows])
        last[rows, 2 * QW : 3 * QW] = jnp.transpose(made).astype(bf16)
    last[:, 3 * QW :] = jnp.zeros((1024, 128), bf16)
    lines = [gain_mlp[k : k + 1, :] for k in range(8)] + [sum_q, sum_k]
    row = lax.broadcasted_iota(jnp.int32, (16, HEAD_SIZE), 0)
    for k in range(5):
        made = jnp.zeros((16, HEAD_SIZE), f32)
        for at, line in ((0, lines[2 * k]), (8, lines[2 * k + 1])):
            high = line.astype(bf16).astype(f32)
            made = jnp.where(row == at, high, made)
            made = jnp.where(row == at + 1, line - high, made)
        last[16 * k : 16 * k + 16, 3 * QW :] = made.astype(bf16)


def in_vmem():
    return pl.BlockSpec(memory_space=pltpu.VMEM)


def in_smem():
    return pl.BlockSpec(memory_space=pltpu.SMEM)


def project_kernel(
    near, far, weight_q, weight_kv, gain_cols, pick, cosine, sine,
    plain, query, query_raw, pair, key_raw, gains,
):
    step = pl.program_id(0)

    @pl.when(step == 0)
    def _():
        gains[...] = dot(pick[...], gain_cols[...])

    is_near = lax.rem(lax.div(step, 2), 2) == 0
    rows = jnp.where(is_near, near[...].reshape(TILE, D), far[...].reshape(TILE, D)).astype(f32)
    scaled = rows * lax.rsqrt(jnp.mean(rows * rows, axis=-1, keepdims=True) + eps_norm)
    plain[...] = scaled.astype(bf16)
    gain = jnp.concatenate([gains[k : k + 1, :] for k in range(8)], axis=1)
    normed = (scaled * gain).astype(bf16)

    def head(raw, head_gain):
        scale = lax.rsqrt(jnp.mean(raw * raw, axis=-1, keepdims=True) + eps_norm)
        made = raw * scale * head_gain
        return (made * cosine[...] + turn(made) * sine[...]).astype(bf16)

    made = dot(normed, weight_kv[...])
    key_raw[...] = made[:, :KW]
    pair[:, :KW] = head(made[:, :KW], gains[17:18, :])
    pair[:, KW:] = made[:, KW:].astype(bf16)

    @pl.when(step < 4)
    def _():
        made = dot(normed, weight_q[...])
        query_raw[...] = made
        for h in range(2):
            cols = slice(h * HEAD_SIZE, (h + 1) * HEAD_SIZE)
            query[:, cols] = head(made[:, cols], gains[16:17, :])


def gain_picker():
    row = jnp.arange(1024)
    line = (row // 8 * 18) // 128 + row % 8
    return ((jnp.arange(24)[:, None] == line[None, :]) & (row % 8 < 2)[None, :]).astype(bf16)


def tiles(width):
    return pl.BlockSpec((TILE, width), lambda t: (t, 0))


def columns(width, at):
    return pl.BlockSpec((1024, width), lambda t: (0, at))


def early_tiles(width):
    return pl.BlockSpec((TILE, width), lambda t: (jnp.minimum(t, 1), 0))


def late_tiles(width):
    return pl.BlockSpec((TILE, width), lambda t: (jnp.maximum(t - 2, 0), 0))


def project(near, far, w_first, cosine, sine):
    def first(width):
        return pl.BlockSpec((TILE, width), lambda t: (jnp.minimum(t, 3), 0))

    def near_at(t):
        core = lax.rem(lax.div(t, 2), 2)
        return (jnp.where(core == 0, lax.rem(t, 2), 1), lax.div(t, 4), 0, 0)

    def far_at(t):
        core = lax.rem(lax.div(t, 2), 2)
        return (jnp.where(core == 0, 0, lax.rem(t, 2)), lax.div(t, 4), 0, 0)

    return pl.pallas_call(
        project_kernel,
        grid=(8,),
        out_shape=[
            jax.ShapeDtypeStruct((2048, D), bf16),
            jax.ShapeDtypeStruct((1024, QW), bf16),
            jax.ShapeDtypeStruct((1024, QW), f32),
            jax.ShapeDtypeStruct((2048, QW), bf16),
            jax.ShapeDtypeStruct((2048, KW), f32),
            jax.ShapeDtypeStruct((24, HEAD_SIZE), f32),
        ],
        in_specs=[
            pl.BlockSpec((2, 1, 128, D), near_at),
            pl.BlockSpec((2, 1, 128, D), far_at),
            columns(QW, 0),
            columns(QW, 1),
            columns(128, 6),
            pl.BlockSpec((24, 1024), lambda t: (0, 0)),
            tiles(HEAD_SIZE),
            tiles(HEAD_SIZE),
        ],
        out_specs=[
            tiles(D), first(QW), first(QW), tiles(QW), tiles(KW),
            pl.BlockSpec((24, HEAD_SIZE), lambda t: (0, 0)),
        ],
        compiler_params=pltpu.CompilerParams(vmem_limit_bytes=32 * 2**20),
        cost_estimate=pl.CostEstimate(
            flops=8000000000, bytes_accessed=20000000, transcendentals=0
        ),
        name="project",
    )(near, far, w_first, w_first, w_first, gain_picker(), cosine, sine)


def mlp_kernel(
    near, far, backs_near, backs_far, weight, down, normed, backs, hidden, grad_gu, low, total, low_out, total_out
):
    step = pl.program_id(0)
    rows = jnp.where(step < 2, far[...], near[...])
    normed[...] = rows
    made = dot(rows, weight[...])
    gate = made[:, :FW]
    upper = made[:, FW:]
    sigma = jax.nn.sigmoid(gate)
    acted = gate * sigma
    hidden[...] = (acted * upper).astype(bf16)
    back = jnp.where(step < 2, backs_far[...], backs_near[...])
    backs[...] = back
    grad = dot(back, down[...])
    grad_gu[:, :FW] = (grad * upper * sigma * (1.0 + gate * (1.0 - sigma))).astype(bf16)
    grad_gu[:, FW:] = (grad * acted).astype(bf16)
    part = dot(grad_gu[...], weight[...], contract_cols)
    part_out = dot(hidden[...], down[...], contract_cols)

    @pl.when(step < 2)
    def _():
        low[...] = part.astype(bf16)
        low_out[...] = part_out.astype(bf16)

    @pl.when(step >= 2)
    def _():
        total[...] = part
        total_out[...] = part_out


def mlp(near, far, backs_near, backs_far, w_rest):
    def rows(width):
        return pl.BlockSpec((TILE, width), lambda t: (lax.rem(t + 2, 4), 0))

    return pl.pallas_call(
        mlp_kernel,
        grid=(4,),
        out_shape=[
            jax.ShapeDtypeStruct((1024, D), bf16),
            jax.ShapeDtypeStruct((1024, D), bf16),
            jax.ShapeDtypeStruct((1024, FW), bf16),
            jax.ShapeDtypeStruct((1024, 2 * FW), bf16),
            jax.ShapeDtypeStruct((512, D), bf16),
            jax.ShapeDtypeStruct((512, D), f32),
            jax.ShapeDtypeStruct((512, D), bf16),
            jax.ShapeDtypeStruct((512, D), f32),
        ],
        in_specs=[
            late_tiles(D),
            early_tiles(D),
            late_tiles(D),
            early_tiles(D),
            columns(2 * FW, 0),
            columns(FW, 2),
        ],
        out_specs=[
            rows(D), rows(D), rows(FW), rows(2 * FW),
            early_tiles(D), late_tiles(D), early_tiles(D), late_tiles(D),
        ],
        compiler_params=pltpu.CompilerParams(vmem_limit_bytes=40 * 2**20),
        cost_estimate=pl.CostEstimate(flops=1000000, bytes_accessed=100000, transcendentals=0),
        name="mlp",
    )(near, far, backs_near, backs_far, w_rest, w_rest)


def attend(table, query, pair):
    return pl.pallas_call(
        attend_kernel,
        out_shape=[
            jax.ShapeDtypeStruct((1024, QW), bf16),
            jax.ShapeDtypeStruct((16, 2 * BLK), f32),
        ],
        in_specs=[in_smem()]
        + [in_vmem()] * 2,
        out_specs=[in_vmem()] * 2,
        scratch_shapes=[
            pltpu.VMEM((2048, HEAD_SIZE), bf16),
            pltpu.VMEM((2048, HEAD_SIZE), bf16),
            pltpu.VMEM((HEAD_SIZE, 2048), bf16),
        ],
        compiler_params=pltpu.CompilerParams(vmem_limit_bytes=48 * 2**20),
        cost_estimate=pl.CostEstimate(flops=12000000000, bytes_accessed=20000000, transcendentals=0),
        name="attend",
    )(table, query, pair)


def attend_back(*args):
    return pl.pallas_call(
        attend_back_kernel,
        out_shape=[
            jax.ShapeDtypeStruct((1024, 3 * QW + 128), bf16),
            jax.ShapeDtypeStruct((1024, QW), bf16),
            jax.ShapeDtypeStruct((1024, QW), f32),
            jax.ShapeDtypeStruct((1024, QW), bf16),
        ],
        in_specs=[in_smem()]
        + [in_vmem()] * (len(args) - 2)
        + [pl.BlockSpec(memory_space=pl.ANY)],
        out_specs=[in_vmem()] * 4,
        scratch_shapes=[
            pltpu.VMEM((2048, HEAD_SIZE), bf16),
            pltpu.VMEM((2048, HEAD_SIZE), bf16),
            pltpu.VMEM((HEAD_SIZE, 2048), bf16),
            pltpu.VMEM((2048, HEAD_SIZE), f32),
            pltpu.VMEM((2048, HEAD_SIZE), f32),
            pltpu.VMEM((1024, QW), f32),
            pltpu.VMEM((1024, QW), f32),
            pltpu.VMEM((1024, QW), f32),
            pltpu.VMEM((1024, QW), bf16),
        ],
        compiler_params=pltpu.CompilerParams(vmem_limit_bytes=48 * 2**20),
        cost_estimate=pl.CostEstimate(
            flops=25000000000, bytes_accessed=30000000, transcendentals=0
        ),
        name="attend_back",
    )(*args)


def collect_kernel(got, mlp, weights, own_gain, share, stats):
    total = got[0:64, :].astype(f32)
    for k in range(1, 16):
        total = total + got[64 * k : 64 * k + 64, :].astype(f32)
    gain_sum = total[0:1, 3 * QW :] + total[1:2, 3 * QW :]
    squares = jnp.zeros((8, HEAD_SIZE), f32)
    for j in range(1, 8):
        gain_sum = gain_sum + total[8 * j : 8 * j + 1, 3 * QW :]
        gain_sum = gain_sum + total[8 * j + 1 : 8 * j + 2, 3 * QW :]
    gain_part = jnp.zeros((8, HEAD_SIZE), f32)
    gain = own_gain[...]
    at_mlp = QKVC + 8 * QW

    def fold(v):
        made = v[:, :HEAD_SIZE]
        for k in range(1, v.shape[1] // HEAD_SIZE):
            made = made + v[:, k * HEAD_SIZE : (k + 1) * HEAD_SIZE]
        return made

    for j in range(8):
        rows = slice(8 * j, 8 * j + 8)
        for at, width, base in ((0, QW, 0), (QW, KW, 2048), (QW + KW, KW, 3072)):
            spot = slice(base + j * width, base + (j + 1) * width)
            plain = total[rows, at : at + width]
            gain_part = gain_part + fold(plain * weights[:, spot].astype(f32))
            made = plain * gain
            share[:, spot] = made
            squares = squares + fold(made * made)
        made = total[rows, 2 * QW : 3 * QW]
        share[:, QKVC + j * QW : QKVC + (j + 1) * QW] = made
        squares = squares + fold(made * made)
        for part in range(3):
            made = mlp[rows, part * FW : (part + 1) * FW]
            first = at_mlp + part * FF + j * FW
            share[:, first : first + FW] = made
            squares = squares + fold(made * made)
    attn = jnp.sum(gain_part, axis=1, keepdims=True)
    whole = jnp.sum(squares) + jnp.sum(gain_sum * gain_sum) + jnp.sum(attn * attn)
    row = lax.broadcasted_iota(jnp.int32, (8, HEAD_SIZE), 0)
    lane = lax.broadcasted_iota(jnp.int32, (8, HEAD_SIZE), 1)
    own_attn = jnp.sum(jnp.where(lane == row, attn, 0.0), axis=0, keepdims=True)
    first = lax.broadcasted_iota(jnp.int32, (1, HEAD_SIZE), 1)
    stats[:, :HEAD_SIZE] = jnp.broadcast_to(gain_sum, (128, HEAD_SIZE))
    stats[:, HEAD_SIZE:] = jnp.broadcast_to(
        jnp.where(first == 8, whole, own_attn), (128, HEAD_SIZE)
    )


def collect(got, mlp, weights, own_gain):
    return pl.pallas_call(
        collect_kernel,
        out_shape=[
            jax.ShapeDtypeStruct((8, 15360), f32),
            jax.ShapeDtypeStruct((128, 2 * HEAD_SIZE), f32),
        ],
        in_specs=[in_vmem()] * 4,
        out_specs=[in_vmem()] * 2,
        compiler_params=pltpu.CompilerParams(vmem_limit_bytes=32 * 2**20),
        name="collect",
    )(got, mlp, weights, own_gain)


def norm_step_kernel(total, one, two, three, rows, base, gain, out, low, gain_grad):
    grad = total[...] + one[...].astype(f32) + two[...].astype(f32) + three[...].astype(f32)
    v = rows[...]
    scale = lax.rsqrt(jnp.mean(v * v, axis=-1, keepdims=True) + eps_norm)
    line = jnp.sum(grad * v * scale, axis=0, keepdims=True)
    weighted = grad * gain[...]
    mean = jnp.mean(weighted * v, axis=-1, keepdims=True)
    made = base[...] + scale * weighted - v * (scale * scale * scale * mean)
    out[...] = made
    low[...] = made.astype(bf16)
    for k in range(8):
        gain_grad[k : k + 1, :] = line[:, k * HEAD_SIZE : (k + 1) * HEAD_SIZE]


def norm_step(*args):
    return pl.pallas_call(
        norm_step_kernel,
        out_shape=[
            jax.ShapeDtypeStruct((128, D), f32),
            jax.ShapeDtypeStruct((128, D), bf16),
            jax.ShapeDtypeStruct((8, HEAD_SIZE), f32),
        ],
        in_specs=[in_vmem()] * 7,
        out_specs=[in_vmem()] * 3,
        compiler_params=pltpu.CompilerParams(vmem_limit_bytes=16 * 2**20),
        cost_estimate=pl.CostEstimate(flops=1000000, bytes_accessed=100000, transcendentals=0),
        name="norm_step",
    )(*args)


def x_parts(low):
    return tuple(
        flip_x(low[k * 128 : (k + 1) * 128], mask) for k, mask in ((1, 1), (2, 3), (3, 2))
    )


def slot_places(positions):
    seq = lax.axis_index("ylo") * 4 + lax.axis_index("z")
    table = lax.dynamic_index_in_dim(positions, seq, 0, keepdims=False).reshape(2, 4, 2, 128)
    xi = lax.axis_index("x")
    table = jnp.stack(
        [
            lax.dynamic_index_in_dim(table, jnp.bitwise_xor(xi, mask), 1, keepdims=False)
            for mask in (0, 1, 3, 2)
        ],
        axis=1,
    )
    table = jnp.transpose(table, (0, 2, 1, 3))
    table = jnp.where(lax.axis_index("core") == 0, table, table[:, ::-1])
    table = jnp.where(lax.axis_index("yhi") == 0, table, table[::-1])
    return table.reshape(2048)


def body(
    tokens,
    cotangent,
    positions,
    weights,
    norm_gains,
    moment_weights,
    second_weights,
    moment_gains,
    second_gains,
):
    o_q, o_k, o_v, o_o = 0, 2048, 3072, 4096
    o_g, o_u, o_d = 6144, 6144 + FF, 6144 + 2 * FF
    w_q = weights[:, o_q:o_k].reshape(8, 8, QW)
    w_k = weights[:, o_k:o_v].reshape(8, 8, KW)
    w_v = weights[:, o_v:o_o].reshape(8, 8, KW)
    w_o = weights[:, o_o:o_g].reshape(8, 8, QW)
    w_g = weights[:, o_g:o_u].reshape(8, 8, FW)
    w_u = weights[:, o_u:o_d].reshape(8, 8, FW)
    w_d = weights[:, o_d:].reshape(8, 8, FW)
    rank = lax.axis_index("ylo")
    for name, size in (("z", 4), ("yhi", 2), ("x", 4), ("core", 2)):
        rank = rank * size + lax.axis_index(name)
    own = tokens[0].astype(f32)
    own_back = cotangent[0].astype(f32)

    ready = positions[0, 0] >= 0

    def region(run, *args):
        made = jax.eval_shape(run, *args)

        def never(*args):
            return jax.tree.map(lambda v: jnp.zeros(v.shape, v.dtype), made)

        return lax.cond(ready, run, never, *args)

    gain_row = jnp.concatenate([norm_gains, jnp.zeros(238, bf16)])
    gain_row = jnp.roll(gain_row, lax.rem(rank * 18, 128)).reshape(1, 2, 128)
    w_gains = jnp.broadcast_to(jnp.pad(gain_row, ((0, 0), (0, 6), (0, 0))), (8, 8, 128))
    w_gains = jnp.transpose(w_gains, (1, 0, 2))

    def spread(v):
        n = v.shape[1]
        return jnp.broadcast_to(v[None], (16, 64, n)).reshape(1024, n)

    def pack(tokens, *parts):
        mine = jnp.transpose(jnp.concatenate(parts, axis=2), (1, 0, 2))
        mine = group_exchange(mine).reshape(64, 2048)
        more = jnp.concatenate([tokens, swap_yhi(tokens)], axis=0)
        return more, spread(mine[:, : 3 * QW + 128]), spread(mine[:, 3 * QW + 128 :])

    more, first_sent, rest_sent = region(
        pack, tokens[0], w_q, w_k, w_v, w_o, w_gains, w_g, w_u, w_d
    )
    w_first = lax.all_to_all(first_sent, PLANE, 0, 0, tiled=True)

    def fetch(more, positions):
        near = near_gather_halves(more)
        table = slot_places(positions)[::BLK] // BLK
        far = swap_core(near).reshape(4, 2, 128, D)
        return (near.reshape(4, 2, 128, D), far, table, *turn_tables(table))

    near, far, table, cosine, sine = region(fetch, more, positions)
    w_rest = lax.all_to_all(after(rest_sent, w_first, far), PLANE, 0, 0, tiled=True)

    def mix(near, far, w_first, cosine, sine, table, back, own):
        back_parts = [flip_x(back, mask) for mask in (1, 3, 2)]
        plain, query, query_raw, pair, key_raw, gains = project(near, far, w_first, cosine, sine)
        attended, logsum = attend(table, query, pair)
        attended = after(attended, *back_parts)
        back_near = jnp.concatenate([back] + back_parts, axis=0)
        w_out = w_first[:, 2 * QW : 3 * QW]
        middle = own + group_scatter(attended, w_out, contract_cols)
        normed_two = middle * rms_scale(middle) * gains[8:16].reshape(D)
        normed_two = near_gather(normed_two.astype(bf16))
        return (
            plain, query, query_raw, pair, key_raw, gains, attended, logsum,
            back_near, swap_core(back_near), middle, normed_two, swap_core(normed_two),
        )

    (
        plain, query, query_raw, pair, key_raw, gains, attended, logsum,
        back_near, back_far, middle, two_near, two_far,
    ) = region(mix, near, far, w_first, cosine, sine, table, cotangent[0], own)
    w_qkv = w_first[:, : 2 * QW]
    gain_attn = gains[:8].reshape(D)
    gain_mlp = gains[8:16].reshape(D)
    head_gains = gains[16:18]
    normed_all, backs_low, hidden, grad_gu, low, total, low_out, total_out = mlp(
        two_near, two_far, back_near, back_far, w_rest
    )

    def weigh(total, low, normed_all, grad_gu, backs_low, hidden):
        term_gu = dot(normed_all, grad_gu, contract_rows)
        term_down = dot(backs_low, hidden, contract_rows)
        return *core_fold(total, low), term_gu.astype(bf16), term_down.astype(bf16)

    total, low, term_gu, term_down = region(
        weigh, total, low, normed_all, grad_gu, backs_low, hidden
    )
    term_mlp = jnp.concatenate([term_gu, term_down], axis=1)
    got_mlp = lax.all_to_all(term_mlp, PLANE, 0, 0, tiled=True)

    def turn_back(total, low, middle, own_back, gain_mlp, total_out, low_out):
        grad_mid, grad_mid_low, gain_grad = norm_step(
            total, *x_parts(low), middle, own_back, gain_mlp[None]
        )
        mid_near = near_gather(grad_mid_low)
        total_out, low_out = core_fold(total_out, low_out)
        return (
            grad_mid, gain_grad, mid_near, swap_core(mid_near), middle + total_out,
            low_out[128:256], low_out[256:384], low_out[384:],
        )

    grad_mid, gain_mlp_grad, mid_near, mid_far, output, *out_low = region(
        turn_back, total, low, middle, own_back, gain_mlp, total_out, low_out
    )

    def back(low_1, low_2, low_3, *args):
        made = attend_back(*args)
        parts = [after(flip_x(v, m), made[0]) for v, m in ((low_1, 1), (low_2, 3), (low_3, 2))]
        return (*parts, *made)

    part_1, part_2, part_3, last, grad_q_low, grad_pair, grad_pair_away = region(
        back, *out_low,
        table, query, pair, attended, logsum, query_raw, key_raw,
        cosine, sine, head_gains, gain_mlp_grad, plain, mid_near, mid_far, w_first,
        got_mlp,
    )
    got = lax.all_to_all(last, ALL, 0, 0, tiled=True)

    away = swap_yhi(grad_pair_away)

    def share(got_mlp, output, *parts):
        for part in parts:
            output = output + part.astype(f32)
        plane_mlp = jnp.sum(got_mlp.reshape(16, 64, 3 * FW).astype(f32), axis=0)
        return group_exchange(plane_mlp.reshape(8, 8, 3 * FW)).reshape(64, 3 * FW), output

    share_mlp, output = region(share, after(got_mlp, last), output, part_1, part_2, part_3)

    def finish(grad_q_low, grad_pair, away, w_qkv):
        grad_pair = (grad_pair + away.astype(f32)).astype(bf16)
        grad_proj = jnp.concatenate([grad_q_low, grad_pair], axis=1)
        half = dot(grad_proj[512:], w_qkv, contract_cols).astype(bf16)
        return core_fold(dot(grad_proj[:512], w_qkv, contract_cols), half)

    total, low = region(finish, after(grad_q_low, share_mlp), grad_pair, away, w_qkv)
    own_gain = lax.dynamic_slice_in_dim(gain_attn, rank * 8, 8)
    grad_share, stats = collect(got, share_mlp, weights, own_gain[:, None])
    shared = lax.all_to_all(stats, ALL, 0, 0, tiled=True)


    parts = region(x_parts, after(low, stats))
    grad_inputs, _, _ = norm_step(total, *parts, own, grad_mid, gain_attn[None])
    shared = after(shared, *parts)

    norm_all = jnp.sqrt(jnp.sum(shared[:, HEAD_SIZE + 8]))
    gain_whole = jnp.concatenate(
        [shared[:, HEAD_SIZE : HEAD_SIZE + 8].reshape(D), shared[:10, :HEAD_SIZE].reshape(1280)]
    )
    gain_grad = lax.dynamic_slice_in_dim(gain_whole, rank * 18, 18)
    factor = jnp.minimum(1.0, clip_limit / (norm_all + 1e-06))
    column = jnp.arange(grad_share.shape[1])
    rates = jnp.where(
        (column >= QKVC) & (column < QKVC + QUERY_HEADS * HEAD_SIZE), rate_output, rate_matrix
    )
    new_w, new_mw, new_vw = adam(
        weights.astype(f32),
        grad_share * factor,
        moment_weights,
        second_weights,
        rates[None, :],
        decay_rate,
    )
    new_g, new_mg, new_vg = adam(
        norm_gains.astype(f32),
        gain_grad * factor,
        moment_gains,
        second_gains,
        rate_gain,
        0.0,
    )
    return (
        output[None],
        grad_inputs[None],
        norm_all.reshape(1),
        new_w,
        new_mw,
        new_vw,
        new_g,
        new_mg,
        new_vg,
    )


def solution(mesh):
    parts = Mesh(mesh.devices.reshape(2, 4, 2, 4, 2), ALL)
    rows = P(("ylo", "z"), ("yhi", "x", "core"), None)
    owned = P(ALL, None)
    small = P(ALL)
    return jax.shard_map(
        body,
        mesh=parts,
        in_specs=(rows, rows, P(), owned, small, owned, owned, small, small),
        out_specs=(rows, rows, P(), owned, owned, owned, small, small, small),
        check_vma=False,
    )
```
